32 devices in a mesh: groups: 2 (over x), gx: 4 (over y, core), gz: 4 (over z).
Axes of the slice: x: 2, y: 2, z: 4, core: 2. Of those that a mesh axis runs over, the one named last changes fastest.
Arguments:
- charges: float32 [64, 64, 512], P(('groups', 'gx'), 'gz'), parts along dimension 0, may hold values from -24 to 24
Outputs:
- potential: float32 [64, 64, 512], P(('groups', 'gx'), 'gz'), parts along dimension 0
The draws below stay inside these ranges and needn't reach their ends.
There are 2 independent parts, one for each index of `groups`. The reference program is written for one: setup_inputs(seed, part) draws one part's arguments, and reference() takes and returns one part's arrays. A program takes and returns all parts, laid end to end along the dimension named above; each array names one. Nothing has to cross between parts.
All inputs are finite; a program needn't handle non-finite values.
Results may differ from the reference program's by a relative error of at most 0.0001.
Values sent between devices are 32-bit elements; how exact they have to be, the bound alone decides.
No kernel may reach another device: no remote copies, remote signals or barrier semaphores. Data moves between devices by JAX's collectives and lax.ppermute only.
A program may use at most 128 MiB of HBM per device.

```python
import jax
import jax.numpy as jnp

NY = 512
LEVELS = 4
SWEEPS = 2
COARSE_SWEEPS = 8
CYCLES = 2
NX = 32
NZ = 64


def shard_levels(rng, shape, cuts, smallest, largest):
    factor_of = 1.0
    for position, blocks in cuts:
        draws = jax.random.uniform(jax.random.fold_in(jax.random.fold_in(rng, 6), position), (blocks,), jnp.float32, smallest / len(cuts), largest / len(cuts))
        factor_of = factor_of * jnp.repeat(jnp.exp(draws), shape[position] // blocks).reshape((-1,) + (1,) * (len(shape) - 1 - position))
    return factor_of


def normal_values(stream_key, shape, deviation, bound, pieces=(), held_as=jnp.bfloat16):
    result = jax.random.normal(stream_key, shape, jnp.float32) * deviation
    if len(pieces) > 0:
        result = shard_levels(stream_key, shape, pieces, -0.22, 0.18) * result
    return jnp.clip(result, min=-bound, max=bound).astype(held_as)


def setup_inputs(seed: int = 0, part: int = 0) -> dict:
    streams_of = jax.random.split(jax.random.key(seed), 2)
    part_keys = jax.random.split(jax.random.fold_in(streams_of[1], part), 2)
    charges = normal_values(part_keys[0], (NX, NZ, NY), 4.0, 24.0, ((0, 4), (1, 4)), jnp.float32)
    return dict(charges=charges)


OMEGA = 0.8


def mehrstellen(padded, grid_level):
    size_x = padded.shape[0] - 2
    size_z = padded.shape[1] - 2
    size_y = padded.shape[2] - 2

    def window(i, j, k):
        return padded[1 + i:1 + i + size_x, 1 + j:1 + j + size_z, 1 + k:1 + k + size_y]

    face_sum = window(1, 0, 0) + window(-1, 0, 0) + window(0, 1, 0) + window(0, -1, 0) + window(0, 0, 1) + window(0, 0, -1)
    edge_sum = window(1, 1, 0) + window(1, -1, 0) + window(-1, 1, 0) + window(-1, -1, 0)
    edge_sum = edge_sum + window(1, 0, 1) + window(1, 0, -1) + window(-1, 0, 1) + window(-1, 0, -1)
    edge_sum = edge_sum + window(0, 1, 1) + window(0, 1, -1) + window(0, -1, 1) + window(0, -1, -1)
    return (24.0 * window(0, 0, 0) - 2.0 * face_sum - edge_sum) * (1.0 / (6.0 * 4.0 ** grid_level))


def charge_source(padded):
    size_x = padded.shape[0] - 2
    size_z = padded.shape[1] - 2
    size_y = padded.shape[2] - 2

    def window(i, j, k):
        return padded[1 + i:1 + i + size_x, 1 + j:1 + j + size_z, 1 + k:1 + k + size_y]

    face_sum = window(1, 0, 0) + window(-1, 0, 0) + window(0, 1, 0) + window(0, -1, 0) + window(0, 0, 1) + window(0, 0, -1)
    return (6.0 * window(0, 0, 0) + face_sum) * (1.0 / 12.0)


def jacobi(approx, source, applied, grid_level):
    return approx + OMEGA * (source - applied) * (4.0 ** grid_level / 4.0)


def restrict(residue):
    size_x, size_z, size_y = residue.shape
    return residue.reshape(size_x // 2, 2, size_z // 2, 2, size_y // 2, 2).sum(axis=(1, 3, 5)) * 0.125


def prolong(coarse):
    return jnp.repeat(jnp.repeat(jnp.repeat(coarse, 2, 0), 2, 1), 2, 2)


def whole_cycle(approx, source, grid_level):
    if grid_level == LEVELS - 1:
        for sweep_index in range(COARSE_SWEEPS):
            approx = jacobi(approx, source, mehrstellen(jnp.pad(approx, 1), grid_level), grid_level)
        return approx
    for sweep_index in range(SWEEPS):
        approx = jacobi(approx, source, mehrstellen(jnp.pad(approx, 1), grid_level), grid_level)
    residue = source - mehrstellen(jnp.pad(approx, 1), grid_level)
    coarse_source = restrict(residue)
    correction = whole_cycle(jnp.zeros_like(coarse_source), coarse_source, grid_level + 1)
    approx = approx + prolong(correction)
    for sweep_index in range(SWEEPS):
        approx = jacobi(approx, source, mehrstellen(jnp.pad(approx, 1), grid_level), grid_level)
    return approx


def reference(charges):
    source = charge_source(jnp.pad(charges, 1))
    approx = jnp.zeros_like(charges)
    for cycle_index in range(CYCLES):
        approx = whole_cycle(approx, source, 0)
    return approx
```

```python
import functools

import jax
import jax.numpy as jnp
from jax import lax
from jax.experimental import pallas as pl
from jax.experimental.pallas import tpu as pltpu
from jax.sharding import PartitionSpec as P

COARSE_SWEEPS = 8
LANES = 128
RIM = 8
BRICK_X = 8
BRICK_Z = 16
WIDE_X = BRICK_X + 2 * RIM
WIDE_Z = BRICK_Z + 2 * RIM
VMEM_BYTES = 48 * 1024 * 1024


def lane_of(shape):
    return lax.broadcasted_iota(jnp.int32, shape, len(shape) - 1)


def row_of(shape):
    return lax.broadcasted_iota(jnp.int32, shape, len(shape) - 2)


def next_row(tile, step, cyclic):
    rows = tile.shape[0]
    moved = pltpu.roll(tile, rows - step, 0)
    return moved if cyclic else jnp.where(row_of(tile.shape) < rows - step, moved, 0.0)


def last_row(tile, step, cyclic):
    moved = pltpu.roll(tile, step, 0)
    return moved if cyclic else jnp.where(row_of(tile.shape) >= step, moved, 0.0)


def next_lane(tile, step):
    moved = pltpu.roll(tile, LANES - step, 1)
    return jnp.where(lane_of(tile.shape) < LANES - step, moved, 0.0)


def last_lane(tile, step):
    moved = pltpu.roll(tile, step, 1)
    return jnp.where(lane_of(tile.shape) >= step, moved, 0.0)


def load_plane(ref, x, count_q, count_p):
    return [[ref[x, q, p] for p in range(count_p)] for q in range(count_q)]


def store_plane(ref, x, plane):
    for q, line in enumerate(plane):
        for p, tile in enumerate(line):
            ref[x, q, p] = tile


def along_z(plane, step, cyclic):
    count_q, count_p = len(plane), len(plane[0])
    result = []
    for q in range(count_q):
        line = []
        for p in range(count_p):
            after = plane[q + 1][p] if q + 1 < count_q else next_row(plane[0][p], step, cyclic)
            before = plane[q - 1][p] if q > 0 else last_row(plane[-1][p], step, cyclic)
            line.append(after + before)
        result.append(line)
    return result


def along_y(line, step):
    count_p = len(line)
    result = []
    for p in range(count_p):
        after = line[p + 1] if p + 1 < count_p else next_lane(line[0], step)
        before = line[p - 1] if p > 0 else last_lane(line[-1], step)
        result.append(after + before)
    return result


class Level:
    def __init__(self, count_q, count_p, step, cyclic):
        self.count_q, self.count_p, self.step, self.cyclic = count_q, count_p, step, cyclic

    def load(self, ref, x):
        return load_plane(ref, x, self.count_q, self.count_p)

    def put(self, u_ref, g_ref, x, plane):
        store_plane(u_ref, x, plane)
        sums = along_z(plane, self.step, self.cyclic)
        store_plane(
            g_ref,
            x,
            [
                [s + (v + v) for s, v in zip(sum_line, line)]
                for sum_line, line in zip(sums, plane)
            ],
        )

    def spread(self, u_ref, g_ref, x):
        result = []
        for q in range(self.count_q):
            sides, both = [], []
            for p in range(self.count_p):
                here = g_ref[x, q, p]
                sides.append((u_ref[x - 1, q, p] + u_ref[x + 1, q, p]) + here)
                both.append((g_ref[x - 1, q, p] + g_ref[x + 1, q, p]) + (here + here))
            result.append([a + b for a, b in zip(both, along_y(sides, self.step))])
        return result

    def sweep(self, u_ref, g_ref, b_ref, x, weight):
        wide = self.spread(u_ref, g_ref, x)
        return [
            [
                u_ref[x, q, p] * (1.0 / 15.0) + b_ref[x, q, p] + wide[q][p] * weight
                for p in range(self.count_p)
            ]
            for q in range(self.count_q)
        ]

    def residual(self, u_ref, g_ref, b_ref, x):
        wide = self.spread(u_ref, g_ref, x)
        return [
            [
                b_ref[x, q, p] * 5.0 + (wide[q][p] * (1.0 / 6.0) - u_ref[x, q, p] * (14.0 / 3.0))
                for p in range(self.count_p)
            ]
            for q in range(self.count_q)
        ]


def add_planes(one, other):
    return [[a + b for a, b in zip(l, m)] for l, m in zip(one, other)]


def join(plane):
    lines = [[a + b for a, b in zip(plane[q], plane[q + 1])] for q in range(0, len(plane), 2)]
    return [[line[p] + line[p + 1] for p in range(0, len(line), 2)] for line in lines]


def join_within(tile):
    rows = tile.shape[0]
    even = row_of(tile.shape) % 2 == 0
    tile = tile + jnp.where(even, pltpu.roll(tile, rows - 1, 0), pltpu.roll(tile, 1, 0))
    even = lane_of(tile.shape) % 2 == 0
    return tile + jnp.where(even, pltpu.roll(tile, LANES - 1, 1), pltpu.roll(tile, 1, 1))


def scaled(plane, factor):
    return [[tile * factor for tile in line] for line in plane]


def each(lo, hi, body, chunk):
    count = hi - lo
    whole = count // chunk
    if whole == 1:
        for x in range(lo, lo + chunk):
            body(x)
    elif whole > 1:

        def step(i, carry):
            for d in range(chunk):
                body(lo + i * chunk + d)
            return carry

        lax.fori_loop(0, whole, step, 0)
    for x in range(lo + whole * chunk, hi):
        body(x)


FINE = Level(4, 4, 1, True)
LEVEL_1 = Level(2, 2, 1, False)
LEVEL_2 = Level(1, 1, 1, False)
LEVEL_3 = Level(1, 1, 2, False)
PAD = RIM // 2


def zero_planes(ref, indices):
    for x in indices:
        ref[x] = jnp.zeros(ref.shape[1:], ref.dtype)


def coarse_grids(count_x, count_z):
    rows = count_z * BRICK_Z // 4
    shapes = []
    for planes, count in ((4 * count_x + 2 * PAD, 2), (2 * count_x + 2, 1), (count_x + 2, 1)):
        shapes += [pltpu.VMEM((planes, count, count, rows, LANES), jnp.float32)] * 5
    return shapes


def coarse_solve(count_x, count_z, pieces_ref, grids):
    (ua1, ub1, ga1, gb1, b1), (ua2, ub2, ga2, gb2, b2), (ua3, ub3, ga3, gb3, b3) = (
        grids[0:5],
        grids[5:10],
        grids[10:15],
    )
    size_1, size_2, size_3 = 4 * count_x, 2 * count_x, count_x
    for ref in (ua1, ub1, ga1, gb1):
        zero_planes(ref, list(range(PAD)) + list(range(PAD + size_1, PAD + size_1 + PAD)))
    for ref, size in ((ua2, size_2), (ub2, size_2), (ga2, size_2), (gb2, size_2)):
        zero_planes(ref, (0, size + 1))
    for ref, size in ((ua3, size_3), (ub3, size_3), (ga3, size_3), (gb3, size_3)):
        zero_planes(ref, (0, size + 1))
    third = 1.0 / 30.0

    def gather(at_x):
        for i in range(4):
            x = PAD + at_x * 4 + i
            for q in range(2):
                for p in range(2):
                    for at_z in range(count_z):
                        piece = pieces_ref[at_x * count_z + at_z, i, q, p] * 0.2
                        b1[x, q, p, 4 * at_z : 4 * at_z + 4, :] = piece
            LEVEL_1.put(ub1, gb1, x, LEVEL_1.load(b1, x))

    each(0, count_x, gather, 1)

    def sweep(level, u_in, g_in, u_out, g_out, b):
        return lambda x: level.put(u_out, g_out, x, level.sweep(u_in, g_in, b, x, third))

    each(PAD, PAD + size_1, sweep(LEVEL_1, ub1, gb1, ua1, ga1, b1), 4)

    def restrict_1(x):
        fine = PAD + 2 * (x - 1)
        pair = add_planes(
            LEVEL_1.residual(ua1, ga1, b1, fine), LEVEL_1.residual(ua1, ga1, b1, fine + 1)
        )
        plane = scaled(join(pair), 0.5 * 0.2)
        store_plane(b2, x, plane)
        LEVEL_2.put(ub2, gb2, x, plane)

    each(1, 1 + size_2, restrict_1, 2)
    each(1, 1 + size_2, sweep(LEVEL_2, ub2, gb2, ua2, ga2, b2), 8)

    def restrict_2(x):
        fine = 1 + 2 * (x - 1)
        pair = add_planes(
            LEVEL_2.residual(ua2, ga2, b2, fine), LEVEL_2.residual(ua2, ga2, b2, fine + 1)
        )
        plane = [[join_within(pair[0][0]) * (0.5 * 0.2)]]
        store_plane(b3, x, plane)
        LEVEL_3.put(ub3, gb3, x, plane)

    each(1, 1 + size_3, restrict_2, 4)
    now, later = (ub3, gb3), (ua3, ga3)
    for _ in range(COARSE_SWEEPS - 1):
        each(1, 1 + size_3, sweep(LEVEL_3, *now, *later, b3), 4)
        now, later = later, now

    def prolong_3(x):
        for d in range(2):
            fine = 1 + 2 * (x - 1) + d
            LEVEL_2.put(ua2, ga2, fine, [[ua2[fine, 0, 0] + now[0][x, 0, 0]]])

    each(1, 1 + size_3, prolong_3, 4)
    each(1, 1 + size_2, sweep(LEVEL_2, ua2, ga2, ub2, gb2, b2), 8)
    each(1, 1 + size_2, sweep(LEVEL_2, ub2, gb2, ua2, ga2, b2), 8)

    def prolong_2(x):
        error = ua2[x, 0, 0]
        for d in range(2):
            fine = PAD + 2 * (x - 1) + d
            LEVEL_1.put(
                ua1, ga1, fine, [[t + error for t in line] for line in LEVEL_1.load(ua1, fine)]
            )

    each(1, 1 + size_2, prolong_2, 2)
    each(PAD, PAD + size_1, sweep(LEVEL_1, ua1, ga1, ub1, gb1, b1), 4)
    each(PAD, PAD + size_1, sweep(LEVEL_1, ub1, gb1, ua1, ga1, b1), 4)
    return ua1


def rim_masks(count_x, count_z, where_ref):
    at_x, at_z = where_ref[0], where_ref[1]
    k = row_of((8, LANES))
    low = (at_z > 0).astype(jnp.float32)
    high = (at_z < count_z - 1).astype(jnp.float32)
    rows = jnp.where(k < 4, 1.0, jnp.where(k < 6, high, low))
    below = (at_x > 0).astype(jnp.float32)
    above = (at_x < count_x - 1).astype(jnp.float32)
    return rows, below, above


def in_segments(lo, hi, body, masks, scale, chunk):
    rows, below, above = masks
    inner = rows * scale
    for start, end, weight in (
        (lo, min(hi, RIM), inner * below),
        (max(lo, RIM), min(hi, RIM + BRICK_X), inner),
        (max(lo, RIM + BRICK_X), hi, inner * above),
    ):
        if end > start:
            each(start, end, functools.partial(body, weight=weight), chunk)


def fine_sweep(u_in, g_in, u_out, g_out, b_ref, margin, masks):
    def body(x, weight):
        FINE.put(u_out, g_out, x, FINE.sweep(u_in, g_in, b_ref, x, weight))

    in_segments(margin, WIDE_X - margin, body, masks, 1.0 / 30.0, 2)


def add_correction(coarse_ref, count_z, where_ref, masks, u_in, u_out, g_out, margin):
    at_x, at_z = where_ref[0], where_ref[1]
    rows_1 = coarse_ref.shape[3]
    turn = lax.rem(rows_1 - 4 * at_z, rows_1)
    k = row_of((8, LANES))
    rows = masks[0]

    def body(i):
        error = []
        for q in range(2):
            line = []
            for p in range(2):
                turned = pltpu.roll(coarse_ref[4 * at_x + i, q, p], turn, 0)
                tile = jnp.where(k < 6, turned[0:8], turned[rows_1 - 8 : rows_1])
                line.append(tile * rows)
            error.append(line)
        for d in range(2):
            x = 2 * i + d
            plane = [
                [u_in[x, q, p] + error[q // 2][p // 2] for p in range(4)] for q in range(4)
            ]
            FINE.put(u_out, g_out, x, plane)

    each(margin // 2, (WIDE_X - margin) // 2, body, 1)


def send_residual(u_ref, g_ref, b_ref, out_ref):
    def body(i):
        x = RIM + 2 * i
        pair = add_planes(
            FINE.residual(u_ref, g_ref, b_ref, x), FINE.residual(u_ref, g_ref, b_ref, x + 1)
        )
        for q, line in enumerate(join(pair)):
            for p, tile in enumerate(line):
                out_ref[0, i, q, p] = (tile * 0.5)[0:4]

    each(0, BRICK_X // 2, body, 1)
    piece = out_ref[0]

    def copy(n, carry):
        out_ref[n] = piece
        return carry

    lax.fori_loop(1, out_ref.shape[0], copy, 0)


def swap_blocks(tiles):
    shape = tiles[0].shape
    lane = lane_of(shape)
    half = lane < 64
    even = (lane // 32) % 2 == 0
    a, b, c, d = tiles
    a, c = jnp.where(half, a, pltpu.roll(c, 64, 1)), jnp.where(half, pltpu.roll(a, 64, 1), c)
    b, d = jnp.where(half, b, pltpu.roll(d, 64, 1)), jnp.where(half, pltpu.roll(b, 64, 1), d)
    a, b = jnp.where(even, a, pltpu.roll(b, 32, 1)), jnp.where(even, pltpu.roll(a, 96, 1), b)
    c, d = jnp.where(even, c, pltpu.roll(d, 32, 1)), jnp.where(even, pltpu.roll(c, 96, 1), d)
    return [a, b, c, d]


def pick_lanes(tile, index):
    return jnp.take_along_axis(tile, index, axis=1, mode="promise_in_bounds")


def down_kernel(count_x, count_z, where_ref, low_ref, mid_ref, high_ref, u_ref, b_ref, out_ref,
                c_ref, g_ref, h_ref, rows_ref):
    masks = rim_masks(count_x, count_z, where_ref)
    lane = lane_of((8, LANES))
    index = (lane % 32) * 4 + lane // 32
    for part, ref in enumerate((low_ref, mid_ref, high_ref)):

        def convert(x, part=part, ref=ref):
            for r in range(0, WIDE_Z, 8):
                tiles = []
                for t in range(4):
                    tile = ref[x, r : r + 8, t * LANES : (t + 1) * LANES]
                    tiles.append(pick_lanes(tile, index))
                for p, tile in enumerate(swap_blocks(tiles)):
                    rows_ref[x, p, r : r + 8, :] = tile
            for q in range(4):
                for p in range(4):
                    c_ref[part * BRICK_X + x, q, p] = rows_ref[x, p, pl.ds(q, 8, stride=4), :]

        each(0, BRICK_X, convert, 2)

    def source(x, weight):
        here = FINE.load(c_ref, x)
        sums = along_z(here, 1, True)
        plane = []
        for q in range(4):
            y_sums = along_y(here[q], 1)
            line = []
            for p in range(4):
                face = (c_ref[x - 1, q, p] + c_ref[x + 1, q, p]) + (sums[q][p] + y_sums[p])
                line.append((here[q][p] * 6.0 + face) * weight)
            plane.append(line)
        FINE.put(b_ref, g_ref, x, plane)

    in_segments(1, WIDE_X - 1, source, masks, 0.2 / 12.0, 2)

    def body(x, weight):
        FINE.put(u_ref, h_ref, x, FINE.sweep(b_ref, g_ref, b_ref, x, weight))

    in_segments(2, WIDE_X - 2, body, masks, 1.0 / 30.0, 2)
    send_residual(u_ref, h_ref, b_ref, out_ref)


def middle_kernel(count_x, count_z, where_ref, pieces_ref, u_ref, b_ref, v_ref, out_ref,
                  ga_ref, gb_ref, ua_ref, *grids):
    masks = rim_masks(count_x, count_z, where_ref)
    coarse = coarse_solve(count_x, count_z, pieces_ref, grids)
    add_correction(coarse, count_z, where_ref, masks, u_ref, ua_ref, ga_ref, 2)
    fine_sweep(ua_ref, ga_ref, v_ref, gb_ref, b_ref, 3, masks)
    fine_sweep(v_ref, gb_ref, ua_ref, ga_ref, b_ref, 4, masks)
    fine_sweep(ua_ref, ga_ref, v_ref, gb_ref, b_ref, 5, masks)
    fine_sweep(v_ref, gb_ref, ua_ref, ga_ref, b_ref, 6, masks)

    def keep(x):
        store_plane(v_ref, x, FINE.load(ua_ref, x))

    each(6, WIDE_X - 6, keep, 2)
    send_residual(ua_ref, ga_ref, b_ref, out_ref)


def up_kernel(count_x, count_z, where_ref, pieces_ref, u_ref, b_ref, out_ref,
              ga_ref, gb_ref, ua_ref, ub_ref, rows_ref, *grids):
    masks = rim_masks(count_x, count_z, where_ref)
    coarse = coarse_solve(count_x, count_z, pieces_ref, grids)
    add_correction(coarse, count_z, where_ref, masks, u_ref, ua_ref, ga_ref, 6)
    fine_sweep(ua_ref, ga_ref, ub_ref, gb_ref, b_ref, 7, masks)
    lane = lane_of((8, LANES))
    index = (lane % 4) * 32 + lane // 4

    def body(x):
        plane = FINE.sweep(ub_ref, gb_ref, b_ref, x, 1.0 / 30.0)
        for q in range(4):
            for t, tile in enumerate(swap_blocks(plane[q])):
                rows = pick_lanes(tile, index)[0:4]
                rows_ref[x - RIM, t, pl.ds(q, 4, stride=4), :] = rows
        for t in range(4):
            out_ref[x - RIM, :, t * LANES : (t + 1) * LANES] = rows_ref[x - RIM, t]

    each(RIM, RIM + BRICK_X, body, 2)


def call(kernel, outputs, scratch):
    shapes = [jax.ShapeDtypeStruct(shape, jnp.float32) for shape in outputs]
    return lambda where, *arrays: pl.pallas_call(
        kernel,
        out_shape=shapes,
        in_specs=[pl.BlockSpec(memory_space=pltpu.SMEM)]
        + [pl.BlockSpec(memory_space=pltpu.VMEM)] * len(arrays),
        out_specs=[pl.BlockSpec(memory_space=pltpu.VMEM)] * len(shapes),
        scratch_shapes=scratch,
        compiler_params=pltpu.CompilerParams(vmem_limit_bytes=VMEM_BYTES),
    )(where, *arrays)


def both_ways(axis, to_next, to_last):
    count = lax.axis_size(axis)
    forward = [(i, i + 1) for i in range(count - 1)]
    backward = [(target, source) for source, target in forward]
    return lax.ppermute(to_next, axis, forward), lax.ppermute(to_last, axis, backward)


def per_device(charges):
    count_x, count_z = lax.axis_size("gx"), lax.axis_size("gz")
    where = jnp.stack([lax.axis_index("gx"), lax.axis_index("gz")]).astype(jnp.int32)
    low, high = both_ways("gz", charges[:, BRICK_Z - RIM :], charges[:, :RIM])
    middle = jnp.concatenate([charges, high, low], axis=1)
    below, above = both_ways("gx", middle, middle)

    wide = (WIDE_X, 4, 4, 8, LANES)
    pieces = (count_x * count_z, BRICK_X // 2, 2, 2, 4, LANES)
    fine = pltpu.VMEM(wide, jnp.float32)
    grids = coarse_grids(count_x, count_z)
    rows_in = pltpu.VMEM((BRICK_X, 4, WIDE_Z, LANES), jnp.float32)
    rows_out = pltpu.VMEM((BRICK_X, 4, BRICK_Z, LANES), jnp.float32)

    u, b, piece = call(
        functools.partial(down_kernel, count_x, count_z), [wide, wide, pieces], [fine] * 3 + [rows_in]
    )(where, below, middle, above)
    gathered = lax.all_to_all(piece, ("gx", "gz"), 0, 0)
    u, piece = call(
        functools.partial(middle_kernel, count_x, count_z), [wide, pieces], [fine] * 3 + grids
    )(where, gathered, u, b)
    gathered = lax.all_to_all(piece, ("gx", "gz"), 0, 0)
    (potential,) = call(
        functools.partial(up_kernel, count_x, count_z), [charges.shape], [fine] * 4 + [rows_out] + grids
    )(where, gathered, u, b)
    return potential


def solution(mesh):
    return jax.shard_map(
        per_device,
        mesh=mesh,
        in_specs=(P(("groups", "gx"), "gz", None),),
        out_specs=P(("groups", "gx"), "gz", None),
        check_vma=False,
    )
```

```python
import functools

import jax
import jax.numpy as jnp
from jax import lax
from jax.experimental import pallas as pl
from jax.experimental.pallas import tpu as pltpu
from jax.sharding import PartitionSpec as P

COARSE_SWEEPS = 8
LANES = 128
RIM = 8
BRICK_X = 8
BRICK_Z = 16
WIDE_X = BRICK_X + 2 * RIM
WIDE_Z = BRICK_Z + 2 * RIM
VMEM_BYTES = 48 * 1024 * 1024


def lane_of(shape):
    return lax.broadcasted_iota(jnp.int32, shape, len(shape) - 1)


def row_of(shape):
    return lax.broadcasted_iota(jnp.int32, shape, len(shape) - 2)


def next_row(tile, step, cyclic):
    rows = tile.shape[0]
    moved = pltpu.roll(tile, rows - step, 0)
    return moved if cyclic else jnp.where(row_of(tile.shape) < rows - step, moved, 0.0)


def last_row(tile, step, cyclic):
    moved = pltpu.roll(tile, step, 0)
    return moved if cyclic else jnp.where(row_of(tile.shape) >= step, moved, 0.0)


def next_lane(tile, step):
    moved = pltpu.roll(tile, LANES - step, 1)
    return jnp.where(lane_of(tile.shape) < LANES - step, moved, 0.0)


def last_lane(tile, step):
    moved = pltpu.roll(tile, step, 1)
    return jnp.where(lane_of(tile.shape) >= step, moved, 0.0)


def load_plane(ref, x, count_q, count_p):
    return [[ref[x, q, p] for p in range(count_p)] for q in range(count_q)]


def store_plane(ref, x, plane):
    for q, line in enumerate(plane):
        for p, tile in enumerate(line):
            ref[x, q, p] = tile


def along_z(plane, step, cyclic):
    count_q, count_p = len(plane), len(plane[0])
    result = []
    for q in range(count_q):
        line = []
        for p in range(count_p):
            after = plane[q + 1][p] if q + 1 < count_q else next_row(plane[0][p], step, cyclic)
            before = plane[q - 1][p] if q > 0 else last_row(plane[-1][p], step, cyclic)
            line.append(after + before)
        result.append(line)
    return result


def along_y(line, step):
    count_p = len(line)
    result = []
    for p in range(count_p):
        after = line[p + 1] if p + 1 < count_p else next_lane(line[0], step)
        before = line[p - 1] if p > 0 else last_lane(line[-1], step)
        result.append(after + before)
    return result


class Level:
    def __init__(self, count_q, count_p, step, cyclic):
        self.count_q, self.count_p, self.step, self.cyclic = count_q, count_p, step, cyclic

    def load(self, ref, x):
        return load_plane(ref, x, self.count_q, self.count_p)

    def put(self, u_ref, g_ref, x, plane):
        store_plane(u_ref, x, plane)
        sums = along_z(plane, self.step, self.cyclic)
        store_plane(
            g_ref,
            x,
            [
                [s + (v + v) for s, v in zip(sum_line, line)]
                for sum_line, line in zip(sums, plane)
            ],
        )

    def spread(self, u_ref, g_ref, x):
        result = []
        for q in range(self.count_q):
            sides, both = [], []
            for p in range(self.count_p):
                here = g_ref[x, q, p]
                sides.append((u_ref[x - 1, q, p] + u_ref[x + 1, q, p]) + here)
                both.append((g_ref[x - 1, q, p] + g_ref[x + 1, q, p]) + (here + here))
            result.append([a + b for a, b in zip(both, along_y(sides, self.step))])
        return result

    def sweep(self, u_ref, g_ref, b_ref, x, weight):
        wide = self.spread(u_ref, g_ref, x)
        return [
            [
                u_ref[x, q, p] * (1.0 / 15.0) + b_ref[x, q, p] + wide[q][p] * weight
                for p in range(self.count_p)
            ]
            for q in range(self.count_q)
        ]

    def residual(self, u_ref, g_ref, b_ref, x):
        wide = self.spread(u_ref, g_ref, x)
        return [
            [
                b_ref[x, q, p] * 5.0 + (wide[q][p] - u_ref[x, q, p] * 28.0) * (1.0 / 6.0)
                for p in range(self.count_p)
            ]
            for q in range(self.count_q)
        ]


def add_planes(one, other):
    return [[a + b for a, b in zip(l, m)] for l, m in zip(one, other)]


def join(plane):
    lines = [[a + b for a, b in zip(plane[q], plane[q + 1])] for q in range(0, len(plane), 2)]
    return [[line[p] + line[p + 1] for p in range(0, len(line), 2)] for line in lines]


def join_within(tile):
    rows = tile.shape[0]
    even = row_of(tile.shape) % 2 == 0
    tile = tile + jnp.where(even, pltpu.roll(tile, rows - 1, 0), pltpu.roll(tile, 1, 0))
    even = lane_of(tile.shape) % 2 == 0
    return tile + jnp.where(even, pltpu.roll(tile, LANES - 1, 1), pltpu.roll(tile, 1, 1))


def scaled(plane, factor):
    return [[tile * factor for tile in line] for line in plane]


def each(lo, hi, body, chunk):
    count = hi - lo
    whole = count // chunk
    if whole == 1:
        for x in range(lo, lo + chunk):
            body(x)
    elif whole > 1:

        def step(i, carry):
            for d in range(chunk):
                body(lo + i * chunk + d)
            return carry

        lax.fori_loop(0, whole, step, 0)
    for x in range(lo + whole * chunk, hi):
        body(x)


FINE = Level(4, 4, 1, True)
LEVEL_1 = Level(2, 2, 1, False)
LEVEL_2 = Level(1, 1, 1, False)
LEVEL_3 = Level(1, 1, 2, False)
PAD = RIM // 2


def zero_planes(ref, indices):
    for x in indices:
        ref[x] = jnp.zeros(ref.shape[1:], ref.dtype)


def coarse_grids(count_x, count_z):
    rows = count_z * BRICK_Z // 4
    shapes = []
    for planes, count in ((4 * count_x + 2 * PAD, 2), (2 * count_x + 2, 1), (count_x + 2, 1)):
        shapes += [pltpu.VMEM((planes, count, count, rows, LANES), jnp.float32)] * 5
    return shapes


def coarse_solve(count_x, count_z, pieces_ref, grids):
    (ua1, ub1, ga1, gb1, b1), (ua2, ub2, ga2, gb2, b2), (ua3, ub3, ga3, gb3, b3) = (
        grids[0:5],
        grids[5:10],
        grids[10:15],
    )
    size_1, size_2, size_3 = 4 * count_x, 2 * count_x, count_x
    for ref in (ua1, ub1, ga1, gb1):
        zero_planes(ref, list(range(PAD)) + list(range(PAD + size_1, PAD + size_1 + PAD)))
    for ref, size in ((ua2, size_2), (ub2, size_2), (ga2, size_2), (gb2, size_2)):
        zero_planes(ref, (0, size + 1))
    for ref, size in ((ua3, size_3), (ub3, size_3), (ga3, size_3), (gb3, size_3)):
        zero_planes(ref, (0, size + 1))
    third = 1.0 / 30.0

    def gather(at_x):
        for i in range(4):
            x = PAD + at_x * 4 + i
            for q in range(2):
                for at_z in range(0, count_z, 2):
                    one, two = (pieces_ref[at_x * count_z + at_z + d, i, q] for d in range(2))
                    first = row_of(one.shape) < 4
                    rows = slice(4 * at_z, 4 * at_z + 8)
                    b1[x, q, 0, rows] = jnp.where(first, one, pltpu.roll(two, 4, 0))
                    b1[x, q, 1, rows] = jnp.where(first, pltpu.roll(one, 4, 0), two)
            LEVEL_1.put(ub1, gb1, x, LEVEL_1.load(b1, x))

    each(0, count_x, gather, 4)

    def sweep(level, u_in, g_in, u_out, g_out, b):
        return lambda x: level.put(u_out, g_out, x, level.sweep(u_in, g_in, b, x, third))

    each(PAD, PAD + size_1, sweep(LEVEL_1, ub1, gb1, ua1, ga1, b1), 16)

    def restrict_1(x):
        fine = PAD + 2 * (x - 1)
        pair = add_planes(
            LEVEL_1.residual(ua1, ga1, b1, fine), LEVEL_1.residual(ua1, ga1, b1, fine + 1)
        )
        plane = scaled(join(pair), 0.5 * 0.2)
        store_plane(b2, x, plane)
        LEVEL_2.put(ub2, gb2, x, plane)

    each(1, 1 + size_2, restrict_1, 8)
    each(1, 1 + size_2, sweep(LEVEL_2, ub2, gb2, ua2, ga2, b2), 8)

    def restrict_2(x):
        fine = 1 + 2 * (x - 1)
        pair = add_planes(
            LEVEL_2.residual(ua2, ga2, b2, fine), LEVEL_2.residual(ua2, ga2, b2, fine + 1)
        )
        plane = [[join_within(pair[0][0]) * (0.5 * 0.2)]]
        store_plane(b3, x, plane)
        LEVEL_3.put(ub3, gb3, x, plane)

    each(1, 1 + size_3, restrict_2, 4)
    now, later = (ub3, gb3), (ua3, ga3)
    for _ in range(COARSE_SWEEPS - 1):
        each(1, 1 + size_3, sweep(LEVEL_3, *now, *later, b3), 4)
        now, later = later, now

    def prolong_3(x):
        for d in range(2):
            fine = 1 + 2 * (x - 1) + d
            LEVEL_2.put(ua2, ga2, fine, [[ua2[fine, 0, 0] + now[0][x, 0, 0]]])

    each(1, 1 + size_3, prolong_3, 4)
    each(1, 1 + size_2, sweep(LEVEL_2, ua2, ga2, ub2, gb2, b2), 8)
    each(1, 1 + size_2, sweep(LEVEL_2, ub2, gb2, ua2, ga2, b2), 8)

    def prolong_2(x):
        error = ua2[x, 0, 0]
        for d in range(2):
            fine = PAD + 2 * (x - 1) + d
            LEVEL_1.put(
                ua1, ga1, fine, [[t + error for t in line] for line in LEVEL_1.load(ua1, fine)]
            )

    each(1, 1 + size_2, prolong_2, 8)
    each(PAD, PAD + size_1, sweep(LEVEL_1, ua1, ga1, ub1, gb1, b1), 16)
    each(PAD, PAD + size_1, sweep(LEVEL_1, ub1, gb1, ua1, ga1, b1), 16)
    return ua1


def rim_masks(count_x, count_z, where_ref):
    at_x, at_z = where_ref[0], where_ref[1]
    k = row_of((8, LANES))
    low = (at_z > 0).astype(jnp.float32)
    high = (at_z < count_z - 1).astype(jnp.float32)
    rows = jnp.where(k < 4, 1.0, jnp.where(k < 6, high, low))
    below = (at_x > 0).astype(jnp.float32)
    above = (at_x < count_x - 1).astype(jnp.float32)
    return rows, below, above


def in_segments(lo, hi, body, masks, scale, chunk):
    rows, below, above = masks
    inner = rows * scale
    for start, end, weight in (
        (lo, min(hi, RIM), inner * below),
        (max(lo, RIM), min(hi, RIM + BRICK_X), inner),
        (max(lo, RIM + BRICK_X), hi, inner * above),
    ):
        if end > start:
            each(start, end, functools.partial(body, weight=weight), chunk)


def fine_sweep(u_in, g_in, u_out, g_out, b_ref, margin, masks):
    def body(x, weight):
        FINE.put(u_out, g_out, x, FINE.sweep(u_in, g_in, b_ref, x, weight))

    in_segments(margin, WIDE_X - margin, body, masks, 1.0 / 30.0, 4)


def add_correction(coarse_ref, count_z, where_ref, masks, u_in, u_out, g_out, margin):
    at_x, at_z = where_ref[0], where_ref[1]
    rows_1 = coarse_ref.shape[3]
    turn = lax.rem(rows_1 - 4 * at_z, rows_1)
    k = row_of((8, LANES))
    rows = masks[0]

    def body(i):
        error = []
        for q in range(2):
            line = []
            for p in range(2):
                turned = pltpu.roll(coarse_ref[4 * at_x + i, q, p], turn, 0)
                tile = jnp.where(k < 6, turned[0:8], turned[rows_1 - 8 : rows_1])
                line.append(tile * rows)
            error.append(line)
        for d in range(2):
            x = 2 * i + d
            plane = [
                [u_in[x, q, p] + error[q // 2][p // 2] for p in range(4)] for q in range(4)
            ]
            FINE.put(u_out, g_out, x, plane)

    each(margin // 2, (WIDE_X - margin) // 2, body, 3)


def send_residual(u_ref, g_ref, b_ref, out_ref):
    def body(i):
        x = RIM + 2 * i
        pair = add_planes(
            FINE.residual(u_ref, g_ref, b_ref, x), FINE.residual(u_ref, g_ref, b_ref, x + 1)
        )
        for q, (even, odd) in enumerate(join(pair)):
            out_ref[i, q] = 0.1 * jnp.where(row_of(even.shape) < 4, even, pltpu.roll(odd, 4, 0))

    each(0, BRICK_X // 2, body, BRICK_X // 2)


def swap_blocks(tiles):
    shape = tiles[0].shape
    lane = lane_of(shape)
    half = lane < 64
    even = (lane // 32) % 2 == 0
    a, b, c, d = tiles
    a, c = jnp.where(half, a, pltpu.roll(c, 64, 1)), jnp.where(half, pltpu.roll(a, 64, 1), c)
    b, d = jnp.where(half, b, pltpu.roll(d, 64, 1)), jnp.where(half, pltpu.roll(b, 64, 1), d)
    a, b = jnp.where(even, a, pltpu.roll(b, 32, 1)), jnp.where(even, pltpu.roll(a, 96, 1), b)
    c, d = jnp.where(even, c, pltpu.roll(d, 32, 1)), jnp.where(even, pltpu.roll(c, 96, 1), d)
    return [a, b, c, d]


def pick_lanes(tile, index):
    return jnp.take_along_axis(tile, index, axis=1, mode="promise_in_bounds")


def down_kernel(count_x, count_z, where_ref, low_ref, mid_ref, high_ref, u_ref, b_ref, out_ref,
                c_ref, g_ref, h_ref, rows_ref):
    masks = rim_masks(count_x, count_z, where_ref)
    lane = lane_of((8, LANES))
    index = (lane % 32) * 4 + lane // 32
    for part, ref in enumerate((low_ref, mid_ref, high_ref)):

        def convert(x, part=part, ref=ref):
            for r in range(0, WIDE_Z, 8):
                tiles = []
                for t in range(4):
                    tile = ref[x, r : r + 8, t * LANES : (t + 1) * LANES]
                    tiles.append(pick_lanes(tile, index))
                for p, tile in enumerate(swap_blocks(tiles)):
                    rows_ref[x, p, r : r + 8, :] = tile
            for q in range(4):
                for p in range(4):
                    c_ref[part * BRICK_X + x, q, p] = rows_ref[x, p, pl.ds(q, 8, stride=4), :]

        each(0, BRICK_X, convert, 8)

    def source(x, weight):
        here = FINE.load(c_ref, x)
        sums = along_z(here, 1, True)
        plane = []
        for q in range(4):
            y_sums = along_y(here[q], 1)
            line = []
            for p in range(4):
                face = (c_ref[x - 1, q, p] + c_ref[x + 1, q, p]) + (sums[q][p] + y_sums[p])
                line.append((here[q][p] * 6.0 + face) * weight)
            plane.append(line)
        FINE.put(b_ref, g_ref, x, plane)

    in_segments(1, WIDE_X - 1, source, masks, 0.2 / 12.0, 4)

    def body(x, weight):
        FINE.put(u_ref, h_ref, x, FINE.sweep(b_ref, g_ref, b_ref, x, weight))

    in_segments(2, WIDE_X - 2, body, masks, 1.0 / 30.0, 4)
    send_residual(u_ref, h_ref, b_ref, out_ref)


def middle_kernel(count_x, count_z, where_ref, pieces_ref, u_ref, b_ref, v_ref, out_ref,
                  ga_ref, gb_ref, ua_ref, *grids):
    masks = rim_masks(count_x, count_z, where_ref)
    coarse = coarse_solve(count_x, count_z, pieces_ref, grids)
    add_correction(coarse, count_z, where_ref, masks, u_ref, ua_ref, ga_ref, 2)
    fine_sweep(ua_ref, ga_ref, v_ref, gb_ref, b_ref, 3, masks)
    fine_sweep(v_ref, gb_ref, ua_ref, ga_ref, b_ref, 4, masks)
    fine_sweep(ua_ref, ga_ref, v_ref, gb_ref, b_ref, 5, masks)
    fine_sweep(v_ref, gb_ref, ua_ref, ga_ref, b_ref, 6, masks)

    def keep(x):
        store_plane(v_ref, x, FINE.load(ua_ref, x))

    each(6, WIDE_X - 6, keep, 2)
    send_residual(ua_ref, ga_ref, b_ref, out_ref)


def up_kernel(count_x, count_z, where_ref, pieces_ref, u_ref, b_ref, out_ref,
              ga_ref, gb_ref, ua_ref, ub_ref, rows_ref, *grids):
    masks = rim_masks(count_x, count_z, where_ref)
    coarse = coarse_solve(count_x, count_z, pieces_ref, grids)
    add_correction(coarse, count_z, where_ref, masks, u_ref, ua_ref, ga_ref, 6)
    fine_sweep(ua_ref, ga_ref, ub_ref, gb_ref, b_ref, 7, masks)
    lane = lane_of((8, LANES))
    index = (lane % 4) * 32 + lane // 4

    def body(x):
        plane = FINE.sweep(ub_ref, gb_ref, b_ref, x, 1.0 / 30.0)
        for q in range(4):
            for t, tile in enumerate(swap_blocks(plane[q])):
                rows = pick_lanes(tile, index)[0:4]
                rows_ref[x - RIM, t, pl.ds(q, 4, stride=4), :] = rows
        for t in range(4):
            out_ref[x - RIM, :, t * LANES : (t + 1) * LANES] = rows_ref[x - RIM, t]

    each(RIM, RIM + BRICK_X, body, 4)


def call(kernel, outputs, scratch):
    shapes = [jax.ShapeDtypeStruct(shape, jnp.float32) for shape in outputs]
    return lambda where, *arrays: pl.pallas_call(
        kernel,
        out_shape=shapes,
        in_specs=[pl.BlockSpec(memory_space=pltpu.SMEM)]
        + [pl.BlockSpec(memory_space=pltpu.VMEM)] * len(arrays),
        out_specs=[pl.BlockSpec(memory_space=pltpu.VMEM)] * len(shapes),
        scratch_shapes=scratch,
        compiler_params=pltpu.CompilerParams(vmem_limit_bytes=VMEM_BYTES),
    )(where, *arrays)


def both_ways(axis, to_next, to_last):
    count = lax.axis_size(axis)
    forward = [(i, i + 1) for i in range(count - 1)]
    backward = [(target, source) for source, target in forward]
    return lax.ppermute(to_next, axis, forward), lax.ppermute(to_last, axis, backward)


def every_piece_by_axes(piece):
    line = lax.all_to_all(
        jnp.broadcast_to(piece[None], (lax.axis_size("gz"),) + piece.shape), "gz", 0, 0
    )
    grid = lax.all_to_all(
        jnp.broadcast_to(line[None], (lax.axis_size("gx"),) + line.shape), "gx", 0, 0
    )
    return grid.reshape((-1,) + piece.shape)


def per_device(charges):
    count_x, count_z = lax.axis_size("gx"), lax.axis_size("gz")
    where = jnp.stack([lax.axis_index("gx"), lax.axis_index("gz")]).astype(jnp.int32)
    low, high = both_ways("gz", charges[:, BRICK_Z - RIM :], charges[:, :RIM])
    middle = jnp.concatenate([charges, high, low], axis=1)
    below, above = both_ways("gx", middle, middle)

    wide = (WIDE_X, 4, 4, 8, LANES)
    piece_shape = (BRICK_X // 2, 2, 8, LANES)
    fine = pltpu.VMEM(wide, jnp.float32)
    grids = coarse_grids(count_x, count_z)
    rows_in = pltpu.VMEM((BRICK_X, 4, WIDE_Z, LANES), jnp.float32)
    rows_out = pltpu.VMEM((BRICK_X, 4, BRICK_Z, LANES), jnp.float32)

    u, b, piece = call(
        functools.partial(down_kernel, count_x, count_z), [wide, wide, piece_shape], [fine] * 3 + [rows_in]
    )(where, below, middle, above)
    gathered = every_piece_by_axes(piece)
    u, piece = call(
        functools.partial(middle_kernel, count_x, count_z), [wide, piece_shape], [fine] * 3 + grids
    )(where, gathered, u, b)
    gathered = lax.all_gather(piece, ("gx", "gz"), axis=0)
    (potential,) = call(
        functools.partial(up_kernel, count_x, count_z), [charges.shape], [fine] * 4 + [rows_out] + grids
    )(where, gathered, u, b)
    return potential


def solution(mesh):
    return jax.shard_map(
        per_device,
        mesh=mesh,
        in_specs=(P(("groups", "gx"), "gz", None),),
        out_specs=P(("groups", "gx"), "gz", None),
        check_vma=False,
    )
```

```python
import functools

import jax
import jax.numpy as jnp
from jax import lax
from jax.experimental import pallas as pl
from jax.experimental.pallas import tpu as pltpu
from jax.sharding import PartitionSpec as P

COARSE_SWEEPS = 8
LANES = 128
RIM = 8
BRICK_X = 8
BRICK_Z = 16
WIDE_X = BRICK_X + 2 * RIM
WIDE_Z = BRICK_Z + 2 * RIM
VMEM_BYTES = 48 * 1024 * 1024


def lane_of(shape):
    return lax.broadcasted_iota(jnp.int32, shape, len(shape) - 1)


def row_of(shape):
    return lax.broadcasted_iota(jnp.int32, shape, len(shape) - 2)


def next_row(tile, step, cyclic):
    rows = tile.shape[0]
    moved = pltpu.roll(tile, rows - step, 0)
    return moved if cyclic else jnp.where(row_of(tile.shape) < rows - step, moved, 0.0)


def last_row(tile, step, cyclic):
    moved = pltpu.roll(tile, step, 0)
    return moved if cyclic else jnp.where(row_of(tile.shape) >= step, moved, 0.0)


def next_lane(tile, step):
    moved = pltpu.roll(tile, LANES - step, 1)
    return jnp.where(lane_of(tile.shape) < LANES - step, moved, 0.0)


def last_lane(tile, step):
    moved = pltpu.roll(tile, step, 1)
    return jnp.where(lane_of(tile.shape) >= step, moved, 0.0)


def load_plane(ref, x, count_q, count_p):
    return [[ref[x, q, p] for p in range(count_p)] for q in range(count_q)]


def store_plane(ref, x, plane):
    for q, line in enumerate(plane):
        for p, tile in enumerate(line):
            ref[x, q, p] = tile


def along_z(plane, step, cyclic):
    count_q, count_p = len(plane), len(plane[0])
    result = []
    for q in range(count_q):
        line = []
        for p in range(count_p):
            after = plane[q + 1][p] if q + 1 < count_q else next_row(plane[0][p], step, cyclic)
            before = plane[q - 1][p] if q > 0 else last_row(plane[-1][p], step, cyclic)
            line.append(after + before)
        result.append(line)
    return result


def along_y(line, step):
    count_p = len(line)
    result = []
    for p in range(count_p):
        after = line[p + 1] if p + 1 < count_p else next_lane(line[0], step)
        before = line[p - 1] if p > 0 else last_lane(line[-1], step)
        result.append(after + before)
    return result


class Level:
    def __init__(self, count_q, count_p, step, cyclic):
        self.count_q, self.count_p, self.step, self.cyclic = count_q, count_p, step, cyclic

    def load(self, ref, x):
        return load_plane(ref, x, self.count_q, self.count_p)

    def put(self, u_ref, g_ref, x, plane):
        store_plane(u_ref, x, plane)
        sums = along_z(plane, self.step, self.cyclic)
        store_plane(
            g_ref,
            x,
            [
                [s + (v + v) for s, v in zip(sum_line, line)]
                for sum_line, line in zip(sums, plane)
            ],
        )

    def spread(self, u_ref, g_ref, x):
        result = []
        for q in range(self.count_q):
            sides, both = [], []
            for p in range(self.count_p):
                here = g_ref[x, q, p]
                sides.append((u_ref[x - 1, q, p] + u_ref[x + 1, q, p]) + here)
                both.append((g_ref[x - 1, q, p] + g_ref[x + 1, q, p]) + (here + here))
            result.append([a + b for a, b in zip(both, along_y(sides, self.step))])
        return result

    def sweep(self, u_ref, g_ref, b_ref, x, weight):
        wide = self.spread(u_ref, g_ref, x)
        return [
            [
                u_ref[x, q, p] * (1.0 / 15.0) + b_ref[x, q, p] + wide[q][p] * weight
                for p in range(self.count_p)
            ]
            for q in range(self.count_q)
        ]

    def residual(self, u_ref, g_ref, b_ref, x):
        wide = self.spread(u_ref, g_ref, x)
        return [
            [
                b_ref[x, q, p] * 5.0 + (wide[q][p] - u_ref[x, q, p] * 28.0) * (1.0 / 6.0)
                for p in range(self.count_p)
            ]
            for q in range(self.count_q)
        ]


def add_planes(one, other):
    return [[a + b for a, b in zip(l, m)] for l, m in zip(one, other)]


def join(plane):
    lines = [[a + b for a, b in zip(plane[q], plane[q + 1])] for q in range(0, len(plane), 2)]
    return [[line[p] + line[p + 1] for p in range(0, len(line), 2)] for line in lines]


def join_within(tile):
    rows = tile.shape[0]
    even = row_of(tile.shape) % 2 == 0
    tile = tile + jnp.where(even, pltpu.roll(tile, rows - 1, 0), pltpu.roll(tile, 1, 0))
    even = lane_of(tile.shape) % 2 == 0
    return tile + jnp.where(even, pltpu.roll(tile, LANES - 1, 1), pltpu.roll(tile, 1, 1))


def scaled(plane, factor):
    return [[tile * factor for tile in line] for line in plane]


def each(lo, hi, body, chunk):
    count = hi - lo
    whole = count // chunk
    if whole == 1:
        for x in range(lo, lo + chunk):
            body(x)
    elif whole > 1:

        def step(i, carry):
            for d in range(chunk):
                body(lo + i * chunk + d)
            return carry

        lax.fori_loop(0, whole, step, 0)
    for x in range(lo + whole * chunk, hi):
        body(x)


FINE = Level(4, 4, 1, True)
LEVEL_1 = Level(2, 2, 1, False)
LEVEL_2 = Level(1, 1, 1, False)
LEVEL_3 = Level(1, 1, 2, False)
PAD = RIM // 2


def zero_planes(ref, indices):
    for x in indices:
        ref[x] = jnp.zeros(ref.shape[1:], ref.dtype)


def coarse_grids(count_x, count_z):
    rows = count_z * BRICK_Z // 4
    shapes = []
    for planes, count in ((4 * count_x + 2 * PAD, 2), (2 * count_x + 2, 1), (count_x + 2, 1)):
        shapes += [pltpu.VMEM((planes, count, count, rows, LANES), jnp.float32)] * 5
    return shapes


def coarse_solve(count_x, count_z, where_ref, pieces, grids):
    (ua1, ub1, ga1, gb1, b1), (ua2, ub2, ga2, gb2, b2), (ua3, ub3, ga3, gb3, b3) = (
        grids[0:5],
        grids[5:10],
        grids[10:15],
    )
    size_1, size_2, size_3 = 4 * count_x, 2 * count_x, count_x
    for ref in (ua1, ub1, ga1, gb1):
        zero_planes(ref, list(range(PAD)) + list(range(PAD + size_1, PAD + size_1 + PAD)))
    for ref, size in ((ua2, size_2), (ub2, size_2), (ga2, size_2), (gb2, size_2)):
        zero_planes(ref, (0, size + 1))
    for ref, size in ((ua3, size_3), (ub3, size_3), (ga3, size_3), (gb3, size_3)):
        zero_planes(ref, (0, size + 1))
    third = 1.0 / 30.0

    at_x, at_z = where_ref[0], where_ref[1]

    def place(x, load):
        for i in range(4):
            for q in range(2):
                for z in range(0, count_z, 2):
                    one, two = load(z, i, q), load(z + 1, i, q)
                    first = row_of(one.shape) < 4
                    rows = slice(4 * z, 4 * z + 8)
                    b1[x + i, q, 0, rows] = jnp.where(first, one, pltpu.roll(two, 4, 0))
                    b1[x + i, q, 1, rows] = jnp.where(first, pltpu.roll(one, 4, 0), two)
            LEVEL_1.put(ub1, gb1, x + i, LEVEL_1.load(b1, x + i))

    if len(pieces) == 1:

        def gather(n):
            place(PAD + 4 * n, lambda z, i, q: pieces[0][n * count_z + z, i, q])

        each(0, count_x, gather, 1)
    else:

        def gather(n):
            for core in range(2):
                x = PAD + 4 * ((2 * n + core) ^ at_x)
                place(x, lambda z, i, q: pieces[core][n * count_z + (z ^ at_z), i, q])

        each(0, count_x // 2, gather, 1)

    def sweep(level, u_in, g_in, u_out, g_out, b):
        return lambda x: level.put(u_out, g_out, x, level.sweep(u_in, g_in, b, x, third))

    each(PAD, PAD + size_1, sweep(LEVEL_1, ub1, gb1, ua1, ga1, b1), 8)

    def restrict_1(x):
        fine = PAD + 2 * (x - 1)
        pair = add_planes(
            LEVEL_1.residual(ua1, ga1, b1, fine), LEVEL_1.residual(ua1, ga1, b1, fine + 1)
        )
        plane = scaled(join(pair), 0.5 * 0.2)
        store_plane(b2, x, plane)
        LEVEL_2.put(ub2, gb2, x, plane)

    each(1, 1 + size_2, restrict_1, 8)
    each(1, 1 + size_2, sweep(LEVEL_2, ub2, gb2, ua2, ga2, b2), 8)

    def restrict_2(x):
        fine = 1 + 2 * (x - 1)
        pair = add_planes(
            LEVEL_2.residual(ua2, ga2, b2, fine), LEVEL_2.residual(ua2, ga2, b2, fine + 1)
        )
        plane = [[join_within(pair[0][0]) * (0.5 * 0.2)]]
        store_plane(b3, x, plane)
        LEVEL_3.put(ub3, gb3, x, plane)

    each(1, 1 + size_3, restrict_2, 4)
    now, later = (ub3, gb3), (ua3, ga3)
    for _ in range(COARSE_SWEEPS - 1):
        each(1, 1 + size_3, sweep(LEVEL_3, *now, *later, b3), 4)
        now, later = later, now

    def prolong_3(x):
        for d in range(2):
            fine = 1 + 2 * (x - 1) + d
            LEVEL_2.put(ua2, ga2, fine, [[ua2[fine, 0, 0] + now[0][x, 0, 0]]])

    each(1, 1 + size_3, prolong_3, 4)
    each(1, 1 + size_2, sweep(LEVEL_2, ua2, ga2, ub2, gb2, b2), 8)
    each(1, 1 + size_2, sweep(LEVEL_2, ub2, gb2, ua2, ga2, b2), 8)

    def prolong_2(x):
        error = ua2[x, 0, 0]
        for d in range(2):
            fine = PAD + 2 * (x - 1) + d
            LEVEL_1.put(
                ua1, ga1, fine, [[t + error for t in line] for line in LEVEL_1.load(ua1, fine)]
            )

    each(1, 1 + size_2, prolong_2, 8)
    each(PAD, PAD + size_1, sweep(LEVEL_1, ua1, ga1, ub1, gb1, b1), 8)
    each(PAD, PAD + size_1, sweep(LEVEL_1, ub1, gb1, ua1, ga1, b1), 8)
    return ua1


def rim_masks(count_x, count_z, where_ref):
    at_x, at_z = where_ref[0], where_ref[1]
    k = row_of((8, LANES))
    low = (at_z > 0).astype(jnp.float32)
    high = (at_z < count_z - 1).astype(jnp.float32)
    rows = jnp.where(k < 4, 1.0, jnp.where(k < 6, high, low))
    below = (at_x > 0).astype(jnp.float32)
    above = (at_x < count_x - 1).astype(jnp.float32)
    return rows, below, above


def in_segments(lo, hi, body, masks, scale, chunk):
    rows, below, above = masks
    inner = rows * scale
    for start, end, weight in (
        (lo, min(hi, RIM), inner * below),
        (max(lo, RIM), min(hi, RIM + BRICK_X), inner),
        (max(lo, RIM + BRICK_X), hi, inner * above),
    ):
        if end > start:
            each(start, end, functools.partial(body, weight=weight), chunk)


def fine_sweep(u_in, g_in, u_out, g_out, b_ref, margin, masks):
    def body(x, weight):
        FINE.put(u_out, g_out, x, FINE.sweep(u_in, g_in, b_ref, x, weight))

    in_segments(margin, WIDE_X - margin, body, masks, 1.0 / 30.0, 4)


def add_correction(coarse_ref, count_z, where_ref, masks, u_in, u_out, g_out, margin):
    at_x, at_z = where_ref[0], where_ref[1]
    rows_1 = coarse_ref.shape[3]
    turn = lax.rem(rows_1 - 4 * at_z, rows_1)
    k = row_of((8, LANES))
    rows = masks[0]

    def body(i):
        error = []
        for q in range(2):
            line = []
            for p in range(2):
                turned = pltpu.roll(coarse_ref[4 * at_x + i, q, p], turn, 0)
                tile = jnp.where(k < 6, turned[0:8], turned[rows_1 - 8 : rows_1])
                line.append(tile * rows)
            error.append(line)
        for d in range(2):
            x = 2 * i + d
            plane = [
                [u_in[x, q, p] + error[q // 2][p // 2] for p in range(4)] for q in range(4)
            ]
            FINE.put(u_out, g_out, x, plane)

    each(margin // 2, (WIDE_X - margin) // 2, body, 3)


def send_residual(u_ref, g_ref, b_ref, out_ref):
    def body(i):
        x = RIM + 2 * i
        pair = add_planes(
            FINE.residual(u_ref, g_ref, b_ref, x), FINE.residual(u_ref, g_ref, b_ref, x + 1)
        )
        for q, (even, odd) in enumerate(join(pair)):
            out_ref[i, q] = 0.1 * jnp.where(row_of(even.shape) < 4, even, pltpu.roll(odd, 4, 0))

    each(0, BRICK_X // 2, body, BRICK_X // 2)


def swap_blocks(tiles):
    shape = tiles[0].shape
    lane = lane_of(shape)
    half = lane < 64
    even = (lane // 32) % 2 == 0
    a, b, c, d = tiles
    a, c = jnp.where(half, a, pltpu.roll(c, 64, 1)), jnp.where(half, pltpu.roll(a, 64, 1), c)
    b, d = jnp.where(half, b, pltpu.roll(d, 64, 1)), jnp.where(half, pltpu.roll(b, 64, 1), d)
    a, b = jnp.where(even, a, pltpu.roll(b, 32, 1)), jnp.where(even, pltpu.roll(a, 96, 1), b)
    c, d = jnp.where(even, c, pltpu.roll(d, 32, 1)), jnp.where(even, pltpu.roll(c, 96, 1), d)
    return [a, b, c, d]


def pick_lanes(tile, index):
    return jnp.take_along_axis(tile, index, axis=1, mode="promise_in_bounds")


def down_kernel(count_x, count_z, where_ref, mid_ref, one_ref, two_ref, u_ref, b_ref, out_ref,
                c_ref, g_ref, h_ref, rows_ref):
    masks = rim_masks(count_x, count_z, where_ref)
    lane = lane_of((8, LANES))
    index = (lane % 32) * 4 + lane // 32
    odd = where_ref[0] % 2

    def convert_from(ref, part):
        def convert(x):
            for r in range(0, WIDE_Z, 8):
                tiles = []
                for t in range(4):
                    tile = ref[x, r : r + 8, t * LANES : (t + 1) * LANES]
                    tiles.append(pick_lanes(tile, index))
                for p, tile in enumerate(swap_blocks(tiles)):
                    rows_ref[x, p, r : r + 8, :] = tile
            for q in range(4):
                for p in range(4):
                    c_ref[part * BRICK_X + x, q, p] = rows_ref[x, p, pl.ds(q, 8, stride=4), :]

        each(0, BRICK_X, convert, 2)

    convert_from(mid_ref, 1)
    convert_from(one_ref, 2 - 2 * odd)
    convert_from(two_ref, 2 * odd)

    def source(x, weight):
        here = FINE.load(c_ref, x)
        sums = along_z(here, 1, True)
        plane = []
        for q in range(4):
            y_sums = along_y(here[q], 1)
            line = []
            for p in range(4):
                face = (c_ref[x - 1, q, p] + c_ref[x + 1, q, p]) + (sums[q][p] + y_sums[p])
                line.append((here[q][p] * 6.0 + face) * weight)
            plane.append(line)
        FINE.put(b_ref, g_ref, x, plane)

    in_segments(1, WIDE_X - 1, source, masks, 0.2 / 12.0, 4)

    def body(x, weight):
        FINE.put(u_ref, h_ref, x, FINE.sweep(b_ref, g_ref, b_ref, x, weight))

    in_segments(2, WIDE_X - 2, body, masks, 1.0 / 30.0, 4)
    send_residual(u_ref, h_ref, b_ref, out_ref)


def middle_kernel(count_x, count_z, count_pieces, where_ref, *refs):
    pieces, refs = refs[:count_pieces], refs[count_pieces:]
    u_ref, b_ref, v_ref, out_ref, ga_ref, gb_ref, ua_ref, *grids = refs
    masks = rim_masks(count_x, count_z, where_ref)
    coarse = coarse_solve(count_x, count_z, where_ref, pieces, grids)
    add_correction(coarse, count_z, where_ref, masks, u_ref, ua_ref, ga_ref, 2)
    fine_sweep(ua_ref, ga_ref, v_ref, gb_ref, b_ref, 3, masks)
    fine_sweep(v_ref, gb_ref, ua_ref, ga_ref, b_ref, 4, masks)
    fine_sweep(ua_ref, ga_ref, v_ref, gb_ref, b_ref, 5, masks)
    fine_sweep(v_ref, gb_ref, ua_ref, ga_ref, b_ref, 6, masks)

    def keep(x):
        store_plane(v_ref, x, FINE.load(ua_ref, x))

    each(6, WIDE_X - 6, keep, 2)
    send_residual(ua_ref, ga_ref, b_ref, out_ref)


def up_kernel(count_x, count_z, count_pieces, where_ref, *refs):
    pieces, refs = refs[:count_pieces], refs[count_pieces:]
    u_ref, b_ref, out_ref, ga_ref, gb_ref, ua_ref, ub_ref, rows_ref, *grids = refs
    masks = rim_masks(count_x, count_z, where_ref)
    coarse = coarse_solve(count_x, count_z, where_ref, pieces, grids)
    add_correction(coarse, count_z, where_ref, masks, u_ref, ua_ref, ga_ref, 6)
    fine_sweep(ua_ref, ga_ref, ub_ref, gb_ref, b_ref, 7, masks)
    lane = lane_of((8, LANES))
    index = (lane % 4) * 32 + lane // 4

    def body(x):
        plane = FINE.sweep(ub_ref, gb_ref, b_ref, x, 1.0 / 30.0)
        for q in range(4):
            for t, tile in enumerate(swap_blocks(plane[q])):
                rows = pick_lanes(tile, index)[0:4]
                rows_ref[x - RIM, t, pl.ds(q, 4, stride=4), :] = rows
        for t in range(4):
            out_ref[x - RIM, :, t * LANES : (t + 1) * LANES] = rows_ref[x - RIM, t]

    each(RIM, RIM + BRICK_X, body, 4)


def call(kernel, outputs, scratch):
    shapes = [jax.ShapeDtypeStruct(shape, jnp.float32) for shape in outputs]
    return lambda where, *arrays: pl.pallas_call(
        kernel,
        out_shape=shapes,
        in_specs=[pl.BlockSpec(memory_space=pltpu.SMEM)]
        + [pl.BlockSpec(memory_space=pltpu.VMEM)] * len(arrays),
        out_specs=[pl.BlockSpec(memory_space=pltpu.VMEM)] * len(shapes),
        scratch_shapes=scratch,
        compiler_params=pltpu.CompilerParams(vmem_limit_bytes=VMEM_BYTES),
    )(where, *arrays)


def swap(axis, values, distance):
    count = lax.axis_size(axis)
    return lax.ppermute(values, axis, [(i, i ^ distance) for i in range(count)])


def swap_shifted(axis, values):
    pairs = [(i, i + 1) for i in range(1, lax.axis_size(axis) - 1, 2)]
    return lax.ppermute(values, axis, pairs + [(target, source) for source, target in pairs])


def every_piece(piece):
    count = lax.axis_size("gx") * lax.axis_size("gz")
    return (lax.all_to_all(jnp.broadcast_to(piece[None], (count,) + piece.shape), ("gx", "gz"), 0, 0),)


def every_piece_by_doubling(piece):
    held = piece[None]
    distance = 1
    while distance < lax.axis_size("gz"):
        held = jnp.concatenate([held, swap("gz", held, distance)])
        distance *= 2
    distance = 2
    while distance < lax.axis_size("gx"):
        held = jnp.concatenate([held, swap("gx", held, distance)])
        distance *= 2
    return held, swap("gx", held, 1)


def per_device(charges):
    count_x, count_z = lax.axis_size("gx"), lax.axis_size("gz")
    at_x, at_z = lax.axis_index("gx"), lax.axis_index("gz")
    where = jnp.stack([at_x, at_z]).astype(jnp.int32)
    even = at_z % 2 == 0
    first, last = charges[:, :RIM], charges[:, BRICK_Z - RIM :]
    one = swap("gz", jnp.where(even, last, first), 1)
    two = swap_shifted("gz", jnp.where(even, first, last))
    middle = jnp.concatenate(
        [charges, jnp.where(even, one, two), jnp.where(even, two, one)], axis=1
    )
    far = swap_shifted("gx", middle)
    near = swap("gx", middle, 1)

    wide = (WIDE_X, 4, 4, 8, LANES)
    piece_shape = (BRICK_X // 2, 2, 8, LANES)
    fine = pltpu.VMEM(wide, jnp.float32)
    grids = coarse_grids(count_x, count_z)
    rows_in = pltpu.VMEM((BRICK_X, 4, WIDE_Z, LANES), jnp.float32)
    rows_out = pltpu.VMEM((BRICK_X, 4, BRICK_Z, LANES), jnp.float32)

    u, b, piece = call(
        functools.partial(down_kernel, count_x, count_z),
        [wide, wide, piece_shape],
        [fine] * 3 + [rows_in],
    )(where, middle, near, far)
    pieces = every_piece(piece)
    u, piece = call(
        functools.partial(middle_kernel, count_x, count_z, len(pieces)),
        [wide, piece_shape],
        [fine] * 3 + grids,
    )(where, *pieces, u, b)
    pieces = every_piece_by_doubling(piece)
    (potential,) = call(
        functools.partial(up_kernel, count_x, count_z, len(pieces)),
        [charges.shape],
        [fine] * 4 + [rows_out] + grids,
    )(where, *pieces, u, b)
    return potential


def solution(mesh):
    return jax.shard_map(
        per_device,
        mesh=mesh,
        in_specs=(P(("groups", "gx"), "gz", None),),
        out_specs=P(("groups", "gx"), "gz", None),
        check_vma=False,
    )
```

```python
import functools
import math

import jax
import jax.numpy as jnp
from jax import lax
from jax.experimental import pallas as pl
from jax.experimental.pallas import tpu as pltpu
from jax.sharding import PartitionSpec as P

COARSE_SWEEPS = 8
LANES = 128
RIM = 8
BRICK_X = 8
BRICK_Z = 16
WIDE_X = BRICK_X + 2 * RIM
WIDE_Z = BRICK_Z + 2 * RIM
SPARE_BYTES = 4 * 1024 * 1024


def lane_of(shape):
    return lax.broadcasted_iota(jnp.int32, shape, len(shape) - 1)


def row_of(shape):
    return lax.broadcasted_iota(jnp.int32, shape, len(shape) - 2)


def next_row(tile, step, cyclic):
    rows = tile.shape[0]
    moved = pltpu.roll(tile, rows - step, 0)
    return moved if cyclic else jnp.where(row_of(tile.shape) < rows - step, moved, 0.0)


def last_row(tile, step, cyclic):
    moved = pltpu.roll(tile, step, 0)
    return moved if cyclic else jnp.where(row_of(tile.shape) >= step, moved, 0.0)


def next_lane(tile, step):
    moved = pltpu.roll(tile, LANES - step, 1)
    return jnp.where(lane_of(tile.shape) < LANES - step, moved, 0.0)


def last_lane(tile, step):
    moved = pltpu.roll(tile, step, 1)
    return jnp.where(lane_of(tile.shape) >= step, moved, 0.0)


def load_plane(ref, x, count_q, count_p):
    return [[ref[x, q, p] for p in range(count_p)] for q in range(count_q)]


def store_plane(ref, x, plane):
    for q, line in enumerate(plane):
        for p, tile in enumerate(line):
            ref[x, q, p] = tile


def along_z(plane, step, cyclic):
    count_q, count_p = len(plane), len(plane[0])
    result = []
    for q in range(count_q):
        line = []
        for p in range(count_p):
            after = plane[q + 1][p] if q + 1 < count_q else next_row(plane[0][p], step, cyclic)
            before = plane[q - 1][p] if q > 0 else last_row(plane[-1][p], step, cyclic)
            line.append(after + before)
        result.append(line)
    return result


def along_y(line, step):
    count_p = len(line)
    result = []
    for p in range(count_p):
        after = line[p + 1] if p + 1 < count_p else next_lane(line[0], step)
        before = line[p - 1] if p > 0 else last_lane(line[-1], step)
        result.append(after + before)
    return result


class Level:
    def __init__(self, count_q, count_p, step, cyclic):
        self.count_q, self.count_p, self.step, self.cyclic = count_q, count_p, step, cyclic

    def load(self, ref, x):
        return load_plane(ref, x, self.count_q, self.count_p)

    def put(self, u_ref, g_ref, x, plane):
        store_plane(u_ref, x, plane)
        sums = along_z(plane, self.step, self.cyclic)
        store_plane(
            g_ref,
            x,
            [
                [s + (v + v) for s, v in zip(sum_line, line)]
                for sum_line, line in zip(sums, plane)
            ],
        )

    def spread(self, u_ref, g_ref, x):
        result = []
        for q in range(self.count_q):
            sides, both = [], []
            for p in range(self.count_p):
                here = g_ref[x, q, p]
                sides.append((u_ref[x - 1, q, p] + u_ref[x + 1, q, p]) + here)
                both.append((g_ref[x - 1, q, p] + g_ref[x + 1, q, p]) + (here + here))
            result.append([a + b for a, b in zip(both, along_y(sides, self.step))])
        return result

    def sweep(self, u_ref, g_ref, b_ref, x, weight):
        wide = self.spread(u_ref, g_ref, x)
        return [
            [
                u_ref[x, q, p] * (1.0 / 15.0) + b_ref[x, q, p] + wide[q][p] * weight
                for p in range(self.count_p)
            ]
            for q in range(self.count_q)
        ]

    def residual(self, u_ref, g_ref, b_ref, x):
        wide = self.spread(u_ref, g_ref, x)
        return [
            [
                b_ref[x, q, p] * 5.0 + (wide[q][p] - u_ref[x, q, p] * 28.0) * (1.0 / 6.0)
                for p in range(self.count_p)
            ]
            for q in range(self.count_q)
        ]


def add_planes(one, other):
    return [[a + b for a, b in zip(l, m)] for l, m in zip(one, other)]


def join(plane):
    lines = [[a + b for a, b in zip(plane[q], plane[q + 1])] for q in range(0, len(plane), 2)]
    return [[line[p] + line[p + 1] for p in range(0, len(line), 2)] for line in lines]


def join_within(tile):
    rows = tile.shape[0]
    even = row_of(tile.shape) % 2 == 0
    tile = tile + jnp.where(even, pltpu.roll(tile, rows - 1, 0), pltpu.roll(tile, 1, 0))
    even = lane_of(tile.shape) % 2 == 0
    return tile + jnp.where(even, pltpu.roll(tile, LANES - 1, 1), pltpu.roll(tile, 1, 1))


def scaled(plane, factor):
    return [[tile * factor for tile in line] for line in plane]


def each(lo, hi, body, chunk):
    count = hi - lo
    whole = count // chunk
    if whole == 1:
        for x in range(lo, lo + chunk):
            body(x)
    elif whole > 1:

        def step(i, carry):
            for d in range(chunk):
                body(lo + i * chunk + d)
            return carry

        lax.fori_loop(0, whole, step, 0)
    for x in range(lo + whole * chunk, hi):
        body(x)


FINE = Level(4, 4, 1, True)
LEVEL_1 = Level(2, 2, 1, False)
LEVEL_2 = Level(1, 1, 1, False)
LEVEL_3 = Level(1, 1, 2, False)
PAD = RIM // 2


def zero_planes(ref, indices):
    for x in indices:
        ref[x] = jnp.zeros(ref.shape[1:], ref.dtype)


def coarse_grids(count_x, count_z):
    rows = count_z * BRICK_Z // 4
    shapes = []
    for planes, count in ((4 * count_x + 2 * PAD, 2), (2 * count_x + 2, 1), (count_x + 2, 1)):
        shapes += [pltpu.VMEM((planes, count, count, rows, LANES), jnp.float32)] * 5
    return shapes


def coarse_solve(count_x, count_z, where_ref, pieces, grids):
    (ua1, ub1, ga1, gb1, b1), (ua2, ub2, ga2, gb2, b2), (ua3, ub3, ga3, gb3, b3) = (
        grids[0:5],
        grids[5:10],
        grids[10:15],
    )
    size_1, size_2, size_3 = 4 * count_x, 2 * count_x, count_x
    for ref in (ua1, ub1, ga1, gb1):
        zero_planes(ref, list(range(PAD)) + list(range(PAD + size_1, PAD + size_1 + PAD)))
    for ref, size in ((ua2, size_2), (ub2, size_2), (ga2, size_2), (gb2, size_2)):
        zero_planes(ref, (0, size + 1))
    for ref, size in ((ua3, size_3), (ub3, size_3), (ga3, size_3), (gb3, size_3)):
        zero_planes(ref, (0, size + 1))
    third = 1.0 / 30.0

    at_x, at_z = where_ref[0], where_ref[1]

    def place(x, load):
        for i in range(4):
            for q in range(2):
                for z in range(0, count_z, 2):
                    one, two = load(z, i, q), load(z + 1, i, q)
                    first = row_of(one.shape) < 4
                    rows = slice(4 * z, 4 * z + 8)
                    b1[x + i, q, 0, rows] = jnp.where(first, one, pltpu.roll(two, 4, 0))
                    b1[x + i, q, 1, rows] = jnp.where(first, pltpu.roll(one, 4, 0), two)
            LEVEL_1.put(ub1, gb1, x + i, LEVEL_1.load(b1, x + i))

    if len(pieces) == 1:

        def gather(n):
            place(PAD + 4 * n, lambda z, i, q: pieces[0][n * count_z + z, i, q])

        each(0, count_x, gather, 1)
    else:

        def gather(n):
            for core in range(2):
                x = PAD + 4 * ((2 * n + core) ^ at_x)
                place(x, lambda z, i, q: pieces[core][n * count_z + (z ^ at_z), i, q])

        each(0, count_x // 2, gather, 1)

    def sweep(level, u_in, g_in, u_out, g_out, b):
        return lambda x: level.put(u_out, g_out, x, level.sweep(u_in, g_in, b, x, third))

    each(PAD, PAD + size_1, sweep(LEVEL_1, ub1, gb1, ua1, ga1, b1), 8)

    def restrict_1(x):
        fine = PAD + 2 * (x - 1)
        pair = add_planes(
            LEVEL_1.residual(ua1, ga1, b1, fine), LEVEL_1.residual(ua1, ga1, b1, fine + 1)
        )
        plane = scaled(join(pair), 0.5 * 0.2)
        store_plane(b2, x, plane)
        LEVEL_2.put(ub2, gb2, x, plane)

    each(1, 1 + size_2, restrict_1, 8)
    each(1, 1 + size_2, sweep(LEVEL_2, ub2, gb2, ua2, ga2, b2), 8)

    def restrict_2(x):
        fine = 1 + 2 * (x - 1)
        pair = add_planes(
            LEVEL_2.residual(ua2, ga2, b2, fine), LEVEL_2.residual(ua2, ga2, b2, fine + 1)
        )
        plane = [[join_within(pair[0][0]) * (0.5 * 0.2)]]
        store_plane(b3, x, plane)
        LEVEL_3.put(ub3, gb3, x, plane)

    each(1, 1 + size_3, restrict_2, 4)
    now, later = (ub3, gb3), (ua3, ga3)
    for _ in range(COARSE_SWEEPS - 1):
        each(1, 1 + size_3, sweep(LEVEL_3, *now, *later, b3), 4)
        now, later = later, now

    def prolong_3(x):
        for d in range(2):
            fine = 1 + 2 * (x - 1) + d
            LEVEL_2.put(ua2, ga2, fine, [[ua2[fine, 0, 0] + now[0][x, 0, 0]]])

    each(1, 1 + size_3, prolong_3, 4)
    each(1, 1 + size_2, sweep(LEVEL_2, ua2, ga2, ub2, gb2, b2), 8)
    each(1, 1 + size_2, sweep(LEVEL_2, ub2, gb2, ua2, ga2, b2), 8)

    def prolong_2(x):
        error = ua2[x, 0, 0]
        for d in range(2):
            fine = PAD + 2 * (x - 1) + d
            LEVEL_1.put(
                ua1, ga1, fine, [[t + error for t in line] for line in LEVEL_1.load(ua1, fine)]
            )

    each(1, 1 + size_2, prolong_2, 8)
    each(PAD, PAD + size_1, sweep(LEVEL_1, ua1, ga1, ub1, gb1, b1), 8)
    each(PAD, PAD + size_1, sweep(LEVEL_1, ub1, gb1, ua1, ga1, b1), 8)
    return ua1


def rim_masks(count_x, count_z, where_ref):
    at_x, at_z = where_ref[0], where_ref[1]
    k = row_of((8, LANES))
    low = (at_z > 0).astype(jnp.float32)
    high = (at_z < count_z - 1).astype(jnp.float32)
    rows = jnp.where(k < 4, 1.0, jnp.where(k < 6, high, low))
    below = (at_x > 0).astype(jnp.float32)
    above = (at_x < count_x - 1).astype(jnp.float32)
    return rows, below, above


def in_segments(lo, hi, body, masks, scale, chunk):
    rows, below, above = masks
    inner = rows * scale
    for start, end, weight in (
        (lo, min(hi, RIM), inner * below),
        (max(lo, RIM), min(hi, RIM + BRICK_X), inner),
        (max(lo, RIM + BRICK_X), hi, inner * above),
    ):
        if end > start:
            each(start, end, functools.partial(body, weight=weight), chunk)


def fine_sweep(u_in, g_in, u_out, g_out, b_ref, margin, masks):
    def body(x, weight):
        FINE.put(u_out, g_out, x, FINE.sweep(u_in, g_in, b_ref, x, weight))

    in_segments(margin, WIDE_X - margin, body, masks, 1.0 / 30.0, 4)


def add_correction(coarse_ref, count_z, where_ref, masks, u_in, u_out, g_out, margin):
    at_x, at_z = where_ref[0], where_ref[1]
    rows_1 = coarse_ref.shape[3]
    turn = lax.rem(rows_1 - 4 * at_z, rows_1)
    k = row_of((8, LANES))
    rows = masks[0]

    def body(i):
        error = []
        for q in range(2):
            line = []
            for p in range(2):
                turned = pltpu.roll(coarse_ref[4 * at_x + i, q, p], turn, 0)
                tile = jnp.where(k < 6, turned[0:8], turned[rows_1 - 8 : rows_1])
                line.append(tile * rows)
            error.append(line)
        for d in range(2):
            x = 2 * i + d
            plane = [
                [u_in[x, q, p] + error[q // 2][p // 2] for p in range(4)] for q in range(4)
            ]
            FINE.put(u_out, g_out, x, plane)

    each(margin // 2, (WIDE_X - margin) // 2, body, 3)


def send_residual(u_ref, g_ref, b_ref, out_ref):
    def body(i):
        x = RIM + 2 * i
        pair = add_planes(
            FINE.residual(u_ref, g_ref, b_ref, x), FINE.residual(u_ref, g_ref, b_ref, x + 1)
        )
        for q, (even, odd) in enumerate(join(pair)):
            out_ref[i, q] = 0.1 * jnp.where(row_of(even.shape) < 4, even, pltpu.roll(odd, 4, 0))

    each(0, BRICK_X // 2, body, BRICK_X // 2)


def swap_blocks(tiles):
    shape = tiles[0].shape
    lane = lane_of(shape)
    half = lane < 64
    even = (lane // 32) % 2 == 0
    a, b, c, d = tiles
    a, c = jnp.where(half, a, pltpu.roll(c, 64, 1)), jnp.where(half, pltpu.roll(a, 64, 1), c)
    b, d = jnp.where(half, b, pltpu.roll(d, 64, 1)), jnp.where(half, pltpu.roll(b, 64, 1), d)
    a, b = jnp.where(even, a, pltpu.roll(b, 32, 1)), jnp.where(even, pltpu.roll(a, 96, 1), b)
    c, d = jnp.where(even, c, pltpu.roll(d, 32, 1)), jnp.where(even, pltpu.roll(c, 96, 1), d)
    return [a, b, c, d]


def pick_lanes(tile, index):
    return jnp.take_along_axis(tile, index, axis=1, mode="promise_in_bounds")


def lanes_kernel(where_ref, charges_ref, rows_ref, one_ref, two_ref):
    lane = lane_of((8, LANES))
    index = (lane % 32) * 4 + lane // 32
    odd = where_ref[1] % 2

    def body(x):
        for part in range(2):
            rows = slice(8 * part, 8 * part + 8)
            tiles = [
                pick_lanes(charges_ref[x, rows, t * LANES : (t + 1) * LANES], index)
                for t in range(4)
            ]
            for p, tile in enumerate(swap_blocks(tiles)):
                rows_ref[x, p, rows] = tile
        for p in range(4):
            first, last = rows_ref[x, p, 0:8], rows_ref[x, p, 8:16]
            one_ref[x, p] = jnp.where(odd == 0, last, first)
            two_ref[x, p] = jnp.where(odd == 0, first, last)

    each(0, BRICK_X, body, 2)


def down_kernel(count_x, count_z, where_ref, mid_ref, mid_rim_ref, one_ref, one_rim_ref, two_ref,
                two_rim_ref, u_ref, b_ref, out_ref, c_ref, g_ref, h_ref, rows_ref):
    masks = rim_masks(count_x, count_z, where_ref)
    odd = where_ref[0] % 2

    def split_rows(ref, rim_ref, part):
        def split(x):
            for p in range(4):
                rows_ref[x, p, 0:BRICK_Z] = ref[x, p]
                rows_ref[x, p, BRICK_Z:WIDE_Z] = rim_ref[x, p]
                for q in range(4):
                    c_ref[part * BRICK_X + x, q, p] = rows_ref[x, p, pl.ds(q, 8, stride=4), :]

        each(0, BRICK_X, split, 2)

    split_rows(mid_ref, mid_rim_ref, 1)
    split_rows(one_ref, one_rim_ref, 2 - 2 * odd)
    split_rows(two_ref, two_rim_ref, 2 * odd)

    def source(x, weight):
        here = FINE.load(c_ref, x)
        sums = along_z(here, 1, True)
        plane = []
        for q in range(4):
            y_sums = along_y(here[q], 1)
            line = []
            for p in range(4):
                face = (c_ref[x - 1, q, p] + c_ref[x + 1, q, p]) + (sums[q][p] + y_sums[p])
                line.append((here[q][p] * 6.0 + face) * weight)
            plane.append(line)
        FINE.put(b_ref, g_ref, x, plane)

    in_segments(1, WIDE_X - 1, source, masks, 0.2 / 12.0, 4)

    def body(x, weight):
        FINE.put(u_ref, h_ref, x, FINE.sweep(b_ref, g_ref, b_ref, x, weight))

    in_segments(2, WIDE_X - 2, body, masks, 1.0 / 30.0, 4)
    send_residual(u_ref, h_ref, b_ref, out_ref)


def middle_kernel(count_x, count_z, count_pieces, where_ref, *refs):
    pieces, refs = refs[:count_pieces], refs[count_pieces:]
    u_ref, b_ref, v_ref, out_ref, ga_ref, gb_ref, ua_ref, *grids = refs
    masks = rim_masks(count_x, count_z, where_ref)
    coarse = coarse_solve(count_x, count_z, where_ref, pieces, grids)
    add_correction(coarse, count_z, where_ref, masks, u_ref, ua_ref, ga_ref, 2)
    fine_sweep(ua_ref, ga_ref, v_ref, gb_ref, b_ref, 3, masks)
    fine_sweep(v_ref, gb_ref, ua_ref, ga_ref, b_ref, 4, masks)
    fine_sweep(ua_ref, ga_ref, v_ref, gb_ref, b_ref, 5, masks)
    fine_sweep(v_ref, gb_ref, ua_ref, ga_ref, b_ref, 6, masks)

    def keep(x):
        store_plane(v_ref, x, FINE.load(ua_ref, x))

    each(6, WIDE_X - 6, keep, 2)
    send_residual(ua_ref, ga_ref, b_ref, out_ref)


def up_kernel(count_x, count_z, count_pieces, where_ref, *refs):
    pieces, refs = refs[:count_pieces], refs[count_pieces:]
    u_ref, b_ref, out_ref, ga_ref, gb_ref, ua_ref, ub_ref, rows_ref, *grids = refs
    masks = rim_masks(count_x, count_z, where_ref)
    coarse = coarse_solve(count_x, count_z, where_ref, pieces, grids)
    add_correction(coarse, count_z, where_ref, masks, u_ref, ua_ref, ga_ref, 6)
    fine_sweep(ua_ref, ga_ref, ub_ref, gb_ref, b_ref, 7, masks)
    lane = lane_of((8, LANES))
    index = (lane % 4) * 32 + lane // 4

    def body(x):
        plane = FINE.sweep(ub_ref, gb_ref, b_ref, x, 1.0 / 30.0)
        for q in range(4):
            for t, tile in enumerate(swap_blocks(plane[q])):
                rows = pick_lanes(tile, index)[0:4]
                rows_ref[x - RIM, t, pl.ds(q, 4, stride=4), :] = rows
        for t in range(4):
            out_ref[x - RIM, :, t * LANES : (t + 1) * LANES] = rows_ref[x - RIM, t]

    each(RIM, RIM + BRICK_X, body, 4)


def call(kernel, outputs, scratch):
    shapes = [jax.ShapeDtypeStruct(shape, jnp.float32) for shape in outputs]
    held = sum(4 * math.prod(shape.shape) for shape in scratch)

    def run(where, *arrays):
        moved = sum(4 * math.prod(array.shape) for array in arrays + tuple(shapes))
        return pl.pallas_call(
            kernel,
            out_shape=shapes,
            in_specs=[pl.BlockSpec(memory_space=pltpu.SMEM)]
            + [pl.BlockSpec(memory_space=pltpu.VMEM)] * len(arrays),
            out_specs=[pl.BlockSpec(memory_space=pltpu.VMEM)] * len(shapes),
            scratch_shapes=scratch,
            compiler_params=pltpu.CompilerParams(vmem_limit_bytes=held + moved + SPARE_BYTES),
        )(where, *arrays)

    return run


def swap(axis, values, distance):
    count = lax.axis_size(axis)
    return lax.ppermute(values, axis, [(i, i ^ distance) for i in range(count)])


def swap_shifted(axis, values):
    pairs = [(i, i + 1) for i in range(1, lax.axis_size(axis) - 1, 2)]
    return lax.ppermute(values, axis, pairs + [(target, source) for source, target in pairs])


def every_piece(piece):
    held = piece[None]
    distance = 1
    while distance < lax.axis_size("gz"):
        held = jnp.concatenate([held, swap("gz", held, distance)])
        distance *= 2
    distance = 2
    while distance < lax.axis_size("gx"):
        held = jnp.concatenate([held, swap("gx", held, distance)])
        distance *= 2
    return held, swap("gx", held, 1)


def per_device(charges):
    count_x, count_z = lax.axis_size("gx"), lax.axis_size("gz")
    at_x, at_z = lax.axis_index("gx"), lax.axis_index("gz")
    where = jnp.stack([at_x, at_z]).astype(jnp.int32)
    brick, rim = (BRICK_X, 4, BRICK_Z, LANES), (BRICK_X, 4, RIM, LANES)
    middle, one, two = call(lanes_kernel, [brick, rim, rim], [])(where, charges)
    far = swap_shifted("gx", middle)
    near = swap("gx", middle, 1)
    one = swap("gz", one, 1)
    two = swap_shifted("gz", two)
    even = at_z % 2 == 0
    middle_rim = jnp.concatenate([jnp.where(even, one, two), jnp.where(even, two, one)], axis=2)
    far_rim = swap_shifted("gx", middle_rim)
    near_rim = swap("gx", middle_rim, 1)

    wide = (WIDE_X, 4, 4, 8, LANES)
    piece_shape = (BRICK_X // 2, 2, 8, LANES)
    fine = pltpu.VMEM(wide, jnp.float32)
    grids = coarse_grids(count_x, count_z)
    rows_in = pltpu.VMEM((BRICK_X, 4, WIDE_Z, LANES), jnp.float32)
    rows_out = pltpu.VMEM((BRICK_X, 4, BRICK_Z, LANES), jnp.float32)

    u, b, piece = call(
        functools.partial(down_kernel, count_x, count_z),
        [wide, wide, piece_shape],
        [fine] * 3 + [rows_in],
    )(where, middle, middle_rim, near, near_rim, far, far_rim)
    pieces = every_piece(piece)
    u, piece = call(
        functools.partial(middle_kernel, count_x, count_z, len(pieces)),
        [wide, piece_shape],
        [fine] * 3 + grids,
    )(where, *pieces, u, b)
    pieces = every_piece(piece)
    (potential,) = call(
        functools.partial(up_kernel, count_x, count_z, len(pieces)),
        [charges.shape],
        [fine] * 4 + [rows_out] + grids,
    )(where, *pieces, u, b)
    return potential


def solution(mesh):
    return jax.shard_map(
        per_device,
        mesh=mesh,
        in_specs=(P(("groups", "gx"), "gz", None),),
        out_specs=P(("groups", "gx"), "gz", None),
        check_vma=False,
    )
```

```python
import functools
import math

import jax
import jax.numpy as jnp
from jax import lax
from jax.experimental import pallas as pl
from jax.experimental.pallas import tpu as pltpu
from jax.sharding import PartitionSpec as P

COARSE_SWEEPS = 8
LANES = 128
RIM = 8
BRICK_X = 8
BRICK_Z = 16
WIDE_X = BRICK_X + 2 * RIM
WIDE_Z = BRICK_Z + 2 * RIM
SPARE_BYTES = 4 * 1024 * 1024


def lane_of(shape):
    return lax.broadcasted_iota(jnp.int32, shape, len(shape) - 1)


def row_of(shape):
    return lax.broadcasted_iota(jnp.int32, shape, len(shape) - 2)


def next_row(tile, step, cyclic):
    rows = tile.shape[0]
    moved = pltpu.roll(tile, rows - step, 0)
    return moved if cyclic else jnp.where(row_of(tile.shape) < rows - step, moved, 0.0)


def last_row(tile, step, cyclic):
    moved = pltpu.roll(tile, step, 0)
    return moved if cyclic else jnp.where(row_of(tile.shape) >= step, moved, 0.0)


def next_lane(tile, step):
    moved = pltpu.roll(tile, LANES - step, 1)
    return jnp.where(lane_of(tile.shape) < LANES - step, moved, 0.0)


def last_lane(tile, step):
    moved = pltpu.roll(tile, step, 1)
    return jnp.where(lane_of(tile.shape) >= step, moved, 0.0)


def load_plane(ref, x, count_q, count_p):
    return [[ref[x, q, p] for p in range(count_p)] for q in range(count_q)]


def store_plane(ref, x, plane):
    for q, line in enumerate(plane):
        for p, tile in enumerate(line):
            ref[x, q, p] = tile


def along_z(plane, step, cyclic):
    count_q, count_p = len(plane), len(plane[0])
    result = []
    for q in range(count_q):
        line = []
        for p in range(count_p):
            after = plane[q + 1][p] if q + 1 < count_q else next_row(plane[0][p], step, cyclic)
            before = plane[q - 1][p] if q > 0 else last_row(plane[-1][p], step, cyclic)
            line.append(after + before)
        result.append(line)
    return result


def along_y(line, step):
    count_p = len(line)
    result = []
    for p in range(count_p):
        after = line[p + 1] if p + 1 < count_p else next_lane(line[0], step)
        before = line[p - 1] if p > 0 else last_lane(line[-1], step)
        result.append(after + before)
    return result


class Level:
    def __init__(self, count_q, count_p, step, cyclic):
        self.count_q, self.count_p, self.step, self.cyclic = count_q, count_p, step, cyclic

    def load(self, ref, x):
        return load_plane(ref, x, self.count_q, self.count_p)

    def put(self, u_ref, g_ref, x, plane):
        store_plane(u_ref, x, plane)
        sums = along_z(plane, self.step, self.cyclic)
        store_plane(
            g_ref,
            x,
            [
                [s + (v + v) for s, v in zip(sum_line, line)]
                for sum_line, line in zip(sums, plane)
            ],
        )

    def spread(self, u_ref, g_ref, x, with_u):
        result = []
        for q in range(self.count_q):
            sides, both = [], []
            for p in range(self.count_p):
                here = g_ref[x, q, p]
                sides.append((u_ref[x - 1, q, p] + u_ref[x + 1, q, p]) + here)
                if with_u:
                    here = here + u_ref[x, q, p]
                both.append((g_ref[x - 1, q, p] + g_ref[x + 1, q, p]) + (here + here))
            result.append([a + b for a, b in zip(both, along_y(sides, self.step))])
        return result

    def sweep(self, u_ref, g_ref, b_ref, x, weight):
        wide = self.spread(u_ref, g_ref, x, True)
        return [
            [b_ref[x, q, p] + wide[q][p] * weight for p in range(self.count_p)]
            for q in range(self.count_q)
        ]

    def residual(self, u_ref, g_ref, b_ref, x):
        wide = self.spread(u_ref, g_ref, x, False)
        return [
            [
                b_ref[x, q, p] * 5.0 + (wide[q][p] - u_ref[x, q, p] * 28.0) * (1.0 / 6.0)
                for p in range(self.count_p)
            ]
            for q in range(self.count_q)
        ]


def add_planes(one, other):
    return [[a + b for a, b in zip(l, m)] for l, m in zip(one, other)]


def join(plane):
    lines = [[a + b for a, b in zip(plane[q], plane[q + 1])] for q in range(0, len(plane), 2)]
    return [[line[p] + line[p + 1] for p in range(0, len(line), 2)] for line in lines]


def join_within(tile):
    rows = tile.shape[0]
    even = row_of(tile.shape) % 2 == 0
    tile = tile + jnp.where(even, pltpu.roll(tile, rows - 1, 0), pltpu.roll(tile, 1, 0))
    even = lane_of(tile.shape) % 2 == 0
    return tile + jnp.where(even, pltpu.roll(tile, LANES - 1, 1), pltpu.roll(tile, 1, 1))


def scaled(plane, factor):
    return [[tile * factor for tile in line] for line in plane]


def each(lo, hi, body, chunk):
    count = hi - lo
    whole = count // chunk
    if whole == 1:
        for x in range(lo, lo + chunk):
            body(x)
    elif whole > 1:

        def step(i, carry):
            for d in range(chunk):
                body(lo + i * chunk + d)
            return carry

        lax.fori_loop(0, whole, step, 0)
    for x in range(lo + whole * chunk, hi):
        body(x)


FINE = Level(4, 4, 1, True)
LEVEL_1 = Level(2, 2, 1, False)
NEAR_1 = Level(2, 2, 1, True)
LEVEL_2 = Level(1, 1, 1, False)
LEVEL_3 = Level(1, 1, 2, False)
PAD = RIM // 2
PAD_2 = RIM // 4


def zero_planes(ref, indices):
    for x in indices:
        ref[x] = jnp.zeros(ref.shape[1:], ref.dtype)


def coarse_grids(count_x, count_z):
    rows = count_z * BRICK_Z // 4
    shapes = []
    for planes, count in ((4 * count_x + 2 * PAD, 2), (2 * count_x + 2 * PAD_2, 1), (count_x + 2, 1)):
        shapes += [pltpu.VMEM((planes, count, count, rows, LANES), jnp.float32)] * 5
    return shapes


def coarse_solve(count_x, count_z, where_ref, pieces, grids):
    (ua1, ub1, ga1, gb1, b1), (ua2, ub2, ga2, gb2, b2), (ua3, ub3, ga3, gb3, b3) = (
        grids[0:5],
        grids[5:10],
        grids[10:15],
    )
    size_1, size_2, size_3 = 4 * count_x, 2 * count_x, count_x
    for refs, pad, size in (
        ((ua1, ub1, ga1, gb1, b1), PAD, size_1),
        ((ua2, ub2, ga2, gb2), PAD_2, size_2),
        ((ua3, ub3, ga3, gb3), 1, size_3),
    ):
        for ref in refs:
            zero_planes(ref, list(range(pad)) + list(range(pad + size, pad + size + pad)))
    third = 1.0 / 30.0

    at_x, at_z = where_ref[0], where_ref[1]

    def place(x, load):
        for i in range(4):
            for q in range(2):
                for z in range(0, count_z, 2):
                    one, two = load(z, i, q), load(z + 1, i, q)
                    first = row_of(one.shape) < 4
                    rows = slice(4 * z, 4 * z + 8)
                    b1[x + i, q, 0, rows] = jnp.where(first, one, pltpu.roll(two, 4, 0))
                    b1[x + i, q, 1, rows] = jnp.where(first, pltpu.roll(one, 4, 0), two)
            LEVEL_1.put(ub1, gb1, x + i, LEVEL_1.load(b1, x + i))

    if len(pieces) == 1:

        def gather(n):
            place(PAD + 4 * n, lambda z, i, q: pieces[0][n * count_z + z, i, q])

        each(0, count_x, gather, 1)
    else:

        def gather(n):
            for core in range(2):
                x = PAD + 4 * ((2 * n + core) ^ at_x)
                place(x, lambda z, i, q: pieces[core][n * count_z + (z ^ at_z), i, q])

        each(0, count_x // 2, gather, 1)

    def sweep(level, u_in, g_in, u_out, g_out, b):
        return lambda x: level.put(u_out, g_out, x, level.sweep(u_in, g_in, b, x, third))

    each(PAD, PAD + size_1, sweep(LEVEL_1, ub1, gb1, ua1, ga1, b1), 8)

    def restrict_1(x):
        fine = PAD + 2 * x
        pair = add_planes(
            LEVEL_1.residual(ua1, ga1, b1, fine), LEVEL_1.residual(ua1, ga1, b1, fine + 1)
        )
        plane = scaled(join(pair), 0.5 * 0.2)
        store_plane(b2, PAD_2 + x, plane)
        LEVEL_2.put(ub2, gb2, PAD_2 + x, plane)

    each(0, size_2, restrict_1, 8)
    all_2 = (PAD_2, PAD_2 + size_2)
    each(*all_2, sweep(LEVEL_2, ub2, gb2, ua2, ga2, b2), 8)

    def restrict_2(x):
        fine = PAD_2 + 2 * x
        pair = add_planes(
            LEVEL_2.residual(ua2, ga2, b2, fine), LEVEL_2.residual(ua2, ga2, b2, fine + 1)
        )
        plane = [[join_within(pair[0][0]) * (0.5 * 0.2)]]
        store_plane(b3, 1 + x, plane)
        LEVEL_3.put(ub3, gb3, 1 + x, plane)

    each(0, size_3, restrict_2, 4)
    now, later = (ub3, gb3), (ua3, ga3)
    for _ in range(COARSE_SWEEPS - 1):
        each(1, 1 + size_3, sweep(LEVEL_3, *now, *later, b3), 4)
        now, later = later, now

    def prolong_3(x):
        for d in range(2):
            fine = PAD_2 + 2 * x + d
            LEVEL_2.put(ua2, ga2, fine, [[ua2[fine, 0, 0] + now[0][1 + x, 0, 0]]])

    each(0, size_3, prolong_3, 4)
    each(*all_2, sweep(LEVEL_2, ua2, ga2, ub2, gb2, b2), 8)
    each(*all_2, sweep(LEVEL_2, ub2, gb2, ua2, ga2, b2), 8)
    return ua1, ua2, b1


def coarse_finish(count_x, grids):
    ua1, ub1, ga1, gb1, b1 = grids[0:5]
    ua2 = grids[5]
    size_1, size_2 = 4 * count_x, 2 * count_x

    def prolong_2(x):
        error = ua2[PAD_2 + x, 0, 0]
        for d in range(2):
            fine = PAD + 2 * x + d
            LEVEL_1.put(
                ua1, ga1, fine, [[t + error for t in line] for line in LEVEL_1.load(ua1, fine)]
            )

    def sweep(u_in, g_in, u_out, g_out):
        return lambda x: LEVEL_1.put(
            u_out, g_out, x, LEVEL_1.sweep(u_in, g_in, b1, x, 1.0 / 30.0)
        )

    each(0, size_2, prolong_2, 8)
    each(PAD, PAD + size_1, sweep(ua1, ga1, ub1, gb1), 8)
    each(PAD, PAD + size_1, sweep(ub1, gb1, ua1, ga1), 8)
    return ua1


def turned_tile(tile, at_z, rows):
    count = tile.shape[0]
    turned = pltpu.roll(tile, lax.rem(count - 4 * at_z, count), 0)
    return jnp.where(row_of((8, LANES)) < 6, turned[0:8], turned[count - 8 : count]) * rows


def near_finish(coarse, where_ref, masks, near):
    ua1, ua2, b1 = coarse
    ua, ga, ub, gb, b = near
    at_x, at_z = where_ref[0], where_ref[1]
    rows = masks[0]

    def take(i):
        error = ua2[2 * at_x + i // 2, 0, 0]
        plane = [[t + error for t in line] for line in LEVEL_1.load(ua1, 4 * at_x + i)]
        plane = [[turned_tile(t, at_z, rows) for t in line] for line in plane]
        NEAR_1.put(ua, ga, i, plane)
        plane = LEVEL_1.load(b1, 4 * at_x + i)
        store_plane(b, i, [[turned_tile(t, at_z, rows) for t in line] for line in plane])

    each(1, 11, take, 5)

    def sweep(u_in, g_in, u_out, g_out):
        def body(i, weight):
            NEAR_1.put(u_out, g_out, i, NEAR_1.sweep(u_in, g_in, b, i, weight))

        return body

    in_segments(2, 10, sweep(ua, ga, ub, gb), masks, 1.0 / 30.0, 4, PAD, BRICK_X // 2)
    in_segments(3, 9, sweep(ub, gb, ua, ga), masks, 1.0 / 30.0, 4, PAD, BRICK_X // 2)
    return ua


def rim_masks(count_x, count_z, where_ref):
    at_x, at_z = where_ref[0], where_ref[1]
    k = row_of((8, LANES))
    low = (at_z > 0).astype(jnp.float32)
    high = (at_z < count_z - 1).astype(jnp.float32)
    rows = jnp.where(k < 4, 1.0, jnp.where(k < 6, high, low))
    below = (at_x > 0).astype(jnp.float32)
    above = (at_x < count_x - 1).astype(jnp.float32)
    return rows, below, above


def in_segments(lo, hi, body, masks, scale, chunk, rim=RIM, brick=BRICK_X):
    rows, below, above = masks
    inner = rows * scale
    for start, end, weight in (
        (lo, min(hi, rim), inner * below),
        (max(lo, rim), min(hi, rim + brick), inner),
        (max(lo, rim + brick), hi, inner * above),
    ):
        if end > start:
            each(start, end, functools.partial(body, weight=weight), chunk)


def fine_sweep(u_in, g_in, u_out, g_out, b_ref, margin, masks):
    def body(x, weight):
        FINE.put(u_out, g_out, x, FINE.sweep(u_in, g_in, b_ref, x, weight))

    in_segments(margin, WIDE_X - margin, body, masks, 1.0 / 30.0, 4)


def add_correction(error_of, u_in, u_out, g_out, margin):
    def body(i):
        error = error_of(i)
        for d in range(2):
            x = 2 * i + d
            plane = [
                [u_in[x, q, p] + error[q // 2][p // 2] for p in range(4)] for q in range(4)
            ]
            FINE.put(u_out, g_out, x, plane)

    each(margin // 2, (WIDE_X - margin) // 2, body, 2)


def send_residual(u_ref, g_ref, b_ref, out_ref):
    def body(i):
        x = RIM + 2 * i
        pair = add_planes(
            FINE.residual(u_ref, g_ref, b_ref, x), FINE.residual(u_ref, g_ref, b_ref, x + 1)
        )
        for q, (even, odd) in enumerate(join(pair)):
            out_ref[i, q] = 0.1 * jnp.where(row_of(even.shape) < 4, even, pltpu.roll(odd, 4, 0))

    each(0, BRICK_X // 2, body, BRICK_X // 2)


def permuted(values, places):
    shape = (values.shape[1], values.shape[1])
    row, column = (lax.broadcasted_iota(jnp.int32, shape, d) for d in range(2))
    matrix = places(row, column).astype(jnp.float32).astype(jnp.bfloat16)
    total, rest = None, values
    terms = []
    for _ in range(3):
        term = rest.astype(jnp.bfloat16)
        rest = rest - term.astype(jnp.float32)
        terms.append(jnp.dot(term, matrix, preferred_element_type=jnp.float32))
    return terms[0] + (terms[1] + terms[2])


def lanes_kernel(where_ref, charges_ref, rows_ref, one_ref, two_ref):
    odd = where_ref[1] % 2
    width = charges_ref.shape[2]
    flat = charges_ref[...].reshape(BRICK_X * BRICK_Z, width)
    split = permuted(flat, lambda y, l: y == (l % LANES) * 4 + l // LANES)
    for p in range(4):
        tile = split[:, p * LANES : (p + 1) * LANES].reshape(BRICK_X, BRICK_Z, LANES)
        rows_ref[:, p] = tile
        first, last = tile[:, 0:8], tile[:, 8:16]
        one_ref[:, p] = jnp.where(odd == 0, last, first)
        two_ref[:, p] = jnp.where(odd == 0, first, last)


def down_kernel(count_x, count_z, where_ref, mid_ref, mid_rim_ref, one_ref, one_rim_ref, two_ref,
                two_rim_ref, u_ref, b_ref, out_ref, c_ref, g_ref, h_ref, rows_ref):
    masks = rim_masks(count_x, count_z, where_ref)
    odd = where_ref[0] % 2

    def split_rows(ref, rim_ref, part):
        def split(x):
            for p in range(4):
                rows_ref[x, p, 0:BRICK_Z] = ref[x, p]
                rows_ref[x, p, BRICK_Z:WIDE_Z] = rim_ref[x, p]
                for q in range(4):
                    c_ref[part * BRICK_X + x, q, p] = rows_ref[x, p, pl.ds(q, 8, stride=4), :]

        each(0, BRICK_X, split, 2)

    split_rows(mid_ref, mid_rim_ref, 1)
    split_rows(one_ref, one_rim_ref, 2 - 2 * odd)
    split_rows(two_ref, two_rim_ref, 2 * odd)

    def source(x, weight):
        here = FINE.load(c_ref, x)
        sums = along_z(here, 1, True)
        plane = []
        for q in range(4):
            y_sums = along_y(here[q], 1)
            line = []
            for p in range(4):
                face = (c_ref[x - 1, q, p] + c_ref[x + 1, q, p]) + (sums[q][p] + y_sums[p])
                line.append((here[q][p] * 6.0 + face) * weight)
            plane.append(line)
        FINE.put(b_ref, g_ref, x, plane)

    in_segments(1, WIDE_X - 1, source, masks, 0.2 / 12.0, 4)

    def body(x, weight):
        FINE.put(u_ref, h_ref, x, FINE.sweep(b_ref, g_ref, b_ref, x, weight))

    in_segments(2, WIDE_X - 2, body, masks, 1.0 / 30.0, 4)
    send_residual(u_ref, h_ref, b_ref, out_ref)


def middle_kernel(count_x, count_z, count_pieces, where_ref, *refs):
    pieces, refs = refs[:count_pieces], refs[count_pieces:]
    u_ref, b_ref, v_ref, out_ref, ga_ref, gb_ref, ua_ref, *grids = refs
    masks = rim_masks(count_x, count_z, where_ref)
    coarse_solve(count_x, count_z, where_ref, pieces, grids)
    coarse_ref = coarse_finish(count_x, grids)
    at_x, at_z = where_ref[0], where_ref[1]

    def error_of(i):
        plane = LEVEL_1.load(coarse_ref, 4 * at_x + i)
        return [[turned_tile(t, at_z, masks[0]) for t in line] for line in plane]

    add_correction(error_of, u_ref, v_ref, ga_ref, 2)
    fine_sweep(v_ref, ga_ref, ua_ref, gb_ref, b_ref, 3, masks)
    fine_sweep(ua_ref, gb_ref, v_ref, ga_ref, b_ref, 4, masks)
    fine_sweep(v_ref, ga_ref, ua_ref, gb_ref, b_ref, 5, masks)
    fine_sweep(ua_ref, gb_ref, v_ref, ga_ref, b_ref, 6, masks)
    send_residual(v_ref, ga_ref, b_ref, out_ref)


def up_kernel(count_x, count_z, count_pieces, where_ref, *refs):
    pieces, refs = refs[:count_pieces], refs[count_pieces:]
    u_ref, b_ref, out_ref, ga_ref, gb_ref, ua_ref, ub_ref, rows_ref, *refs = refs
    near, grids = refs[:5], refs[5:]
    masks = rim_masks(count_x, count_z, where_ref)
    coarse = coarse_solve(count_x, count_z, where_ref, pieces, grids)
    error_ref = near_finish(coarse, where_ref, masks, near)
    add_correction(lambda i: NEAR_1.load(error_ref, i), u_ref, ua_ref, ga_ref, 6)
    fine_sweep(ua_ref, ga_ref, ub_ref, gb_ref, b_ref, 7, masks)

    def body(x):
        plane = FINE.sweep(ub_ref, gb_ref, b_ref, x, 1.0 / 30.0)
        for q in range(4):
            for p in range(4):
                rows_ref[x - RIM, p, pl.ds(q, 4, stride=4), :] = plane[q][p][0:4]

    each(RIM, RIM + BRICK_X, body, 2)
    tiles = [rows_ref[:, p].reshape(BRICK_X * BRICK_Z, LANES) for p in range(4)]
    whole = permuted(
        jnp.concatenate(tiles, axis=1), lambda l, y: y == (l % LANES) * 4 + l // LANES
    )
    out_ref[...] = whole.reshape(out_ref.shape)


def call(kernel, outputs, scratch):
    shapes = [jax.ShapeDtypeStruct(shape, jnp.float32) for shape in outputs]
    held = sum(4 * math.prod(shape.shape) for shape in scratch)

    def run(where, *arrays):
        moved = sum(4 * math.prod(array.shape) for array in arrays + tuple(shapes))
        return pl.pallas_call(
            kernel,
            out_shape=shapes,
            in_specs=[pl.BlockSpec(memory_space=pltpu.SMEM)]
            + [pl.BlockSpec(memory_space=pltpu.VMEM)] * len(arrays),
            out_specs=[pl.BlockSpec(memory_space=pltpu.VMEM)] * len(shapes),
            scratch_shapes=scratch,
            compiler_params=pltpu.CompilerParams(vmem_limit_bytes=held + moved + SPARE_BYTES),
        )(where, *arrays)

    return run


def swap(axis, values, distance):
    count = lax.axis_size(axis)
    return lax.ppermute(values, axis, [(i, i ^ distance) for i in range(count)])


def swap_shifted(axis, values):
    pairs = [(i, i + 1) for i in range(1, lax.axis_size(axis) - 1, 2)]
    return lax.ppermute(values, axis, pairs + [(target, source) for source, target in pairs])


def every_piece(piece):
    held = piece[None]
    held = jnp.concatenate(
        [held] + [swap("gz", held, distance) for distance in range(1, lax.axis_size("gz"))]
    )
    distance = 2
    while distance < lax.axis_size("gx"):
        held = jnp.concatenate([held, swap("gx", held, distance)])
        distance *= 2
    return held, swap("gx", held, 1)


def per_device(charges):
    count_x, count_z = lax.axis_size("gx"), lax.axis_size("gz")
    at_x, at_z = lax.axis_index("gx"), lax.axis_index("gz")
    where = jnp.stack([at_x, at_z]).astype(jnp.int32)
    brick, rim = (BRICK_X, 4, BRICK_Z, LANES), (BRICK_X, 4, RIM, LANES)
    middle, one, two = call(lanes_kernel, [brick, rim, rim], [])(where, charges)
    far = swap_shifted("gx", middle)
    near = swap("gx", middle, 1)
    one = swap("gz", one, 1)
    two = swap_shifted("gz", two)
    even = at_z % 2 == 0
    middle_rim = jnp.concatenate([jnp.where(even, one, two), jnp.where(even, two, one)], axis=2)
    far_rim = swap_shifted("gx", middle_rim)
    near_rim = swap("gx", middle_rim, 1)

    wide = (WIDE_X, 4, 4, 8, LANES)
    piece_shape = (BRICK_X // 2, 2, 8, LANES)
    fine = pltpu.VMEM(wide, jnp.float32)
    grids = coarse_grids(count_x, count_z)
    rows_in = pltpu.VMEM((BRICK_X, 4, WIDE_Z, LANES), jnp.float32)
    close = pltpu.VMEM((WIDE_X // 2, 2, 2, 8, LANES), jnp.float32)
    rows_out = pltpu.VMEM((BRICK_X, 4, BRICK_Z, LANES), jnp.float32)

    u, b, piece = call(
        functools.partial(down_kernel, count_x, count_z),
        [wide, wide, piece_shape],
        [fine] * 3 + [rows_in],
    )(where, middle, middle_rim, near, near_rim, far, far_rim)
    pieces = every_piece(piece)
    u, piece = call(
        functools.partial(middle_kernel, count_x, count_z, len(pieces)),
        [wide, piece_shape],
        [fine] * 3 + grids,
    )(where, *pieces, u, b)
    pieces = every_piece(piece)
    (potential,) = call(
        functools.partial(up_kernel, count_x, count_z, len(pieces)),
        [charges.shape],
        [fine] * 4 + [rows_out] + [close] * 5 + grids,
    )(where, *pieces, u, b)
    return potential


def solution(mesh):
    return jax.shard_map(
        per_device,
        mesh=mesh,
        in_specs=(P(("groups", "gx"), "gz", None),),
        out_specs=P(("groups", "gx"), "gz", None),
        check_vma=False,
    )
```

```python
import functools
import math

import jax
import jax.numpy as jnp
from jax import lax
from jax.experimental import pallas as pl
from jax.experimental.pallas import tpu as pltpu
from jax.sharding import PartitionSpec as P

COARSE_SWEEPS = 8
LANES = 128
RIM = 8
BRICK_X = 8
BRICK_Z = 16
WIDE_X = BRICK_X + 2 * RIM
WIDE_Z = BRICK_Z + 2 * RIM
SPARE_BYTES = 4 * 1024 * 1024


def lane_of(shape):
    return lax.broadcasted_iota(jnp.int32, shape, len(shape) - 1)


def row_of(shape):
    return lax.broadcasted_iota(jnp.int32, shape, len(shape) - 2)


def next_row(tile, step, cyclic):
    rows = tile.shape[0]
    moved = pltpu.roll(tile, rows - step, 0)
    return moved if cyclic else jnp.where(row_of(tile.shape) < rows - step, moved, 0.0)


def last_row(tile, step, cyclic):
    moved = pltpu.roll(tile, step, 0)
    return moved if cyclic else jnp.where(row_of(tile.shape) >= step, moved, 0.0)


def next_lane(tile, step):
    moved = pltpu.roll(tile, LANES - step, 1)
    return jnp.where(lane_of(tile.shape) < LANES - step, moved, 0.0)


def last_lane(tile, step):
    moved = pltpu.roll(tile, step, 1)
    return jnp.where(lane_of(tile.shape) >= step, moved, 0.0)


def load_plane(ref, x, count_q, count_p):
    return [[ref[x, q, p] for p in range(count_p)] for q in range(count_q)]


def store_plane(ref, x, plane):
    for q, line in enumerate(plane):
        for p, tile in enumerate(line):
            ref[x, q, p] = tile


def along_z(plane, step, cyclic):
    count_q, count_p = len(plane), len(plane[0])
    result = []
    for q in range(count_q):
        line = []
        for p in range(count_p):
            after = plane[q + 1][p] if q + 1 < count_q else next_row(plane[0][p], step, cyclic)
            before = plane[q - 1][p] if q > 0 else last_row(plane[-1][p], step, cyclic)
            line.append(after + before)
        result.append(line)
    return result


def along_y(line, step):
    count_p = len(line)
    result = []
    for p in range(count_p):
        after = line[p + 1] if p + 1 < count_p else next_lane(line[0], step)
        before = line[p - 1] if p > 0 else last_lane(line[-1], step)
        result.append(after + before)
    return result


class Level:
    def __init__(self, count_q, count_p, step, cyclic):
        self.count_q, self.count_p, self.step, self.cyclic = count_q, count_p, step, cyclic

    def load(self, ref, x):
        return load_plane(ref, x, self.count_q, self.count_p)

    def put(self, u_ref, g_ref, x, plane):
        store_plane(u_ref, x, plane)
        sums = along_z(plane, self.step, self.cyclic)
        store_plane(
            g_ref,
            x,
            [
                [s + (v + v) for s, v in zip(sum_line, line)]
                for sum_line, line in zip(sums, plane)
            ],
        )

    def spread(self, u_ref, g_ref, x, with_u):
        result = []
        for q in range(self.count_q):
            sides, both = [], []
            for p in range(self.count_p):
                here = g_ref[x, q, p]
                sides.append((u_ref[x - 1, q, p] + u_ref[x + 1, q, p]) + here)
                if with_u:
                    here = here + u_ref[x, q, p]
                both.append((g_ref[x - 1, q, p] + g_ref[x + 1, q, p]) + (here + here))
            result.append([a + b for a, b in zip(both, along_y(sides, self.step))])
        return result

    def sweep(self, u_ref, g_ref, b_ref, x, weight):
        wide = self.spread(u_ref, g_ref, x, True)
        return [
            [b_ref[x, q, p] + wide[q][p] * weight for p in range(self.count_p)]
            for q in range(self.count_q)
        ]

    def residual(self, u_ref, g_ref, b_ref, x):
        wide = self.spread(u_ref, g_ref, x, False)
        return [
            [
                b_ref[x, q, p] * 5.0 + (wide[q][p] - u_ref[x, q, p] * 28.0) * (1.0 / 6.0)
                for p in range(self.count_p)
            ]
            for q in range(self.count_q)
        ]


def add_planes(one, other):
    return [[a + b for a, b in zip(l, m)] for l, m in zip(one, other)]


def join(plane):
    lines = [[a + b for a, b in zip(plane[q], plane[q + 1])] for q in range(0, len(plane), 2)]
    return [[line[p] + line[p + 1] for p in range(0, len(line), 2)] for line in lines]


def join_within(tile):
    rows = tile.shape[0]
    even = row_of(tile.shape) % 2 == 0
    tile = tile + jnp.where(even, pltpu.roll(tile, rows - 1, 0), pltpu.roll(tile, 1, 0))
    even = lane_of(tile.shape) % 2 == 0
    return tile + jnp.where(even, pltpu.roll(tile, LANES - 1, 1), pltpu.roll(tile, 1, 1))


def scaled(plane, factor):
    return [[tile * factor for tile in line] for line in plane]


def each(lo, hi, body, chunk):
    count = hi - lo
    whole = count // chunk
    if whole == 1:
        for x in range(lo, lo + chunk):
            body(x)
    elif whole > 1:

        def step(i, carry):
            for d in range(chunk):
                body(lo + i * chunk + d)
            return carry

        lax.fori_loop(0, whole, step, 0)
    for x in range(lo + whole * chunk, hi):
        body(x)


FINE = Level(4, 4, 1, True)
LEVEL_1 = Level(2, 2, 1, False)
NEAR_1 = Level(2, 2, 1, True)
LEVEL_2 = Level(1, 1, 1, False)
LEVEL_3 = Level(1, 1, 2, False)
PAD = RIM // 2
PAD_2 = RIM // 4


def zero_planes(ref, indices):
    for x in indices:
        ref[x] = jnp.zeros(ref.shape[1:], ref.dtype)


def coarse_grids(count_x, count_z):
    rows = count_z * BRICK_Z // 4
    shapes = []
    for planes, count in ((4 * count_x + 2 * PAD, 2), (2 * count_x + 2 * PAD_2, 1), (count_x + 2, 1)):
        shapes += [pltpu.VMEM((planes, count, count, rows, LANES), jnp.float32)] * 5
    return shapes


def coarse_solve(count_x, count_z, where_ref, pieces, grids):
    (ua1, ub1, ga1, gb1, b1), (ua2, ub2, ga2, gb2, b2), (ua3, ub3, ga3, gb3, b3) = (
        grids[0:5],
        grids[5:10],
        grids[10:15],
    )
    size_1, size_2, size_3 = 4 * count_x, 2 * count_x, count_x
    for refs, pad, size in (
        ((ua1, ub1, ga1, gb1, b1), PAD, size_1),
        ((ua2, ub2, ga2, gb2), PAD_2, size_2),
        ((ua3, ub3, ga3, gb3), 1, size_3),
    ):
        for ref in refs:
            zero_planes(ref, list(range(pad)) + list(range(pad + size, pad + size + pad)))
    third = 1.0 / 30.0

    at_x, at_z = where_ref[0], where_ref[1]

    def place(x, load):
        for i in range(4):
            for q in range(2):
                for z in range(0, count_z, 2):
                    one, two = load(z, i, q), load(z + 1, i, q)
                    first = row_of(one.shape) < 4
                    rows = slice(4 * z, 4 * z + 8)
                    b1[x + i, q, 0, rows] = jnp.where(first, one, pltpu.roll(two, 4, 0))
                    b1[x + i, q, 1, rows] = jnp.where(first, pltpu.roll(one, 4, 0), two)
            LEVEL_1.put(ub1, gb1, x + i, LEVEL_1.load(b1, x + i))

    if len(pieces) == 1:

        def gather(n):
            place(PAD + 4 * n, lambda z, i, q: pieces[0][n * count_z + z, i, q])

        each(0, count_x, gather, 1)
    else:

        def gather(n):
            for core in range(2):
                x = PAD + 4 * ((2 * n + core) ^ at_x)
                place(x, lambda z, i, q: pieces[core][n * count_z + (z ^ at_z ^ (count_z - 1)), i, q])

        each(0, count_x // 2, gather, 1)

    def sweep(level, u_in, g_in, u_out, g_out, b):
        return lambda x: level.put(u_out, g_out, x, level.sweep(u_in, g_in, b, x, third))

    each(PAD, PAD + size_1, sweep(LEVEL_1, ub1, gb1, ua1, ga1, b1), 2)

    def restrict_1(x):
        fine = PAD + 2 * x
        pair = add_planes(
            LEVEL_1.residual(ua1, ga1, b1, fine), LEVEL_1.residual(ua1, ga1, b1, fine + 1)
        )
        plane = scaled(join(pair), 0.5 * 0.2)
        store_plane(b2, PAD_2 + x, plane)
        LEVEL_2.put(ub2, gb2, PAD_2 + x, plane)

    each(0, size_2, restrict_1, 1)
    all_2 = (PAD_2, PAD_2 + size_2)
    each(*all_2, sweep(LEVEL_2, ub2, gb2, ua2, ga2, b2), 8)

    def restrict_2(x):
        fine = PAD_2 + 2 * x
        pair = add_planes(
            LEVEL_2.residual(ua2, ga2, b2, fine), LEVEL_2.residual(ua2, ga2, b2, fine + 1)
        )
        plane = [[join_within(pair[0][0]) * (0.5 * 0.2)]]
        store_plane(b3, 1 + x, plane)
        LEVEL_3.put(ub3, gb3, 1 + x, plane)

    each(0, size_3, restrict_2, 4)
    first, second = (ub3, gb3), (ua3, ga3)

    def two_sweeps(n, carry):
        each(1, 1 + size_3, sweep(LEVEL_3, *first, *second, b3), 4)
        each(1, 1 + size_3, sweep(LEVEL_3, *second, *first, b3), 4)
        return carry

    pairs, rest = divmod(COARSE_SWEEPS - 1, 2)
    lax.fori_loop(0, pairs, two_sweeps, 0)
    if rest:
        each(1, 1 + size_3, sweep(LEVEL_3, *first, *second, b3), 4)
    now = second if rest else first

    def prolong_3(x):
        for d in range(2):
            fine = PAD_2 + 2 * x + d
            LEVEL_2.put(ua2, ga2, fine, [[ua2[fine, 0, 0] + now[0][1 + x, 0, 0]]])

    each(0, size_3, prolong_3, 4)
    each(*all_2, sweep(LEVEL_2, ua2, ga2, ub2, gb2, b2), 8)
    each(*all_2, sweep(LEVEL_2, ub2, gb2, ua2, ga2, b2), 8)
    return ua1, ua2, b1


def coarse_finish(count_x, grids):
    ua1, ub1, ga1, gb1, b1 = grids[0:5]
    ua2 = grids[5]
    size_1, size_2 = 4 * count_x, 2 * count_x

    def prolong_2(x):
        error = ua2[PAD_2 + x, 0, 0]
        for d in range(2):
            fine = PAD + 2 * x + d
            LEVEL_1.put(
                ua1, ga1, fine, [[t + error for t in line] for line in LEVEL_1.load(ua1, fine)]
            )

    def sweep(u_in, g_in, u_out, g_out):
        return lambda x: LEVEL_1.put(
            u_out, g_out, x, LEVEL_1.sweep(u_in, g_in, b1, x, 1.0 / 30.0)
        )

    each(0, size_2, prolong_2, 1)
    each(PAD, PAD + size_1, sweep(ua1, ga1, ub1, gb1), 2)
    each(PAD, PAD + size_1, sweep(ub1, gb1, ua1, ga1), 2)
    return ua1


def turned_tile(tile, at_z, rows):
    count = tile.shape[0]
    turned = pltpu.roll(tile, lax.rem(count - 4 * at_z, count), 0)
    return jnp.where(row_of((8, LANES)) < 6, turned[0:8], turned[count - 8 : count]) * rows


def near_finish(coarse, where_ref, masks_ref, near):
    ua1, ua2, b1 = coarse
    ua, ga, ub, gb, b = near
    at_x, at_z = where_ref[0], where_ref[1]
    rows = masks_ref[1]

    def take(i):
        error = ua2[2 * at_x + i // 2, 0, 0]
        plane = [[t + error for t in line] for line in LEVEL_1.load(ua1, 4 * at_x + i)]
        plane = [[turned_tile(t, at_z, rows) for t in line] for line in plane]
        NEAR_1.put(ua, ga, i, plane)
        plane = LEVEL_1.load(b1, 4 * at_x + i)
        store_plane(b, i, [[turned_tile(t, at_z, rows) for t in line] for line in plane])

    each(1, 11, take, 2)

    def sweep(u_in, g_in, u_out, g_out):
        def body(i, weight):
            NEAR_1.put(u_out, g_out, i, NEAR_1.sweep(u_in, g_in, b, i, weight))

        return body

    each(2, 10, masked(sweep(ua, ga, ub, gb), masks_ref, 1.0 / 30.0, PAD), 2)
    each(3, 9, masked(sweep(ub, gb, ua, ga), masks_ref, 1.0 / 30.0, PAD), 2)
    return ua


def rim_masks(count_x, count_z, where_ref, masks_ref):
    at_x, at_z = where_ref[0], where_ref[1]
    k = row_of((8, LANES))
    low = (at_z > 0).astype(jnp.float32)
    high = (at_z < count_z - 1).astype(jnp.float32)
    rows = jnp.where(k < 4, 1.0, jnp.where(k < 6, high, low))
    masks_ref[0] = rows * (at_x > 0).astype(jnp.float32)
    masks_ref[1] = rows
    masks_ref[2] = rows * (at_x < count_x - 1).astype(jnp.float32)


def masked(body, masks_ref, scale, brick):
    return lambda x: body(x, masks_ref[lax.div(jnp.int32(x), jnp.int32(brick))] * scale)


def fine_sweeps(u_refs, g_refs, b_ref, first, count, masks_ref):
    def sweep(n, carry):
        now, later = n % 2, (n + 1) % 2
        u_in, g_in, u_out, g_out = u_refs.at[now], g_refs.at[now], u_refs.at[later], g_refs.at[later]

        def body(x, weight):
            FINE.put(u_out, g_out, x, FINE.sweep(u_in, g_in, b_ref, x, weight))

        body = masked(body, masks_ref, 1.0 / 30.0, BRICK_X)
        margin = first + n

        def step(i, carry):
            for d in range(2):
                body(margin + 2 * i + d)
            return carry

        lax.fori_loop(0, WIDE_X // 2 - margin, step, 0)
        return carry

    lax.fori_loop(0, count, sweep, 0)


def add_correction(error_of, u_in, u_out, g_out, margin):
    def body(i):
        error = error_of(i)
        for d in range(2):
            x = 2 * i + d
            plane = [
                [u_in[x, q, p] + error[q // 2][p // 2] for p in range(4)] for q in range(4)
            ]
            FINE.put(u_out, g_out, x, plane)

    each(margin // 2, (WIDE_X - margin) // 2, body, 1)


def send_residual(u_ref, g_ref, b_ref, out_ref):
    def body(i):
        x = RIM + 2 * i
        pair = add_planes(
            FINE.residual(u_ref, g_ref, b_ref, x), FINE.residual(u_ref, g_ref, b_ref, x + 1)
        )
        for q, (even, odd) in enumerate(join(pair)):
            out_ref[i, q] = 0.1 * jnp.where(row_of(even.shape) < 4, even, pltpu.roll(odd, 4, 0))

    each(0, BRICK_X // 2, body, 1)


def permuted(values, places):
    shape = (values.shape[1], values.shape[1])
    row, column = (lax.broadcasted_iota(jnp.int32, shape, d) for d in range(2))
    matrix = places(row, column).astype(jnp.float32).astype(jnp.bfloat16)
    total, rest = None, values
    terms = []
    for _ in range(3):
        term = rest.astype(jnp.bfloat16)
        rest = rest - term.astype(jnp.float32)
        terms.append(jnp.dot(term, matrix, preferred_element_type=jnp.float32))
    return terms[0] + (terms[1] + terms[2])


def lanes_kernel(where_ref, charges_ref, rows_ref, one_ref, two_ref):
    odd = where_ref[1] % 2
    width = charges_ref.shape[2]
    flat = charges_ref[...].reshape(BRICK_X * BRICK_Z, width)
    split = permuted(flat, lambda y, l: y == (l % LANES) * 4 + l // LANES)
    for p in range(4):
        tile = split[:, p * LANES : (p + 1) * LANES].reshape(BRICK_X, BRICK_Z, LANES)
        rows_ref[:, p] = tile
        first, last = tile[:, 0:8], tile[:, 8:16]
        one_ref[:, p] = jnp.where(odd == 0, last, first)
        two_ref[:, p] = jnp.where(odd == 0, first, last)


def down_kernel(count_x, count_z, where_ref, mid_ref, mid_rim_ref, one_ref, one_rim_ref, two_ref,
                two_rim_ref, u_ref, b_ref, out_ref, c_ref, g_ref, h_ref, rows_ref, masks_ref):
    rim_masks(count_x, count_z, where_ref, masks_ref)
    odd = where_ref[0] % 2

    def split_rows(ref, rim_ref, part):
        def split(x):
            for p in range(4):
                rows_ref[x, p, 0:BRICK_Z] = ref[x, p]
                rows_ref[x, p, BRICK_Z:WIDE_Z] = rim_ref[x, p]
                for q in range(4):
                    c_ref[part * BRICK_X + x, q, p] = rows_ref[x, p, pl.ds(q, 8, stride=4), :]

        each(0, BRICK_X, split, 1)

    split_rows(mid_ref, mid_rim_ref, 1)
    split_rows(one_ref, one_rim_ref, 2 - 2 * odd)
    split_rows(two_ref, two_rim_ref, 2 * odd)

    def source(x, weight):
        here = FINE.load(c_ref, x)
        sums = along_z(here, 1, True)
        plane = []
        for q in range(4):
            y_sums = along_y(here[q], 1)
            line = []
            for p in range(4):
                face = (c_ref[x - 1, q, p] + c_ref[x + 1, q, p]) + (sums[q][p] + y_sums[p])
                line.append((here[q][p] * 6.0 + face) * weight)
            plane.append(line)
        FINE.put(b_ref, g_ref, x, plane)

    each(1, WIDE_X - 1, masked(source, masks_ref, 0.2 / 12.0, BRICK_X), 2)

    def body(x, weight):
        FINE.put(u_ref, h_ref, x, FINE.sweep(b_ref, g_ref, b_ref, x, weight))

    each(2, WIDE_X - 2, masked(body, masks_ref, 1.0 / 30.0, BRICK_X), 2)
    send_residual(u_ref, h_ref, b_ref, out_ref)


def middle_kernel(count_x, count_z, count_pieces, where_ref, *refs):
    pieces, refs = refs[:count_pieces], refs[count_pieces:]
    u_ref, b_ref, v_ref, out_ref, u_refs, g_refs, masks_ref, *grids = refs
    rim_masks(count_x, count_z, where_ref, masks_ref)
    coarse_solve(count_x, count_z, where_ref, pieces, grids)
    coarse_ref = coarse_finish(count_x, grids)
    at_x, at_z = where_ref[0], where_ref[1]

    def error_of(i):
        plane = LEVEL_1.load(coarse_ref, 4 * at_x + i)
        return [[turned_tile(t, at_z, masks_ref[1]) for t in line] for line in plane]

    add_correction(error_of, u_ref, u_refs.at[0], g_refs.at[0], 2)
    fine_sweeps(u_refs, g_refs, b_ref, 3, 4, masks_ref)

    def keep(x):
        store_plane(v_ref, x, FINE.load(u_refs.at[0], x))

    each(6, WIDE_X - 6, keep, 1)
    send_residual(u_refs.at[0], g_refs.at[0], b_ref, out_ref)


def up_kernel(count_x, count_z, count_pieces, where_ref, *refs):
    pieces, refs = refs[:count_pieces], refs[count_pieces:]
    u_ref, b_ref, out_ref, u_refs, g_refs, rows_ref, masks_ref, *refs = refs
    near, grids = refs[:5], refs[5:]
    rim_masks(count_x, count_z, where_ref, masks_ref)
    coarse = coarse_solve(count_x, count_z, where_ref, pieces, grids)
    error_ref = near_finish(coarse, where_ref, masks_ref, near)
    add_correction(lambda i: NEAR_1.load(error_ref, i), u_ref, u_refs.at[0], g_refs.at[0], 6)
    fine_sweeps(u_refs, g_refs, b_ref, 7, 1, masks_ref)

    def body(x):
        plane = FINE.sweep(u_refs.at[1], g_refs.at[1], b_ref, x, 1.0 / 30.0)
        for q in range(4):
            for p in range(4):
                rows_ref[x - RIM, p, pl.ds(q, 4, stride=4), :] = plane[q][p][0:4]

    each(RIM, RIM + BRICK_X, body, 2)
    tiles = [rows_ref[:, p].reshape(BRICK_X * BRICK_Z, LANES) for p in range(4)]
    whole = permuted(
        jnp.concatenate(tiles, axis=1), lambda l, y: y == (l % LANES) * 4 + l // LANES
    )
    out_ref[...] = whole.reshape(out_ref.shape)


def call(kernel, outputs, scratch):
    shapes = [jax.ShapeDtypeStruct(shape, jnp.float32) for shape in outputs]
    held = sum(4 * math.prod(shape.shape) for shape in scratch)

    def run(where, *arrays):
        moved = sum(4 * math.prod(array.shape) for array in arrays + tuple(shapes))
        return pl.pallas_call(
            kernel,
            out_shape=shapes,
            in_specs=[pl.BlockSpec(memory_space=pltpu.SMEM)]
            + [pl.BlockSpec(memory_space=pltpu.VMEM)] * len(arrays),
            out_specs=[pl.BlockSpec(memory_space=pltpu.VMEM)] * len(shapes),
            scratch_shapes=scratch,
            compiler_params=pltpu.CompilerParams(vmem_limit_bytes=held + moved + SPARE_BYTES),
        )(where, *arrays)

    return run


def swap(axis, values, distance):
    count = lax.axis_size(axis)
    return lax.ppermute(values, axis, [(i, i ^ distance) for i in range(count)])


def swap_shifted(axis, values):
    pairs = [(i, i + 1) for i in range(1, lax.axis_size(axis) - 1, 2)]
    return lax.ppermute(values, axis, pairs + [(target, source) for source, target in pairs])


def every_piece(piece):
    count_x, count_z = lax.axis_size("gx"), lax.axis_size("gz")
    line = [swap("gz", piece[None], count_z - 1 - n) for n in range(count_z - 1)] + [piece[None]]
    halves = [jnp.concatenate(half) for half in (line[: count_z // 2], line[count_z // 2 :])]
    held = jnp.concatenate(halves + [swap("gx", half, 2) for half in halves])
    distance = 4
    while distance < count_x:
        held = jnp.concatenate([held, swap("gx", held, distance)])
        distance *= 2
    return held, swap("gx", held, 1)


def per_device(charges):
    count_x, count_z = lax.axis_size("gx"), lax.axis_size("gz")
    at_x, at_z = lax.axis_index("gx"), lax.axis_index("gz")
    where = jnp.stack([at_x, at_z]).astype(jnp.int32)
    brick, rim = (BRICK_X, 4, BRICK_Z, LANES), (BRICK_X, 4, RIM, LANES)
    middle, one, two = call(lanes_kernel, [brick, rim, rim], [])(where, charges)
    far = swap_shifted("gx", middle)
    near = swap("gx", middle, 1)
    one = swap("gz", one, 1)
    two = swap_shifted("gz", two)
    even = at_z % 2 == 0
    middle_rim = jnp.concatenate([jnp.where(even, one, two), jnp.where(even, two, one)], axis=2)
    far_rim = swap_shifted("gx", middle_rim)
    near_rim = swap("gx", middle_rim, 1)

    wide = (WIDE_X, 4, 4, 8, LANES)
    piece_shape = (BRICK_X // 2, 2, 8, LANES)
    fine = pltpu.VMEM(wide, jnp.float32)
    grids = coarse_grids(count_x, count_z)
    both = pltpu.VMEM((2,) + wide, jnp.float32)
    masks = pltpu.VMEM((3, 8, LANES), jnp.float32)
    rows_in = pltpu.VMEM((BRICK_X, 4, WIDE_Z, LANES), jnp.float32)
    close = pltpu.VMEM((WIDE_X // 2, 2, 2, 8, LANES), jnp.float32)
    rows_out = pltpu.VMEM((BRICK_X, 4, BRICK_Z, LANES), jnp.float32)

    u, b, piece = call(
        functools.partial(down_kernel, count_x, count_z),
        [wide, wide, piece_shape],
        [fine] * 3 + [rows_in, masks],
    )(where, middle, middle_rim, near, near_rim, far, far_rim)
    pieces = every_piece(piece)
    u, piece = call(
        functools.partial(middle_kernel, count_x, count_z, len(pieces)),
        [wide, piece_shape],
        [both, both, masks] + grids,
    )(where, *pieces, u, b)
    pieces = every_piece(piece)
    (potential,) = call(
        functools.partial(up_kernel, count_x, count_z, len(pieces)),
        [charges.shape],
        [both, both, rows_out, masks] + [close] * 5 + grids,
    )(where, *pieces, u, b)
    return potential


def solution(mesh):
    return jax.shard_map(
        per_device,
        mesh=mesh,
        in_specs=(P(("groups", "gx"), "gz", None),),
        out_specs=P(("groups", "gx"), "gz", None),
        check_vma=False,
    )
```

```python
import functools
import math

import jax
import jax.numpy as jnp
from jax import lax
from jax.experimental import pallas as pl
from jax.experimental.pallas import tpu as pltpu
from jax.sharding import PartitionSpec as P

COARSE_SWEEPS = 8
LANES = 128
RIM = 8
BRICK_X = 8
BRICK_Z = 16
WIDE_X = BRICK_X + 2 * RIM
WIDE_Z = BRICK_Z + 2 * RIM
SPARE_BYTES = 4 * 1024 * 1024


def lane_of(shape):
    return lax.broadcasted_iota(jnp.int32, shape, len(shape) - 1)


def row_of(shape):
    return lax.broadcasted_iota(jnp.int32, shape, len(shape) - 2)


def next_row(tile, step, cyclic):
    rows = tile.shape[0]
    moved = pltpu.roll(tile, rows - step, 0)
    return moved if cyclic else jnp.where(row_of(tile.shape) < rows - step, moved, 0.0)


def last_row(tile, step, cyclic):
    moved = pltpu.roll(tile, step, 0)
    return moved if cyclic else jnp.where(row_of(tile.shape) >= step, moved, 0.0)


def next_lane(tile, step):
    moved = pltpu.roll(tile, LANES - step, 1)
    return jnp.where(lane_of(tile.shape) < LANES - step, moved, 0.0)


def last_lane(tile, step):
    moved = pltpu.roll(tile, step, 1)
    return jnp.where(lane_of(tile.shape) >= step, moved, 0.0)


def load_plane(ref, x, count_q, count_p):
    return [[ref[x, q, p] for p in range(count_p)] for q in range(count_q)]


def store_plane(ref, x, plane):
    for q, line in enumerate(plane):
        for p, tile in enumerate(line):
            ref[x, q, p] = tile


def along_z(plane, step, cyclic):
    count_q, count_p = len(plane), len(plane[0])
    result = []
    for q in range(count_q):
        line = []
        for p in range(count_p):
            after = plane[q + 1][p] if q + 1 < count_q else next_row(plane[0][p], step, cyclic)
            before = plane[q - 1][p] if q > 0 else last_row(plane[-1][p], step, cyclic)
            line.append(after + before)
        result.append(line)
    return result


def along_y(line, step):
    count_p = len(line)
    result = []
    for p in range(count_p):
        after = line[p + 1] if p + 1 < count_p else next_lane(line[0], step)
        before = line[p - 1] if p > 0 else last_lane(line[-1], step)
        result.append(after + before)
    return result


class Level:
    def __init__(self, count_q, count_p, step, cyclic):
        self.count_q, self.count_p, self.step, self.cyclic = count_q, count_p, step, cyclic

    def load(self, ref, x):
        return load_plane(ref, x, self.count_q, self.count_p)

    def put(self, u_ref, g_ref, x, plane):
        store_plane(u_ref, x, plane)
        sums = along_z(plane, self.step, self.cyclic)
        store_plane(
            g_ref,
            x,
            [
                [s + (v + v) for s, v in zip(sum_line, line)]
                for sum_line, line in zip(sums, plane)
            ],
        )

    def spread(self, u_ref, g_ref, x, with_u):
        result = []
        for q in range(self.count_q):
            sides, both = [], []
            for p in range(self.count_p):
                here = g_ref[x, q, p]
                sides.append((u_ref[x - 1, q, p] + u_ref[x + 1, q, p]) + here)
                if with_u:
                    here = here + u_ref[x, q, p]
                both.append((g_ref[x - 1, q, p] + g_ref[x + 1, q, p]) + (here + here))
            result.append([a + b for a, b in zip(both, along_y(sides, self.step))])
        return result

    def sweep(self, u_ref, g_ref, b_ref, x, weight):
        wide = self.spread(u_ref, g_ref, x, True)
        return [
            [b_ref[x, q, p] + wide[q][p] * weight for p in range(self.count_p)]
            for q in range(self.count_q)
        ]

    def residual(self, u_ref, g_ref, b_ref, x):
        wide = self.spread(u_ref, g_ref, x, False)
        return [
            [
                b_ref[x, q, p] * 5.0 + (wide[q][p] - u_ref[x, q, p] * 28.0) * (1.0 / 6.0)
                for p in range(self.count_p)
            ]
            for q in range(self.count_q)
        ]


def add_planes(one, other):
    return [[a + b for a, b in zip(l, m)] for l, m in zip(one, other)]


def join(plane):
    lines = [[a + b for a, b in zip(plane[q], plane[q + 1])] for q in range(0, len(plane), 2)]
    return [[line[p] + line[p + 1] for p in range(0, len(line), 2)] for line in lines]


def join_within(tile):
    rows = tile.shape[0]
    even = row_of(tile.shape) % 2 == 0
    tile = tile + jnp.where(even, pltpu.roll(tile, rows - 1, 0), pltpu.roll(tile, 1, 0))
    even = lane_of(tile.shape) % 2 == 0
    return tile + jnp.where(even, pltpu.roll(tile, LANES - 1, 1), pltpu.roll(tile, 1, 1))


def scaled(plane, factor):
    return [[tile * factor for tile in line] for line in plane]


def each(lo, hi, body, chunk):
    count = hi - lo
    whole = count // chunk
    if whole == 1:
        for x in range(lo, lo + chunk):
            body(x)
    elif whole > 1:

        def step(i, carry):
            for d in range(chunk):
                body(lo + i * chunk + d)
            return carry

        lax.fori_loop(0, whole, step, 0)
    for x in range(lo + whole * chunk, hi):
        body(x)


FINE = Level(4, 4, 1, True)
LEVEL_1 = Level(2, 2, 1, False)
NEAR_1 = Level(2, 2, 1, True)
LEVEL_2 = Level(1, 1, 1, False)
LEVEL_3 = Level(1, 1, 2, False)
PAD = RIM // 2
PAD_2 = RIM // 4


def zero_planes(ref, indices):
    for x in indices:
        ref[x] = jnp.zeros(ref.shape[1:], ref.dtype)


def coarse_grids(count_x, count_z):
    rows = count_z * BRICK_Z // 4
    shapes = []
    for planes, count in ((4 * count_x + 2 * PAD, 2), (2 * count_x + 2 * PAD_2, 1), (count_x + 2, 1)):
        shapes += [pltpu.VMEM((planes, count, count, rows, LANES), jnp.float32)] * 5
    return shapes


def coarse_solve(count_x, count_z, where_ref, pieces, grids):
    (ua1, ub1, ga1, gb1, b1), (ua2, ub2, ga2, gb2, b2), (ua3, ub3, ga3, gb3, b3) = (
        grids[0:5],
        grids[5:10],
        grids[10:15],
    )
    size_1, size_2, size_3 = 4 * count_x, 2 * count_x, count_x
    for refs, pad, size in (
        ((ua1, ub1, ga1, gb1, b1), PAD, size_1),
        ((ua2, ub2, ga2, gb2), PAD_2, size_2),
        ((ua3, ub3, ga3, gb3), 1, size_3),
    ):
        for ref in refs:
            zero_planes(ref, list(range(pad)) + list(range(pad + size, pad + size + pad)))
    third = 1.0 / 30.0

    at_x, at_z = where_ref[0], where_ref[1]

    def place(x, load):
        for i in range(4):
            plane = []
            for q in range(2):
                even, odd = [], []
                for z in range(0, count_z, 2):
                    one, two = load(z, i, q), load(z + 1, i, q)
                    first = row_of(one.shape) < 4
                    even.append(jnp.where(first, one, pltpu.roll(two, 4, 0)))
                    odd.append(jnp.where(first, pltpu.roll(one, 4, 0), two))
                plane.append([jnp.concatenate(even, axis=0), jnp.concatenate(odd, axis=0)])
            store_plane(b1, x + i, plane)
            LEVEL_1.put(ub1, gb1, x + i, plane)

    if len(pieces) == 1:

        def gather(n):
            place(PAD + 4 * n, lambda z, i, q: pieces[0][n * count_z + z, i, q])

        each(0, count_x, gather, 1)
    else:

        def gather(n):
            for core in range(2):
                x = PAD + 4 * ((2 * n + core) ^ at_x)
                place(x, lambda z, i, q: pieces[core][n * count_z + (z ^ at_z ^ (count_z - 1)), i, q])

        each(0, count_x // 2, gather, 1)

    def sweep(level, u_in, g_in, u_out, g_out, b):
        return lambda x: level.put(u_out, g_out, x, level.sweep(u_in, g_in, b, x, third))

    each(PAD, PAD + size_1, sweep(LEVEL_1, ub1, gb1, ua1, ga1, b1), 16)

    def restrict_1(x):
        fine = PAD + 2 * x
        pair = add_planes(
            LEVEL_1.residual(ua1, ga1, b1, fine), LEVEL_1.residual(ua1, ga1, b1, fine + 1)
        )
        plane = scaled(join(pair), 0.5 * 0.2)
        store_plane(b2, PAD_2 + x, plane)
        LEVEL_2.put(ub2, gb2, PAD_2 + x, plane)

    each(0, size_2, restrict_1, 8)
    all_2 = (PAD_2, PAD_2 + size_2)
    each(*all_2, sweep(LEVEL_2, ub2, gb2, ua2, ga2, b2), 8)

    def restrict_2(x):
        fine = PAD_2 + 2 * x
        pair = add_planes(
            LEVEL_2.residual(ua2, ga2, b2, fine), LEVEL_2.residual(ua2, ga2, b2, fine + 1)
        )
        plane = [[join_within(pair[0][0]) * (0.5 * 0.2)]]
        store_plane(b3, 1 + x, plane)
        LEVEL_3.put(ub3, gb3, 1 + x, plane)

    each(0, size_3, restrict_2, 4)
    now, later = (ub3, gb3), (ua3, ga3)
    for _ in range(COARSE_SWEEPS - 1):
        each(1, 1 + size_3, sweep(LEVEL_3, *now, *later, b3), 4)
        now, later = later, now

    def prolong_3(x):
        for d in range(2):
            fine = PAD_2 + 2 * x + d
            LEVEL_2.put(ua2, ga2, fine, [[ua2[fine, 0, 0] + now[0][1 + x, 0, 0]]])

    each(0, size_3, prolong_3, 4)
    each(*all_2, sweep(LEVEL_2, ua2, ga2, ub2, gb2, b2), 8)
    each(*all_2, sweep(LEVEL_2, ub2, gb2, ua2, ga2, b2), 8)
    return ua1, ua2, b1


def coarse_finish(count_x, grids):
    ua1, ub1, ga1, gb1, b1 = grids[0:5]
    ua2 = grids[5]
    size_1, size_2 = 4 * count_x, 2 * count_x

    def prolong_2(x):
        error = ua2[PAD_2 + x, 0, 0]
        for d in range(2):
            fine = PAD + 2 * x + d
            LEVEL_1.put(
                ua1, ga1, fine, [[t + error for t in line] for line in LEVEL_1.load(ua1, fine)]
            )

    def sweep(u_in, g_in, u_out, g_out):
        return lambda x: LEVEL_1.put(
            u_out, g_out, x, LEVEL_1.sweep(u_in, g_in, b1, x, 1.0 / 30.0)
        )

    each(0, size_2, prolong_2, 8)
    each(PAD, PAD + size_1, sweep(ua1, ga1, ub1, gb1), 16)
    each(PAD, PAD + size_1, sweep(ub1, gb1, ua1, ga1), 16)
    return ua1


def turned_tile(tile, at_z, rows):
    count = tile.shape[0]
    turned = pltpu.roll(tile, lax.rem(count - 4 * at_z, count), 0)
    return jnp.where(row_of((8, LANES)) < 6, turned[0:8], turned[count - 8 : count]) * rows


def near_finish(coarse, where_ref, masks, near):
    ua1, ua2, b1 = coarse
    ua, ga, ub, gb, b = near
    at_x, at_z = where_ref[0], where_ref[1]
    rows = masks[0]

    def take(i):
        error = ua2[2 * at_x + i // 2, 0, 0]
        plane = [[t + error for t in line] for line in LEVEL_1.load(ua1, 4 * at_x + i)]
        plane = [[turned_tile(t, at_z, rows) for t in line] for line in plane]
        NEAR_1.put(ua, ga, i, plane)
        plane = LEVEL_1.load(b1, 4 * at_x + i)
        store_plane(b, i, [[turned_tile(t, at_z, rows) for t in line] for line in plane])

    each(1, 11, take, 5)

    def sweep(u_in, g_in, u_out, g_out):
        def body(i, weight):
            NEAR_1.put(u_out, g_out, i, NEAR_1.sweep(u_in, g_in, b, i, weight))

        return body

    in_segments(2, 10, sweep(ua, ga, ub, gb), masks, 1.0 / 30.0, 4, PAD, BRICK_X // 2)
    in_segments(3, 9, sweep(ub, gb, ua, ga), masks, 1.0 / 30.0, 4, PAD, BRICK_X // 2)
    return ua


def rim_masks(count_x, count_z, where_ref):
    at_x, at_z = where_ref[0], where_ref[1]
    k = row_of((8, LANES))
    low = (at_z > 0).astype(jnp.float32)
    high = (at_z < count_z - 1).astype(jnp.float32)
    rows = jnp.where(k < 4, 1.0, jnp.where(k < 6, high, low))
    below = (at_x > 0).astype(jnp.float32)
    above = (at_x < count_x - 1).astype(jnp.float32)
    return rows, below, above


def in_segments(lo, hi, body, masks, scale, chunk, rim=RIM, brick=BRICK_X):
    rows, below, above = masks
    inner = rows * scale
    for start, end, weight in (
        (lo, min(hi, rim), inner * below),
        (max(lo, rim), min(hi, rim + brick), inner),
        (max(lo, rim + brick), hi, inner * above),
    ):
        if end > start:
            each(start, end, functools.partial(body, weight=weight), chunk)


def fine_sweep(u_in, g_in, u_out, g_out, b_ref, margin, masks):
    def body(x, weight):
        FINE.put(u_out, g_out, x, FINE.sweep(u_in, g_in, b_ref, x, weight))

    in_segments(margin, WIDE_X - margin, body, masks, 1.0 / 30.0, 4)


def add_correction(error_of, u_in, u_out, g_out, margin):
    def body(i):
        error = error_of(i)
        for d in range(2):
            x = 2 * i + d
            plane = [
                [u_in[x, q, p] + error[q // 2][p // 2] for p in range(4)] for q in range(4)
            ]
            FINE.put(u_out, g_out, x, plane)

    each(margin // 2, (WIDE_X - margin) // 2, body, 2)


def send_residual(u_ref, g_ref, b_ref, out_ref):
    def body(i):
        x = RIM + 2 * i
        pair = add_planes(
            FINE.residual(u_ref, g_ref, b_ref, x), FINE.residual(u_ref, g_ref, b_ref, x + 1)
        )
        for q, (even, odd) in enumerate(join(pair)):
            out_ref[i, q] = 0.1 * jnp.where(row_of(even.shape) < 4, even, pltpu.roll(odd, 4, 0))

    each(0, BRICK_X // 2, body, BRICK_X // 2)


def permuted(values, places):
    shape = (values.shape[1], values.shape[1])
    row, column = (lax.broadcasted_iota(jnp.int32, shape, d) for d in range(2))
    matrix = places(row, column).astype(jnp.float32).astype(jnp.bfloat16)
    total, rest = None, values
    terms = []
    for _ in range(3):
        term = rest.astype(jnp.bfloat16)
        rest = rest - term.astype(jnp.float32)
        terms.append(jnp.dot(term, matrix, preferred_element_type=jnp.float32))
    return terms[0] + (terms[1] + terms[2])


def lanes_kernel(where_ref, charges_ref, rows_ref, one_ref, two_ref):
    odd = where_ref[1] % 2
    width = charges_ref.shape[2]
    flat = charges_ref[...].reshape(BRICK_X * BRICK_Z, width)
    split = permuted(flat, lambda y, l: y == (l % LANES) * 4 + l // LANES)
    for p in range(4):
        tile = split[:, p * LANES : (p + 1) * LANES].reshape(BRICK_X, BRICK_Z, LANES)
        rows_ref[:, p] = tile
        first, last = tile[:, 0:8], tile[:, 8:16]
        one_ref[:, p] = jnp.where(odd == 0, last, first)
        two_ref[:, p] = jnp.where(odd == 0, first, last)


def down_kernel(count_x, count_z, where_ref, mid_ref, mid_rim_ref, one_ref, one_rim_ref, two_ref,
                two_rim_ref, u_ref, b_ref, out_ref, c_ref, g_ref, h_ref, rows_ref):
    masks = rim_masks(count_x, count_z, where_ref)
    odd = where_ref[0] % 2

    def split_rows(ref, rim_ref, part):
        def split(x):
            for p in range(4):
                rows_ref[x, p, 0:BRICK_Z] = ref[x, p]
                rows_ref[x, p, BRICK_Z:WIDE_Z] = rim_ref[x, p]
                for q in range(4):
                    c_ref[part * BRICK_X + x, q, p] = rows_ref[x, p, pl.ds(q, 8, stride=4), :]

        each(0, BRICK_X, split, 2)

    split_rows(mid_ref, mid_rim_ref, 1)
    split_rows(one_ref, one_rim_ref, 2 - 2 * odd)
    split_rows(two_ref, two_rim_ref, 2 * odd)

    def source(x, weight):
        here = FINE.load(c_ref, x)
        sums = along_z(here, 1, True)
        plane = []
        for q in range(4):
            y_sums = along_y(here[q], 1)
            line = []
            for p in range(4):
                face = (c_ref[x - 1, q, p] + c_ref[x + 1, q, p]) + (sums[q][p] + y_sums[p])
                line.append((here[q][p] * 6.0 + face) * weight)
            plane.append(line)
        FINE.put(b_ref, g_ref, x, plane)

    in_segments(1, WIDE_X - 1, source, masks, 0.2 / 12.0, 4)

    def body(x, weight):
        FINE.put(u_ref, h_ref, x, FINE.sweep(b_ref, g_ref, b_ref, x, weight))

    in_segments(2, WIDE_X - 2, body, masks, 1.0 / 30.0, 4)
    send_residual(u_ref, h_ref, b_ref, out_ref)


def middle_kernel(count_x, count_z, count_pieces, where_ref, *refs):
    pieces, refs = refs[:count_pieces], refs[count_pieces:]
    u_ref, b_ref, v_ref, out_ref, ga_ref, gb_ref, ua_ref, *grids = refs
    masks = rim_masks(count_x, count_z, where_ref)
    coarse_solve(count_x, count_z, where_ref, pieces, grids)
    coarse_ref = coarse_finish(count_x, grids)
    at_x, at_z = where_ref[0], where_ref[1]

    def error_of(i):
        plane = LEVEL_1.load(coarse_ref, 4 * at_x + i)
        return [[turned_tile(t, at_z, masks[0]) for t in line] for line in plane]

    add_correction(error_of, u_ref, v_ref, ga_ref, 2)
    fine_sweep(v_ref, ga_ref, ua_ref, gb_ref, b_ref, 3, masks)
    fine_sweep(ua_ref, gb_ref, v_ref, ga_ref, b_ref, 4, masks)
    fine_sweep(v_ref, ga_ref, ua_ref, gb_ref, b_ref, 5, masks)
    fine_sweep(ua_ref, gb_ref, v_ref, ga_ref, b_ref, 6, masks)
    send_residual(v_ref, ga_ref, b_ref, out_ref)


def up_kernel(count_x, count_z, count_pieces, where_ref, *refs):
    pieces, refs = refs[:count_pieces], refs[count_pieces:]
    u_ref, b_ref, out_ref, ga_ref, gb_ref, ua_ref, ub_ref, rows_ref, *refs = refs
    near, grids = refs[:5], refs[5:]
    masks = rim_masks(count_x, count_z, where_ref)
    coarse = coarse_solve(count_x, count_z, where_ref, pieces, grids)
    error_ref = near_finish(coarse, where_ref, masks, near)
    add_correction(lambda i: NEAR_1.load(error_ref, i), u_ref, ua_ref, ga_ref, 6)
    fine_sweep(ua_ref, ga_ref, ub_ref, gb_ref, b_ref, 7, masks)

    def body(x):
        plane = FINE.sweep(ub_ref, gb_ref, b_ref, x, 1.0 / 30.0)
        for q in range(4):
            for p in range(4):
                rows_ref[x - RIM, p, pl.ds(q, 4, stride=4), :] = plane[q][p][0:4]

    each(RIM, RIM + BRICK_X, body, 2)
    tiles = [rows_ref[:, p].reshape(BRICK_X * BRICK_Z, LANES) for p in range(4)]
    whole = permuted(
        jnp.concatenate(tiles, axis=1), lambda l, y: y == (l % LANES) * 4 + l // LANES
    )
    out_ref[...] = whole.reshape(out_ref.shape)


def call(kernel, outputs, scratch):
    shapes = [jax.ShapeDtypeStruct(shape, jnp.float32) for shape in outputs]
    held = sum(4 * math.prod(shape.shape) for shape in scratch)

    def run(where, *arrays):
        moved = sum(4 * math.prod(array.shape) for array in arrays + tuple(shapes))
        return pl.pallas_call(
            kernel,
            out_shape=shapes,
            in_specs=[pl.BlockSpec(memory_space=pltpu.SMEM)]
            + [pl.BlockSpec(memory_space=pltpu.VMEM)] * len(arrays),
            out_specs=[pl.BlockSpec(memory_space=pltpu.VMEM)] * len(shapes),
            scratch_shapes=scratch,
            compiler_params=pltpu.CompilerParams(vmem_limit_bytes=held + moved + SPARE_BYTES),
        )(where, *arrays)

    return run


def pairs_apart(count, distance):
    return [(i, i ^ distance) for i in range(count)]


def pairs_shifted(count):
    pairs = [(i, i + 1) for i in range(1, count - 1, 2)]
    return pairs + [(target, source) for source, target in pairs]


def across(pairs_x, pairs_z, count_z):
    return [
        (x_from * count_z + z_from, x_to * count_z + z_to)
        for x_from, x_to in pairs_x
        for z_from, z_to in pairs_z
    ]


def swap(axis, values, distance):
    return lax.ppermute(values, axis, pairs_apart(lax.axis_size(axis), distance))


def every_piece(piece):
    count_x, count_z = lax.axis_size("gx"), lax.axis_size("gz")
    line = [swap("gz", piece[None], count_z - 1 - n) for n in range(count_z - 1)] + [piece[None]]
    halves = [jnp.concatenate(half) for half in (line[: count_z // 2], line[count_z // 2 :])]
    held = jnp.concatenate(halves + [swap("gx", half, 2) for half in halves])
    distance = 4
    while distance < count_x:
        held = jnp.concatenate([held, swap("gx", held, distance)])
        distance *= 2
    return held, swap("gx", held, 1)


def per_device(charges):
    count_x, count_z = lax.axis_size("gx"), lax.axis_size("gz")
    at_x, at_z = lax.axis_index("gx"), lax.axis_index("gz")
    where = jnp.stack([at_x, at_z]).astype(jnp.int32)
    brick, rim = (BRICK_X, 4, BRICK_Z, LANES), (BRICK_X, 4, RIM, LANES)
    middle, one, two = call(lanes_kernel, [brick, rim, rim], [])(where, charges)
    z_one = pairs_apart(count_z, 1)
    z_two = pairs_shifted(count_z)
    x_far = pairs_shifted(count_x)
    even = at_z % 2 == 0

    def both_rims(from_one, from_two):
        after, before = jnp.where(even, from_one, from_two), jnp.where(even, from_two, from_one)
        return jnp.concatenate([after, before], axis=2)

    far = lax.ppermute(middle, "gx", x_far)
    far_rim = both_rims(
        lax.ppermute(one, ("gx", "gz"), across(x_far, z_one, count_z)),
        lax.ppermute(two, ("gx", "gz"), across(x_far, z_two, count_z)),
    )
    middle_rim = both_rims(lax.ppermute(one, "gz", z_one), lax.ppermute(two, "gz", z_two))
    near = swap("gx", middle, 1)
    near_rim = swap("gx", middle_rim, 1)

    wide = (WIDE_X, 4, 4, 8, LANES)
    piece_shape = (BRICK_X // 2, 2, 8, LANES)
    fine = pltpu.VMEM(wide, jnp.float32)
    grids = coarse_grids(count_x, count_z)
    rows_in = pltpu.VMEM((BRICK_X, 4, WIDE_Z, LANES), jnp.float32)
    close = pltpu.VMEM((WIDE_X // 2, 2, 2, 8, LANES), jnp.float32)
    rows_out = pltpu.VMEM((BRICK_X, 4, BRICK_Z, LANES), jnp.float32)

    u, b, piece = call(
        functools.partial(down_kernel, count_x, count_z),
        [wide, wide, piece_shape],
        [fine] * 3 + [rows_in],
    )(where, middle, middle_rim, near, near_rim, far, far_rim)
    pieces = every_piece(piece)
    u, piece = call(
        functools.partial(middle_kernel, count_x, count_z, len(pieces)),
        [wide, piece_shape],
        [fine] * 3 + grids,
    )(where, *pieces, u, b)
    pieces = every_piece(piece)
    (potential,) = call(
        functools.partial(up_kernel, count_x, count_z, len(pieces)),
        [charges.shape],
        [fine] * 4 + [rows_out] + [close] * 5 + grids,
    )(where, *pieces, u, b)
    return potential


def solution(mesh):
    return jax.shard_map(
        per_device,
        mesh=mesh,
        in_specs=(P(("groups", "gx"), "gz", None),),
        out_specs=P(("groups", "gx"), "gz", None),
        check_vma=False,
    )
```

```python
import functools
import math

import jax
import jax.numpy as jnp
from jax import lax
from jax.experimental import pallas as pl
from jax.experimental.pallas import tpu as pltpu
from jax.sharding import PartitionSpec as P

COARSE_SWEEPS = 8
LANES = 128
RIM = 8
BRICK_X = 8
BRICK_Z = 16
WIDE_X = BRICK_X + 2 * RIM
WIDE_Z = BRICK_Z + 2 * RIM
SPARE_BYTES = 4 * 1024 * 1024


def lane_of(shape):
    return lax.broadcasted_iota(jnp.int32, shape, len(shape) - 1)


def row_of(shape):
    return lax.broadcasted_iota(jnp.int32, shape, len(shape) - 2)


def next_row(tile, step, cyclic):
    rows = tile.shape[0]
    moved = pltpu.roll(tile, rows - step, 0)
    return moved if cyclic else jnp.where(row_of(tile.shape) < rows - step, moved, 0.0)


def last_row(tile, step, cyclic):
    moved = pltpu.roll(tile, step, 0)
    return moved if cyclic else jnp.where(row_of(tile.shape) >= step, moved, 0.0)


def next_lane(tile, step):
    moved = pltpu.roll(tile, LANES - step, 1)
    return jnp.where(lane_of(tile.shape) < LANES - step, moved, 0.0)


def last_lane(tile, step):
    moved = pltpu.roll(tile, step, 1)
    return jnp.where(lane_of(tile.shape) >= step, moved, 0.0)


def load_plane(ref, x, count_q, count_p):
    return [[ref[x, q, p] for p in range(count_p)] for q in range(count_q)]


def store_plane(ref, x, plane):
    for q, line in enumerate(plane):
        for p, tile in enumerate(line):
            ref[x, q, p] = tile


def along_z(plane, step, cyclic):
    count_q, count_p = len(plane), len(plane[0])
    result = []
    for q in range(count_q):
        line = []
        for p in range(count_p):
            after = plane[q + 1][p] if q + 1 < count_q else next_row(plane[0][p], step, cyclic)
            before = plane[q - 1][p] if q > 0 else last_row(plane[-1][p], step, cyclic)
            line.append(after + before)
        result.append(line)
    return result


def along_y(line, step):
    count_p = len(line)
    result = []
    for p in range(count_p):
        after = line[p + 1] if p + 1 < count_p else next_lane(line[0], step)
        before = line[p - 1] if p > 0 else last_lane(line[-1], step)
        result.append(after + before)
    return result


class Level:
    def __init__(self, count_q, count_p, step, cyclic):
        self.count_q, self.count_p, self.step, self.cyclic = count_q, count_p, step, cyclic

    def load(self, ref, x):
        return load_plane(ref, x, self.count_q, self.count_p)

    def put(self, u_ref, g_ref, x, plane):
        store_plane(u_ref, x, plane)
        sums = along_z(plane, self.step, self.cyclic)
        store_plane(
            g_ref,
            x,
            [
                [s + (v + v) for s, v in zip(sum_line, line)]
                for sum_line, line in zip(sums, plane)
            ],
        )

    def spread(self, u_ref, g_ref, x, with_u):
        result = []
        for q in range(self.count_q):
            sides, both = [], []
            for p in range(self.count_p):
                here = g_ref[x, q, p]
                sides.append((u_ref[x - 1, q, p] + u_ref[x + 1, q, p]) + here)
                if with_u:
                    here = here + u_ref[x, q, p]
                both.append((g_ref[x - 1, q, p] + g_ref[x + 1, q, p]) + (here + here))
            result.append([a + b for a, b in zip(both, along_y(sides, self.step))])
        return result

    def sweep(self, u_ref, g_ref, b_ref, x, weight):
        wide = self.spread(u_ref, g_ref, x, True)
        return [
            [b_ref[x, q, p] + wide[q][p] * weight for p in range(self.count_p)]
            for q in range(self.count_q)
        ]

    def residual(self, u_ref, g_ref, b_ref, x):
        wide = self.spread(u_ref, g_ref, x, False)
        return [
            [
                b_ref[x, q, p] * 5.0 + (wide[q][p] - u_ref[x, q, p] * 28.0) * (1.0 / 6.0)
                for p in range(self.count_p)
            ]
            for q in range(self.count_q)
        ]


def add_planes(one, other):
    return [[a + b for a, b in zip(l, m)] for l, m in zip(one, other)]


def join(plane):
    lines = [[a + b for a, b in zip(plane[q], plane[q + 1])] for q in range(0, len(plane), 2)]
    return [[line[p] + line[p + 1] for p in range(0, len(line), 2)] for line in lines]


def join_within(tile):
    rows = tile.shape[0]
    even = row_of(tile.shape) % 2 == 0
    tile = tile + jnp.where(even, pltpu.roll(tile, rows - 1, 0), pltpu.roll(tile, 1, 0))
    even = lane_of(tile.shape) % 2 == 0
    return tile + jnp.where(even, pltpu.roll(tile, LANES - 1, 1), pltpu.roll(tile, 1, 1))


def scaled(plane, factor):
    return [[tile * factor for tile in line] for line in plane]


def each(lo, hi, body, chunk):
    count = hi - lo
    whole = count // chunk
    if whole == 1:
        for x in range(lo, lo + chunk):
            body(x)
    elif whole > 1:

        def step(i, carry):
            for d in range(chunk):
                body(lo + i * chunk + d)
            return carry

        lax.fori_loop(0, whole, step, 0)
    for x in range(lo + whole * chunk, hi):
        body(x)


FINE = Level(4, 4, 1, True)
LEVEL_1 = Level(2, 2, 1, False)
NEAR_1 = Level(2, 2, 1, True)
LEVEL_2 = Level(1, 1, 1, False)
LEVEL_3 = Level(1, 1, 2, False)
PAD = RIM // 2
PAD_2 = RIM // 4


def zero_planes(ref, indices):
    for x in indices:
        ref[x] = jnp.zeros(ref.shape[1:], ref.dtype)


def coarse_grids(count_x, count_z):
    rows = count_z * BRICK_Z // 4
    shapes = []
    for planes, count in ((4 * count_x + 2 * PAD, 2), (2 * count_x + 2 * PAD_2, 1), (count_x + 2, 1)):
        shapes += [pltpu.VMEM((planes, count, count, rows, LANES), jnp.float32)] * 5
    return shapes


def coarse_solve(count_x, count_z, where_ref, pieces, grids):
    (ua1, ub1, ga1, gb1, b1), (ua2, ub2, ga2, gb2, b2), (ua3, ub3, ga3, gb3, b3) = (
        grids[0:5],
        grids[5:10],
        grids[10:15],
    )
    size_1, size_2, size_3 = 4 * count_x, 2 * count_x, count_x
    for refs, pad, size in (
        ((ua1, ub1, ga1, gb1, b1), PAD, size_1),
        ((ua2, ub2, ga2, gb2), PAD_2, size_2),
        ((ua3, ub3, ga3, gb3), 1, size_3),
    ):
        for ref in refs:
            zero_planes(ref, list(range(pad)) + list(range(pad + size, pad + size + pad)))
    third = 1.0 / 30.0

    at_x, at_z = where_ref[0], where_ref[1]

    def place(x, load):
        for i in range(4):
            plane = []
            for q in range(2):
                even, odd = [], []
                for z in range(0, count_z, 2):
                    one, two = load(z, i, q), load(z + 1, i, q)
                    first = row_of(one.shape) < 4
                    even.append(jnp.where(first, one, pltpu.roll(two, 4, 0)))
                    odd.append(jnp.where(first, pltpu.roll(one, 4, 0), two))
                plane.append([jnp.concatenate(even, axis=0), jnp.concatenate(odd, axis=0)])
            store_plane(b1, x + i, plane)
            LEVEL_1.put(ub1, gb1, x + i, plane)

    if len(pieces) == 1:

        def gather(n):
            place(PAD + 4 * n, lambda z, i, q: pieces[0][n * count_z + z, i, q])

        each(0, count_x, gather, 1)
    else:

        def gather(n):
            for core in range(2):
                x = PAD + 4 * ((2 * n + core) ^ at_x)
                place(x, lambda z, i, q: pieces[core][n * count_z + (z ^ at_z ^ (count_z - 1)), i, q])

        each(0, count_x // 2, gather, 1)

    def sweep(level, u_in, g_in, u_out, g_out, b):
        return lambda x: level.put(u_out, g_out, x, level.sweep(u_in, g_in, b, x, third))

    each(PAD, PAD + size_1, sweep(LEVEL_1, ub1, gb1, ua1, ga1, b1), 16)

    def restrict_1(x):
        fine = PAD + 2 * x
        pair = add_planes(
            LEVEL_1.residual(ua1, ga1, b1, fine), LEVEL_1.residual(ua1, ga1, b1, fine + 1)
        )
        plane = scaled(join(pair), 0.5 * 0.2)
        store_plane(b2, PAD_2 + x, plane)
        LEVEL_2.put(ub2, gb2, PAD_2 + x, plane)

    each(0, size_2, restrict_1, 8)
    all_2 = (PAD_2, PAD_2 + size_2)
    each(*all_2, sweep(LEVEL_2, ub2, gb2, ua2, ga2, b2), 8)

    def restrict_2(x):
        fine = PAD_2 + 2 * x
        pair = add_planes(
            LEVEL_2.residual(ua2, ga2, b2, fine), LEVEL_2.residual(ua2, ga2, b2, fine + 1)
        )
        plane = [[join_within(pair[0][0]) * (0.5 * 0.2)]]
        store_plane(b3, 1 + x, plane)
        LEVEL_3.put(ub3, gb3, 1 + x, plane)

    each(0, size_3, restrict_2, 4)
    now, later = (ub3, gb3), (ua3, ga3)
    for _ in range(COARSE_SWEEPS - 1):
        each(1, 1 + size_3, sweep(LEVEL_3, *now, *later, b3), 4)
        now, later = later, now

    def prolong_3(x):
        for d in range(2):
            fine = PAD_2 + 2 * x + d
            LEVEL_2.put(ua2, ga2, fine, [[ua2[fine, 0, 0] + now[0][1 + x, 0, 0]]])

    each(0, size_3, prolong_3, 4)
    each(*all_2, sweep(LEVEL_2, ua2, ga2, ub2, gb2, b2), 8)
    each(*all_2, sweep(LEVEL_2, ub2, gb2, ua2, ga2, b2), 8)
    return ua1, ua2, b1


def coarse_finish(count_x, grids):
    ua1, ub1, ga1, gb1, b1 = grids[0:5]
    ua2 = grids[5]
    size_1, size_2 = 4 * count_x, 2 * count_x

    def prolong_2(x):
        error = ua2[PAD_2 + x, 0, 0]
        for d in range(2):
            fine = PAD + 2 * x + d
            LEVEL_1.put(
                ua1, ga1, fine, [[t + error for t in line] for line in LEVEL_1.load(ua1, fine)]
            )

    def sweep(u_in, g_in, u_out, g_out):
        return lambda x: LEVEL_1.put(
            u_out, g_out, x, LEVEL_1.sweep(u_in, g_in, b1, x, 1.0 / 30.0)
        )

    each(0, size_2, prolong_2, 8)
    each(PAD, PAD + size_1, sweep(ua1, ga1, ub1, gb1), 16)
    each(PAD, PAD + size_1, sweep(ub1, gb1, ua1, ga1), 16)
    return ua1


def turned_tile(tile, at_z, rows):
    count = tile.shape[0]
    turned = pltpu.roll(tile, lax.rem(count - 4 * at_z, count), 0)
    return jnp.where(row_of((8, LANES)) < 6, turned[0:8], turned[count - 8 : count]) * rows


def near_finish(coarse, where_ref, masks, near):
    ua1, ua2, b1 = coarse
    ua, ga, ub, gb, b = near
    at_x, at_z = where_ref[0], where_ref[1]
    rows = masks[0]

    def take(i):
        error = ua2[2 * at_x + i // 2, 0, 0]
        plane = [[t + error for t in line] for line in LEVEL_1.load(ua1, 4 * at_x + i)]
        plane = [[turned_tile(t, at_z, rows) for t in line] for line in plane]
        NEAR_1.put(ua, ga, i, plane)
        plane = LEVEL_1.load(b1, 4 * at_x + i)
        store_plane(b, i, [[turned_tile(t, at_z, rows) for t in line] for line in plane])

    each(1, 11, take, 5)

    def sweep(u_in, g_in, u_out, g_out):
        def body(i, weight):
            NEAR_1.put(u_out, g_out, i, NEAR_1.sweep(u_in, g_in, b, i, weight))

        return body

    in_segments(2, 10, sweep(ua, ga, ub, gb), masks, 1.0 / 30.0, 4, PAD, BRICK_X // 2)
    in_segments(3, 9, sweep(ub, gb, ua, ga), masks, 1.0 / 30.0, 4, PAD, BRICK_X // 2)
    return ua


def rim_masks(count_x, count_z, where_ref):
    at_x, at_z = where_ref[0], where_ref[1]
    k = row_of((8, LANES))
    low = (at_z > 0).astype(jnp.float32)
    high = (at_z < count_z - 1).astype(jnp.float32)
    rows = jnp.where(k < 4, 1.0, jnp.where(k < 6, high, low))
    below = (at_x > 0).astype(jnp.float32)
    above = (at_x < count_x - 1).astype(jnp.float32)
    return rows, below, above


def in_segments(lo, hi, body, masks, scale, chunk, rim=RIM, brick=BRICK_X):
    rows, below, above = masks
    inner = rows * scale
    for start, end, weight in (
        (lo, min(hi, rim), inner * below),
        (max(lo, rim), min(hi, rim + brick), inner),
        (max(lo, rim + brick), hi, inner * above),
    ):
        if end > start:
            each(start, end, functools.partial(body, weight=weight), chunk)


def fine_sweep(u_in, g_in, u_out, g_out, b_ref, margin, masks):
    def body(x, weight):
        FINE.put(u_out, g_out, x, FINE.sweep(u_in, g_in, b_ref, x, weight))

    in_segments(margin, WIDE_X - margin, body, masks, 1.0 / 30.0, 4)


def add_correction(error_of, u_in, u_out, g_out, margin):
    def body(i):
        error = error_of(i)
        for d in range(2):
            x = 2 * i + d
            plane = [
                [u_in[x, q, p] + error[q // 2][p // 2] for p in range(4)] for q in range(4)
            ]
            FINE.put(u_out, g_out, x, plane)

    each(margin // 2, (WIDE_X - margin) // 2, body, 2)


def send_residual(u_ref, g_ref, b_ref, out_ref):
    def body(i):
        x = RIM + 2 * i
        pair = add_planes(
            FINE.residual(u_ref, g_ref, b_ref, x), FINE.residual(u_ref, g_ref, b_ref, x + 1)
        )
        for q, (even, odd) in enumerate(join(pair)):
            out_ref[i, q] = 0.1 * jnp.where(row_of(even.shape) < 4, even, pltpu.roll(odd, 4, 0))

    each(0, BRICK_X // 2, body, BRICK_X // 2)


def permuted(values, places):
    shape = (values.shape[1], values.shape[1])
    row, column = (lax.broadcasted_iota(jnp.int32, shape, d) for d in range(2))
    matrix = places(row, column).astype(jnp.float32).astype(jnp.bfloat16)
    total, rest = None, values
    terms = []
    for _ in range(3):
        term = rest.astype(jnp.bfloat16)
        rest = rest - term.astype(jnp.float32)
        terms.append(jnp.dot(term, matrix, preferred_element_type=jnp.float32))
    return terms[0] + (terms[1] + terms[2])


def split_lanes(values):
    size_x, size_z, size_y = values.shape
    flat = values.reshape(size_x * size_z, size_y)
    split = permuted(flat, lambda y, l: y == (l % LANES) * 4 + l // LANES)
    return [
        split[:, p * LANES : (p + 1) * LANES].reshape(size_x, size_z, LANES) for p in range(4)
    ]


def lanes_kernel(where_ref, charges_ref, rows_ref, one_ref, two_ref):
    odd = where_ref[1] % 2
    for p, tile in enumerate(split_lanes(charges_ref[...])):
        rows_ref[:, p] = tile
        first, last = tile[:, 0:8], tile[:, 8:16]
        one_ref[:, p] = jnp.where(odd == 0, last, first)
        two_ref[:, p] = jnp.where(odd == 0, first, last)


def far_lanes_kernel(where_ref, charges_ref, rows_ref):
    for p, tile in enumerate(split_lanes(charges_ref[...])):
        rows_ref[:, p] = tile


def down_kernel(count_x, count_z, where_ref, mid_ref, mid_rim_ref, one_ref, one_rim_ref, two_ref,
                two_rim_ref, u_ref, b_ref, out_ref, c_ref, g_ref, h_ref, rows_ref):
    masks = rim_masks(count_x, count_z, where_ref)
    odd = where_ref[0] % 2

    def split_rows(ref, rim_ref, part):
        def split(x):
            for p in range(4):
                rows_ref[x, p, 0:BRICK_Z] = ref[x, p]
                rows_ref[x, p, BRICK_Z:WIDE_Z] = rim_ref[x, p]
                for q in range(4):
                    c_ref[part * BRICK_X + x, q, p] = rows_ref[x, p, pl.ds(q, 8, stride=4), :]

        each(0, BRICK_X, split, 2)

    split_rows(mid_ref, mid_rim_ref, 1)
    split_rows(one_ref, one_rim_ref, 2 - 2 * odd)
    split_rows(two_ref, two_rim_ref, 2 * odd)

    def source(x, weight):
        here = FINE.load(c_ref, x)
        sums = along_z(here, 1, True)
        plane = []
        for q in range(4):
            y_sums = along_y(here[q], 1)
            line = []
            for p in range(4):
                face = (c_ref[x - 1, q, p] + c_ref[x + 1, q, p]) + (sums[q][p] + y_sums[p])
                line.append((here[q][p] * 6.0 + face) * weight)
            plane.append(line)
        FINE.put(b_ref, g_ref, x, plane)

    in_segments(1, WIDE_X - 1, source, masks, 0.2 / 12.0, 4)

    def body(x, weight):
        FINE.put(u_ref, h_ref, x, FINE.sweep(b_ref, g_ref, b_ref, x, weight))

    in_segments(2, WIDE_X - 2, body, masks, 1.0 / 30.0, 4)
    send_residual(u_ref, h_ref, b_ref, out_ref)


def middle_kernel(count_x, count_z, count_pieces, where_ref, *refs):
    pieces, refs = refs[:count_pieces], refs[count_pieces:]
    u_ref, b_ref, v_ref, out_ref, ga_ref, gb_ref, ua_ref, *grids = refs
    masks = rim_masks(count_x, count_z, where_ref)
    coarse_solve(count_x, count_z, where_ref, pieces, grids)
    coarse_ref = coarse_finish(count_x, grids)
    at_x, at_z = where_ref[0], where_ref[1]

    def error_of(i):
        plane = LEVEL_1.load(coarse_ref, 4 * at_x + i)
        return [[turned_tile(t, at_z, masks[0]) for t in line] for line in plane]

    add_correction(error_of, u_ref, v_ref, ga_ref, 2)
    fine_sweep(v_ref, ga_ref, ua_ref, gb_ref, b_ref, 3, masks)
    fine_sweep(ua_ref, gb_ref, v_ref, ga_ref, b_ref, 4, masks)
    fine_sweep(v_ref, ga_ref, ua_ref, gb_ref, b_ref, 5, masks)
    fine_sweep(ua_ref, gb_ref, v_ref, ga_ref, b_ref, 6, masks)
    send_residual(v_ref, ga_ref, b_ref, out_ref)


def up_kernel(count_x, count_z, count_pieces, where_ref, *refs):
    pieces, refs = refs[:count_pieces], refs[count_pieces:]
    u_ref, b_ref, out_ref, ga_ref, gb_ref, ua_ref, ub_ref, rows_ref, *refs = refs
    near, grids = refs[:5], refs[5:]
    masks = rim_masks(count_x, count_z, where_ref)
    coarse = coarse_solve(count_x, count_z, where_ref, pieces, grids)
    error_ref = near_finish(coarse, where_ref, masks, near)
    add_correction(lambda i: NEAR_1.load(error_ref, i), u_ref, ua_ref, ga_ref, 6)
    fine_sweep(ua_ref, ga_ref, ub_ref, gb_ref, b_ref, 7, masks)

    def body(x):
        plane = FINE.sweep(ub_ref, gb_ref, b_ref, x, 1.0 / 30.0)
        for q in range(4):
            for p in range(4):
                rows_ref[x - RIM, p, pl.ds(q, 4, stride=4), :] = plane[q][p][0:4]

    each(RIM, RIM + BRICK_X, body, 2)
    tiles = [rows_ref[:, p].reshape(BRICK_X * BRICK_Z, LANES) for p in range(4)]
    whole = permuted(
        jnp.concatenate(tiles, axis=1), lambda l, y: y == (l % LANES) * 4 + l // LANES
    )
    out_ref[...] = whole.reshape(out_ref.shape)


def call(kernel, outputs, scratch):
    shapes = [jax.ShapeDtypeStruct(shape, jnp.float32) for shape in outputs]
    held = sum(4 * math.prod(shape.shape) for shape in scratch)

    def run(where, *arrays):
        moved = sum(4 * math.prod(array.shape) for array in arrays + tuple(shapes))
        return pl.pallas_call(
            kernel,
            out_shape=shapes,
            in_specs=[pl.BlockSpec(memory_space=pltpu.SMEM)]
            + [pl.BlockSpec(memory_space=pltpu.VMEM)] * len(arrays),
            out_specs=[pl.BlockSpec(memory_space=pltpu.VMEM)] * len(shapes),
            scratch_shapes=scratch,
            compiler_params=pltpu.CompilerParams(vmem_limit_bytes=held + moved + SPARE_BYTES),
        )(where, *arrays)

    return run


def pairs_apart(count, distance):
    return [(i, i ^ distance) for i in range(count)]


def pairs_shifted(count):
    pairs = [(i, i + 1) for i in range(1, count - 1, 2)]
    return pairs + [(target, source) for source, target in pairs]


def across(pairs_x, pairs_z, count_z):
    return [
        (x_from * count_z + z_from, x_to * count_z + z_to)
        for x_from, x_to in pairs_x
        for z_from, z_to in pairs_z
    ]


def swap(axis, values, distance):
    return lax.ppermute(values, axis, pairs_apart(lax.axis_size(axis), distance))


def every_piece(piece):
    count_x, count_z = lax.axis_size("gx"), lax.axis_size("gz")
    line = [swap("gz", piece[None], count_z - 1 - n) for n in range(count_z - 1)] + [piece[None]]
    halves = [jnp.concatenate(half) for half in (line[: count_z // 2], line[count_z // 2 :])]
    held = jnp.concatenate(halves + [swap("gx", half, 2) for half in halves])
    distance = 4
    while distance < count_x:
        held = jnp.concatenate([held, swap("gx", held, distance)])
        distance *= 2
    return held, swap("gx", held, 1)


def per_device(charges):
    count_x, count_z = lax.axis_size("gx"), lax.axis_size("gz")
    at_x, at_z = lax.axis_index("gx"), lax.axis_index("gz")
    where = jnp.stack([at_x, at_z]).astype(jnp.int32)
    brick, rim = (BRICK_X, 4, BRICK_Z, LANES), (BRICK_X, 4, RIM, LANES)
    x_far = pairs_shifted(count_x)
    (far,) = call(far_lanes_kernel, [brick], [])(where, lax.ppermute(charges, "gx", x_far))
    middle, one, two = call(lanes_kernel, [brick, rim, rim], [])(where, charges)
    z_one = pairs_apart(count_z, 1)
    z_two = pairs_shifted(count_z)
    even = at_z % 2 == 0

    def both_rims(from_one, from_two):
        after, before = jnp.where(even, from_one, from_two), jnp.where(even, from_two, from_one)
        return jnp.concatenate([after, before], axis=2)

    far_rim = both_rims(
        lax.ppermute(one, ("gx", "gz"), across(x_far, z_one, count_z)),
        lax.ppermute(two, ("gx", "gz"), across(x_far, z_two, count_z)),
    )
    middle_rim = both_rims(lax.ppermute(one, "gz", z_one), lax.ppermute(two, "gz", z_two))
    near = swap("gx", middle, 1)
    near_rim = swap("gx", middle_rim, 1)

    wide = (WIDE_X, 4, 4, 8, LANES)
    piece_shape = (BRICK_X // 2, 2, 8, LANES)
    fine = pltpu.VMEM(wide, jnp.float32)
    grids = coarse_grids(count_x, count_z)
    rows_in = pltpu.VMEM((BRICK_X, 4, WIDE_Z, LANES), jnp.float32)
    close = pltpu.VMEM((WIDE_X // 2, 2, 2, 8, LANES), jnp.float32)
    rows_out = pltpu.VMEM((BRICK_X, 4, BRICK_Z, LANES), jnp.float32)

    u, b, piece = call(
        functools.partial(down_kernel, count_x, count_z),
        [wide, wide, piece_shape],
        [fine] * 3 + [rows_in],
    )(where, middle, middle_rim, near, near_rim, far, far_rim)
    pieces = every_piece(piece)
    u, piece = call(
        functools.partial(middle_kernel, count_x, count_z, len(pieces)),
        [wide, piece_shape],
        [fine] * 3 + grids,
    )(where, *pieces, u, b)
    pieces = every_piece(piece)
    (potential,) = call(
        functools.partial(up_kernel, count_x, count_z, len(pieces)),
        [charges.shape],
        [fine] * 4 + [rows_out] + [close] * 5 + grids,
    )(where, *pieces, u, b)
    return potential


def solution(mesh):
    return jax.shard_map(
        per_device,
        mesh=mesh,
        in_specs=(P(("groups", "gx"), "gz", None),),
        out_specs=P(("groups", "gx"), "gz", None),
        check_vma=False,
    )
```

```python
import functools
import math

import jax
import jax.numpy as jnp
from jax import lax
from jax.experimental import pallas as pl
from jax.experimental.pallas import tpu as pltpu
from jax.sharding import PartitionSpec as P

COARSE_SWEEPS = 8
LANES = 128
RIM = 8
BRICK_X = 8
BRICK_Z = 16
WIDE_X = BRICK_X + 2 * RIM
WIDE_Z = BRICK_Z + 2 * RIM
SPARE_BYTES = 4 * 1024 * 1024


def lane_of(shape):
    return lax.broadcasted_iota(jnp.int32, shape, len(shape) - 1)


def row_of(shape):
    return lax.broadcasted_iota(jnp.int32, shape, len(shape) - 2)


def next_row(tile, step, cyclic):
    rows = tile.shape[0]
    moved = pltpu.roll(tile, rows - step, 0)
    return moved if cyclic else jnp.where(row_of(tile.shape) < rows - step, moved, 0.0)


def last_row(tile, step, cyclic):
    moved = pltpu.roll(tile, step, 0)
    return moved if cyclic else jnp.where(row_of(tile.shape) >= step, moved, 0.0)


def next_lane(tile, step):
    moved = pltpu.roll(tile, LANES - step, 1)
    return jnp.where(lane_of(tile.shape) < LANES - step, moved, 0.0)


def last_lane(tile, step):
    moved = pltpu.roll(tile, step, 1)
    return jnp.where(lane_of(tile.shape) >= step, moved, 0.0)


def load_plane(ref, x, count_q, count_p):
    return [[ref[x, q, p] for p in range(count_p)] for q in range(count_q)]


def store_plane(ref, x, plane):
    for q, line in enumerate(plane):
        for p, tile in enumerate(line):
            ref[x, q, p] = tile


def along_z(plane, step, cyclic):
    count_q, count_p = len(plane), len(plane[0])
    result = []
    for q in range(count_q):
        line = []
        for p in range(count_p):
            after = plane[q + 1][p] if q + 1 < count_q else next_row(plane[0][p], step, cyclic)
            before = plane[q - 1][p] if q > 0 else last_row(plane[-1][p], step, cyclic)
            line.append(after + before)
        result.append(line)
    return result


def along_y(line, step):
    count_p = len(line)
    result = []
    for p in range(count_p):
        after = line[p + 1] if p + 1 < count_p else next_lane(line[0], step)
        before = line[p - 1] if p > 0 else last_lane(line[-1], step)
        result.append(after + before)
    return result


class Level:
    def __init__(self, count_q, count_p, step, cyclic):
        self.count_q, self.count_p, self.step, self.cyclic = count_q, count_p, step, cyclic

    def load(self, ref, x):
        return load_plane(ref, x, self.count_q, self.count_p)

    def put(self, u_ref, g_ref, x, plane):
        store_plane(u_ref, x, plane)
        sums = along_z(plane, self.step, self.cyclic)
        store_plane(
            g_ref,
            x,
            [
                [s + (v + v) for s, v in zip(sum_line, line)]
                for sum_line, line in zip(sums, plane)
            ],
        )

    def spread(self, u_ref, g_ref, x, with_u):
        result = []
        for q in range(self.count_q):
            sides, both = [], []
            for p in range(self.count_p):
                here = g_ref[x, q, p]
                sides.append((u_ref[x - 1, q, p] + u_ref[x + 1, q, p]) + here)
                if with_u:
                    here = here + u_ref[x, q, p]
                both.append((g_ref[x - 1, q, p] + g_ref[x + 1, q, p]) + (here + here))
            result.append([a + b for a, b in zip(both, along_y(sides, self.step))])
        return result

    def sweep(self, u_ref, g_ref, b_ref, x, weight):
        wide = self.spread(u_ref, g_ref, x, True)
        return [
            [b_ref[x, q, p] + wide[q][p] * weight for p in range(self.count_p)]
            for q in range(self.count_q)
        ]

    def residual(self, u_ref, g_ref, b_ref, x):
        wide = self.spread(u_ref, g_ref, x, False)
        return [
            [
                b_ref[x, q, p] * 5.0 + (wide[q][p] - u_ref[x, q, p] * 28.0) * (1.0 / 6.0)
                for p in range(self.count_p)
            ]
            for q in range(self.count_q)
        ]


class Held:
    def __init__(self, rows, zero_at=()):
        self.tiles = {(x, 0, 0): jnp.zeros((rows, LANES), jnp.float32) for x in zero_at}

    def __getitem__(self, place):
        return self.tiles[place]

    def __setitem__(self, place, tile):
        self.tiles[place] = tile


def add_planes(one, other):
    return [[a + b for a, b in zip(l, m)] for l, m in zip(one, other)]


def join(plane):
    lines = [[a + b for a, b in zip(plane[q], plane[q + 1])] for q in range(0, len(plane), 2)]
    return [[line[p] + line[p + 1] for p in range(0, len(line), 2)] for line in lines]


def join_within(tile):
    rows = tile.shape[0]
    even = row_of(tile.shape) % 2 == 0
    tile = tile + jnp.where(even, pltpu.roll(tile, rows - 1, 0), pltpu.roll(tile, 1, 0))
    even = lane_of(tile.shape) % 2 == 0
    return tile + jnp.where(even, pltpu.roll(tile, LANES - 1, 1), pltpu.roll(tile, 1, 1))


def scaled(plane, factor):
    return [[tile * factor for tile in line] for line in plane]


def each(lo, hi, body, chunk):
    count = hi - lo
    whole = count // chunk
    if whole == 1:
        for x in range(lo, lo + chunk):
            body(x)
    elif whole > 1:

        def step(i, carry):
            for d in range(chunk):
                body(lo + i * chunk + d)
            return carry

        lax.fori_loop(0, whole, step, 0)
    for x in range(lo + whole * chunk, hi):
        body(x)


FINE = Level(4, 4, 1, True)
LEVEL_1 = Level(2, 2, 1, False)
NEAR_1 = Level(2, 2, 1, True)
LEVEL_2 = Level(1, 1, 1, False)
LEVEL_3 = Level(1, 1, 2, False)
PAD = RIM // 2
PAD_2 = RIM // 4


def zero_planes(ref, indices):
    for x in indices:
        ref[x] = jnp.zeros(ref.shape[1:], ref.dtype)


def coarse_grids(count_x, count_z):
    rows = count_z * BRICK_Z // 4
    shapes = []
    for planes, count in ((4 * count_x + 2 * PAD, 2), (2 * count_x + 2 * PAD_2, 1)):
        shapes += [pltpu.VMEM((planes, count, count, rows, LANES), jnp.float32)] * 5
    return shapes


def coarse_solve(count_x, count_z, where_ref, pieces, grids):
    ua1, ub1, ga1, gb1, b1 = grids[0:5]
    kept_2 = grids[5]
    size_1, size_2, size_3 = 4 * count_x, 2 * count_x, count_x
    rows = b1.shape[3]

    def ends(pad, size):
        return list(range(pad)) + list(range(pad + size, pad + size + pad))

    for ref in (ua1, ub1, ga1, gb1, b1):
        zero_planes(ref, ends(PAD, size_1))
    zero_planes(kept_2, ends(PAD_2, size_2))
    if size_2 <= 8:
        step_2 = size_2
        ua2, ub2, ga2, gb2, b2 = (Held(rows, ends(PAD_2, size_2)) for _ in range(5))
    else:
        step_2 = 8
        ua2, ub2, ga2, gb2, b2 = grids[5:10]
        for ref in (ub2, ga2, gb2):
            zero_planes(ref, ends(PAD_2, size_2))
    ua3, ub3, ga3, gb3, b3 = (Held(rows, ends(1, size_3)) for _ in range(5))
    third = 1.0 / 30.0

    at_x, at_z = where_ref[0], where_ref[1]

    def place(x, load):
        for i in range(4):
            plane = []
            for q in range(2):
                even, odd = [], []
                for z in range(0, count_z, 2):
                    one, two = load(z, i, q), load(z + 1, i, q)
                    first = row_of(one.shape) < 4
                    even.append(jnp.where(first, one, pltpu.roll(two, 4, 0)))
                    odd.append(jnp.where(first, pltpu.roll(one, 4, 0), two))
                plane.append([jnp.concatenate(even, axis=0), jnp.concatenate(odd, axis=0)])
            LEVEL_1.put(b1, gb1, x + i, plane)

    if len(pieces) == 1:

        def gather(n):
            place(PAD + 4 * n, lambda z, i, q: pieces[0][n * count_z + z, i, q])

        each(0, count_x, gather, 1)
    else:

        def gather(n):
            for core in range(2):
                x = PAD + 4 * ((2 * n + core) ^ at_x)
                place(x, lambda z, i, q: pieces[core][n * count_z + (z ^ at_z ^ (count_z - 1)), i, q])

        each(0, count_x // 2, gather, 1)

    def sweep(level, u_in, g_in, u_out, g_out, b):
        return lambda x: level.put(u_out, g_out, x, level.sweep(u_in, g_in, b, x, third))

    each(PAD, PAD + size_1, sweep(LEVEL_1, b1, gb1, ua1, ga1, b1), 16)

    def restrict_1(x):
        fine = PAD + 2 * x
        pair = add_planes(
            LEVEL_1.residual(ua1, ga1, b1, fine), LEVEL_1.residual(ua1, ga1, b1, fine + 1)
        )
        plane = scaled(join(pair), 0.5 * 0.2)
        store_plane(b2, PAD_2 + x, plane)
        LEVEL_2.put(ub2, gb2, PAD_2 + x, plane)

    each(0, size_2, restrict_1, step_2)
    all_2 = (PAD_2, PAD_2 + size_2)
    each(*all_2, sweep(LEVEL_2, ub2, gb2, ua2, ga2, b2), step_2)

    def restrict_2(x):
        fine = PAD_2 + 2 * x
        pair = add_planes(
            LEVEL_2.residual(ua2, ga2, b2, fine), LEVEL_2.residual(ua2, ga2, b2, fine + 1)
        )
        plane = [[join_within(pair[0][0]) * (0.5 * 0.2)]]
        store_plane(b3, 1 + x, plane)
        LEVEL_3.put(ub3, gb3, 1 + x, plane)

    each(0, size_3, restrict_2, size_3)
    now, later = (ub3, gb3), (ua3, ga3)
    for _ in range(COARSE_SWEEPS - 1):
        each(1, 1 + size_3, sweep(LEVEL_3, *now, *later, b3), size_3)
        now, later = later, now

    def prolong_3(x):
        for d in range(2):
            fine = PAD_2 + 2 * x + d
            LEVEL_2.put(ua2, ga2, fine, [[ua2[fine, 0, 0] + now[0][1 + x, 0, 0]]])

    each(0, size_3, prolong_3, size_3)
    each(*all_2, sweep(LEVEL_2, ua2, ga2, ub2, gb2, b2), step_2)

    def last_sweep(x):
        store_plane(kept_2, x, LEVEL_2.sweep(ub2, gb2, b2, x, third))

    each(*all_2, last_sweep, step_2)
    return ua1, kept_2, b1


def coarse_finish(count_x, grids):
    ua1, ub1, ga1, gb1, b1 = grids[0:5]
    ua2 = grids[5]
    size_1, size_2 = 4 * count_x, 2 * count_x

    def prolong_2(x):
        error = ua2[PAD_2 + x, 0, 0]
        for d in range(2):
            fine = PAD + 2 * x + d
            LEVEL_1.put(
                ua1, ga1, fine, [[t + error for t in line] for line in LEVEL_1.load(ua1, fine)]
            )

    def sweep(u_in, g_in, u_out, g_out):
        return lambda x: LEVEL_1.put(
            u_out, g_out, x, LEVEL_1.sweep(u_in, g_in, b1, x, 1.0 / 30.0)
        )

    each(0, size_2, prolong_2, 8)
    each(PAD, PAD + size_1, sweep(ua1, ga1, ub1, gb1), 16)

    def last_sweep(x):
        store_plane(ua1, x, LEVEL_1.sweep(ub1, gb1, b1, x, 1.0 / 30.0))

    each(PAD, PAD + size_1, last_sweep, 16)
    return ua1


def turned_tile(tile, at_z, rows):
    count = tile.shape[0]
    turned = pltpu.roll(tile, lax.rem(count - 4 * at_z, count), 0)
    return jnp.where(row_of((8, LANES)) < 6, turned[0:8], turned[count - 8 : count]) * rows


def near_finish(coarse, where_ref, masks, near):
    ua1, ua2, b1 = coarse
    ua, ga, ub, gb, b = near
    at_x, at_z = where_ref[0], where_ref[1]
    rows = masks[0]

    def take(i):
        error = ua2[2 * at_x + i // 2, 0, 0]
        plane = [[t + error for t in line] for line in LEVEL_1.load(ua1, 4 * at_x + i)]
        plane = [[turned_tile(t, at_z, rows) for t in line] for line in plane]
        NEAR_1.put(ua, ga, i, plane)
        plane = LEVEL_1.load(b1, 4 * at_x + i)
        store_plane(b, i, [[turned_tile(t, at_z, rows) for t in line] for line in plane])

    each(1, 11, take, 5)

    def sweep(i, weight):
        NEAR_1.put(ub, gb, i, NEAR_1.sweep(ua, ga, b, i, weight))

    def last_sweep(i, weight):
        store_plane(ua, i, NEAR_1.sweep(ub, gb, b, i, weight))

    in_segments(2, 10, sweep, masks, 1.0 / 30.0, 4, PAD, BRICK_X // 2)
    in_segments(3, 9, last_sweep, masks, 1.0 / 30.0, 4, PAD, BRICK_X // 2)
    return ua


def rim_masks(count_x, count_z, where_ref):
    at_x, at_z = where_ref[0], where_ref[1]
    k = row_of((8, LANES))
    low = (at_z > 0).astype(jnp.float32)
    high = (at_z < count_z - 1).astype(jnp.float32)
    rows = jnp.where(k < 4, 1.0, jnp.where(k < 6, high, low))
    below = (at_x > 0).astype(jnp.float32)
    above = (at_x < count_x - 1).astype(jnp.float32)
    return rows, below, above


def in_segments(lo, hi, body, masks, scale, chunk, rim=RIM, brick=BRICK_X):
    rows, below, above = masks
    inner = rows * scale
    for start, end, weight in (
        (lo, min(hi, rim), inner * below),
        (max(lo, rim), min(hi, rim + brick), inner),
        (max(lo, rim + brick), hi, inner * above),
    ):
        if end > start:
            each(start, end, functools.partial(body, weight=weight), chunk)


def fine_sweep(u_in, g_in, u_out, g_out, b_ref, margin, masks):
    def body(x, weight):
        FINE.put(u_out, g_out, x, FINE.sweep(u_in, g_in, b_ref, x, weight))

    in_segments(margin, WIDE_X - margin, body, masks, 1.0 / 30.0, 4)


def add_correction(error_of, u_in, u_out, g_out, margin):
    def body(i):
        error = error_of(i)
        for d in range(2):
            x = 2 * i + d
            plane = [
                [u_in[x, q, p] + error[q // 2][p // 2] for p in range(4)] for q in range(4)
            ]
            FINE.put(u_out, g_out, x, plane)

    each(margin // 2, (WIDE_X - margin) // 2, body, 2)


def send_residual(u_ref, g_ref, b_ref, out_ref):
    def body(i):
        x = RIM + 2 * i
        pair = add_planes(
            FINE.residual(u_ref, g_ref, b_ref, x), FINE.residual(u_ref, g_ref, b_ref, x + 1)
        )
        for q, (even, odd) in enumerate(join(pair)):
            out_ref[i, q] = 0.1 * jnp.where(row_of(even.shape) < 4, even, pltpu.roll(odd, 4, 0))

    each(0, BRICK_X // 2, body, BRICK_X // 2)


def places(size, joins):
    row, column = (lax.broadcasted_iota(jnp.int32, (size, size), d) for d in range(2))
    return joins(row, column).astype(jnp.float32).astype(jnp.bfloat16)


def permuted(values, matrix):
    rest, terms = values, []
    for _ in range(3):
        term = rest.astype(jnp.bfloat16)
        rest = rest - term.astype(jnp.float32)
        terms.append(jnp.dot(term, matrix, preferred_element_type=jnp.float32))
    return terms[0] + (terms[1] + terms[2])


def lanes_kernel(where_ref, charges_ref, rows_ref, one_ref, two_ref):
    odd = where_ref[1] % 2
    width = charges_ref.shape[2]
    matrix = places(width, lambda y, l: y == (l % LANES) * 4 + l // LANES)
    split = permuted(charges_ref[...].reshape(BRICK_X * BRICK_Z, width), matrix)
    for p in range(4):
        tile = split[:, p * LANES : (p + 1) * LANES].reshape(BRICK_X, BRICK_Z, LANES)
        rows_ref[:, p] = tile
        first, last = tile[:, 0:8], tile[:, 8:16]
        one_ref[:, p] = jnp.where(odd == 0, last, first)
        two_ref[:, p] = jnp.where(odd == 0, first, last)


def down_kernel(count_x, count_z, where_ref, mid_ref, mid_rim_ref, one_ref, one_rim_ref, two_ref,
                two_rim_ref, u_ref, b_ref, out_ref, c_ref, g_ref, h_ref, rows_ref):
    masks = rim_masks(count_x, count_z, where_ref)
    odd = where_ref[0] % 2

    def split_rows(ref, rim_ref, part):
        def split(x):
            for p in range(4):
                rows_ref[x, p, 0:BRICK_Z] = ref[x, p]
                rows_ref[x, p, BRICK_Z:WIDE_Z] = rim_ref[x, p]
                for q in range(4):
                    c_ref[part * BRICK_X + x, q, p] = rows_ref[x, p, pl.ds(q, 8, stride=4), :]

        each(0, BRICK_X, split, 2)

    split_rows(mid_ref, mid_rim_ref, 1)
    split_rows(one_ref, one_rim_ref, 2 - 2 * odd)
    split_rows(two_ref, two_rim_ref, 2 * odd)

    def source(x, weight):
        here = FINE.load(c_ref, x)
        sums = along_z(here, 1, True)
        plane = []
        for q in range(4):
            y_sums = along_y(here[q], 1)
            line = []
            for p in range(4):
                face = (c_ref[x - 1, q, p] + c_ref[x + 1, q, p]) + (sums[q][p] + y_sums[p])
                line.append((here[q][p] * 6.0 + face) * weight)
            plane.append(line)
        FINE.put(b_ref, g_ref, x, plane)

    in_segments(1, WIDE_X - 1, source, masks, 0.2 / 12.0, 4)

    def body(x, weight):
        FINE.put(u_ref, h_ref, x, FINE.sweep(b_ref, g_ref, b_ref, x, weight))

    in_segments(2, WIDE_X - 2, body, masks, 1.0 / 30.0, 4)
    send_residual(u_ref, h_ref, b_ref, out_ref)


def middle_kernel(count_x, count_z, count_pieces, where_ref, *refs):
    pieces, refs = refs[:count_pieces], refs[count_pieces:]
    u_ref, b_ref, v_ref, out_ref, ga_ref, gb_ref, ua_ref, *grids = refs
    masks = rim_masks(count_x, count_z, where_ref)
    coarse_solve(count_x, count_z, where_ref, pieces, grids)
    coarse_ref = coarse_finish(count_x, grids)
    at_x, at_z = where_ref[0], where_ref[1]

    def error_of(i):
        plane = LEVEL_1.load(coarse_ref, 4 * at_x + i)
        return [[turned_tile(t, at_z, masks[0]) for t in line] for line in plane]

    add_correction(error_of, u_ref, v_ref, ga_ref, 2)
    fine_sweep(v_ref, ga_ref, ua_ref, gb_ref, b_ref, 3, masks)
    fine_sweep(ua_ref, gb_ref, v_ref, ga_ref, b_ref, 4, masks)
    fine_sweep(v_ref, ga_ref, ua_ref, gb_ref, b_ref, 5, masks)
    fine_sweep(ua_ref, gb_ref, v_ref, ga_ref, b_ref, 6, masks)
    send_residual(v_ref, ga_ref, b_ref, out_ref)


def up_kernel(count_x, count_z, count_pieces, where_ref, *refs):
    pieces, refs = refs[:count_pieces], refs[count_pieces:]
    u_ref, b_ref, out_ref, ga_ref, gb_ref, ua_ref, ub_ref, rows_ref, held_ref, semaphores, *refs = refs
    near, grids = refs[:5], refs[5:]
    masks = rim_masks(count_x, count_z, where_ref)
    coarse = coarse_solve(count_x, count_z, where_ref, pieces, grids)
    error_ref = near_finish(coarse, where_ref, masks, near)
    add_correction(lambda i: NEAR_1.load(error_ref, i), u_ref, ua_ref, ga_ref, 6)
    fine_sweep(ua_ref, ga_ref, ub_ref, gb_ref, b_ref, 7, masks)

    def body(x):
        plane = FINE.sweep(ub_ref, gb_ref, b_ref, x, 1.0 / 30.0)
        for q in range(4):
            for p in range(4):
                rows_ref[x - RIM, p, pl.ds(q, 4, stride=4), :] = plane[q][p][0:4]

    width = out_ref.shape[2]
    matrix = places(width, lambda l, y: y == (l % LANES) * 4 + l // LANES)
    half = BRICK_X // 2
    copies = []
    for start in (0, half):
        each(RIM + start, RIM + start + half, body, 2)
        tiles = [
            rows_ref[start : start + half, p].reshape(half * BRICK_Z, LANES) for p in range(4)
        ]
        whole = permuted(jnp.concatenate(tiles, axis=1), matrix)
        planes = pl.ds(start, half)
        held_ref[planes] = whole.reshape(half, BRICK_Z, width)
        copies.append(
            pltpu.make_async_copy(
                held_ref.at[planes], out_ref.at[planes], semaphores.at[start // half]
            )
        )
        copies[-1].start()
    for copy in copies:
        copy.wait()


def call(kernel, outputs, scratch, far_out=False):
    shapes = [jax.ShapeDtypeStruct(shape, jnp.float32) for shape in outputs]
    held = sum(4 * math.prod(shape.shape) for shape in scratch if hasattr(shape, "memory_space"))

    def run(where, *arrays):
        moved = sum(4 * math.prod(array.shape) for array in arrays + tuple(shapes))
        inside = pl.BlockSpec(memory_space=pltpu.VMEM)
        outside = pl.BlockSpec(memory_space=pltpu.HBM if far_out else pltpu.VMEM)
        return pl.pallas_call(
            kernel,
            out_shape=shapes,
            in_specs=[pl.BlockSpec(memory_space=pltpu.SMEM)] + [inside] * len(arrays),
            out_specs=[outside] * len(shapes),
            scratch_shapes=scratch,
            compiler_params=pltpu.CompilerParams(vmem_limit_bytes=held + moved + SPARE_BYTES),
        )(where, *arrays)

    return run


def pairs_apart(count, distance):
    return [(i, i ^ distance) for i in range(count)]


def pairs_shifted(count):
    pairs = [(i, i + 1) for i in range(1, count - 1, 2)]
    return pairs + [(target, source) for source, target in pairs]


def swap(axis, values, distance):
    return lax.ppermute(values, axis, pairs_apart(lax.axis_size(axis), distance))


def every_piece(piece):
    count_x, count_z = lax.axis_size("gx"), lax.axis_size("gz")
    line = [swap("gz", piece[None], count_z - 1 - n) for n in range(count_z - 1)] + [piece[None]]
    halves = [jnp.concatenate(half) for half in (line[: count_z // 2], line[count_z // 2 :])]
    held = jnp.concatenate(halves + [swap("gx", half, 2) for half in halves])
    distance = 4
    while distance < count_x:
        held = jnp.concatenate([held, swap("gx", held, distance)])
        distance *= 2
    return held, swap("gx", held, 1)


def per_device(charges):
    count_x, count_z = lax.axis_size("gx"), lax.axis_size("gz")
    at_x, at_z = lax.axis_index("gx"), lax.axis_index("gz")
    where = jnp.stack([at_x, at_z]).astype(jnp.int32)
    brick, rim = (BRICK_X, 4, BRICK_Z, LANES), (BRICK_X, 4, RIM, LANES)
    held = pltpu.VMEM(charges.shape, jnp.float32)
    middle, one, two = call(lanes_kernel, [brick, rim, rim], [])(where, charges)
    x_far, z_two = pairs_shifted(count_x), pairs_shifted(count_z)
    far = lax.ppermute(middle, "gx", x_far)
    near = swap("gx", middle, 1)
    one, two = swap("gz", one, 1), lax.ppermute(two, "gz", z_two)
    even = at_z % 2 == 0
    middle_rim = jnp.concatenate([jnp.where(even, one, two), jnp.where(even, two, one)], axis=2)
    far_rim = lax.ppermute(middle_rim, "gx", x_far)
    near_rim = swap("gx", middle_rim, 1)

    wide = (WIDE_X, 4, 4, 8, LANES)
    piece_shape = (BRICK_X // 2, 2, 8, LANES)
    fine = pltpu.VMEM(wide, jnp.float32)
    grids = coarse_grids(count_x, count_z)
    rows_in = pltpu.VMEM((BRICK_X, 4, WIDE_Z, LANES), jnp.float32)
    close = pltpu.VMEM((WIDE_X // 2, 2, 2, 8, LANES), jnp.float32)
    rows_out = pltpu.VMEM((BRICK_X, 4, BRICK_Z, LANES), jnp.float32)

    u, b, piece = call(
        functools.partial(down_kernel, count_x, count_z),
        [wide, wide, piece_shape],
        [fine] * 3 + [rows_in],
    )(where, middle, middle_rim, near, near_rim, far, far_rim)
    pieces = every_piece(piece)
    u, piece = call(
        functools.partial(middle_kernel, count_x, count_z, len(pieces)),
        [wide, piece_shape],
        [fine] * 3 + grids,
    )(where, *pieces, u, b)
    pieces = every_piece(piece)
    (potential,) = call(
        functools.partial(up_kernel, count_x, count_z, len(pieces)),
        [charges.shape],
        [fine] * 4 + [rows_out, held, pltpu.SemaphoreType.DMA((2,))] + [close] * 5 + grids,
        far_out=True,
    )(where, *pieces, u, b)
    return potential


def solution(mesh):
    return jax.shard_map(
        per_device,
        mesh=mesh,
        in_specs=(P(("groups", "gx"), "gz", None),),
        out_specs=P(("groups", "gx"), "gz", None),
        check_vma=False,
    )
```

```python
import functools
import math

import jax
import jax.numpy as jnp
from jax import lax
from jax.experimental import pallas as pl
from jax.experimental.pallas import tpu as pltpu
from jax.sharding import PartitionSpec as P

COARSE_SWEEPS = 8
LANES = 128
RIM = 8
BRICK_X = 8
BRICK_Z = 16
WIDE_X = BRICK_X + 2 * RIM
WIDE_Z = BRICK_Z + 2 * RIM
SPARE_BYTES = 4 * 1024 * 1024


def lane_of(shape):
    return lax.broadcasted_iota(jnp.int32, shape, len(shape) - 1)


def row_of(shape):
    return lax.broadcasted_iota(jnp.int32, shape, len(shape) - 2)


def next_row(tile, step, cyclic):
    rows = tile.shape[0]
    moved = pltpu.roll(tile, rows - step, 0)
    return moved if cyclic else jnp.where(row_of(tile.shape) < rows - step, moved, 0.0)


def last_row(tile, step, cyclic):
    moved = pltpu.roll(tile, step, 0)
    return moved if cyclic else jnp.where(row_of(tile.shape) >= step, moved, 0.0)


def next_lane(tile, step):
    moved = pltpu.roll(tile, LANES - step, 1)
    return jnp.where(lane_of(tile.shape) < LANES - step, moved, 0.0)


def last_lane(tile, step):
    moved = pltpu.roll(tile, step, 1)
    return jnp.where(lane_of(tile.shape) >= step, moved, 0.0)


def load_plane(ref, x, count_q, count_p):
    return [[ref[x, q, p] for p in range(count_p)] for q in range(count_q)]


def store_plane(ref, x, plane):
    for q, line in enumerate(plane):
        for p, tile in enumerate(line):
            ref[x, q, p] = tile


def along_z(plane, step, cyclic):
    count_q, count_p = len(plane), len(plane[0])
    result = []
    for q in range(count_q):
        line = []
        for p in range(count_p):
            after = plane[q + 1][p] if q + 1 < count_q else next_row(plane[0][p], step, cyclic)
            before = plane[q - 1][p] if q > 0 else last_row(plane[-1][p], step, cyclic)
            line.append(after + before)
        result.append(line)
    return result


def along_y(line, step):
    count_p = len(line)
    result = []
    for p in range(count_p):
        after = line[p + 1] if p + 1 < count_p else next_lane(line[0], step)
        before = line[p - 1] if p > 0 else last_lane(line[-1], step)
        result.append(after + before)
    return result


class Level:
    def __init__(self, count_q, count_p, step, cyclic):
        self.count_q, self.count_p, self.step, self.cyclic = count_q, count_p, step, cyclic

    def load(self, ref, x):
        return load_plane(ref, x, self.count_q, self.count_p)

    def put(self, u_ref, g_ref, x, plane):
        store_plane(u_ref, x, plane)
        sums = along_z(plane, self.step, self.cyclic)
        store_plane(
            g_ref,
            x,
            [
                [s + (v + v) for s, v in zip(sum_line, line)]
                for sum_line, line in zip(sums, plane)
            ],
        )

    def spread(self, u_ref, g_ref, x, with_u):
        result = []
        for q in range(self.count_q):
            sides, both = [], []
            for p in range(self.count_p):
                here = g_ref[x, q, p]
                sides.append((u_ref[x - 1, q, p] + u_ref[x + 1, q, p]) + here)
                if with_u:
                    here = here + u_ref[x, q, p]
                both.append((g_ref[x - 1, q, p] + g_ref[x + 1, q, p]) + (here + here))
            result.append([a + b for a, b in zip(both, along_y(sides, self.step))])
        return result

    def sweep(self, u_ref, g_ref, b_ref, x, weight):
        wide = self.spread(u_ref, g_ref, x, True)
        return [
            [b_ref[x, q, p] + wide[q][p] * weight for p in range(self.count_p)]
            for q in range(self.count_q)
        ]

    def residual(self, u_ref, g_ref, b_ref, x):
        wide = self.spread(u_ref, g_ref, x, False)
        return [
            [
                b_ref[x, q, p] * 5.0 + (wide[q][p] - u_ref[x, q, p] * 28.0) * (1.0 / 6.0)
                for p in range(self.count_p)
            ]
            for q in range(self.count_q)
        ]


class Held:
    def __init__(self, rows, zero_at=()):
        self.tiles = {(x, 0, 0): jnp.zeros((rows, LANES), jnp.float32) for x in zero_at}

    def __getitem__(self, place):
        return self.tiles[place]

    def __setitem__(self, place, tile):
        self.tiles[place] = tile


def add_planes(one, other):
    return [[a + b for a, b in zip(l, m)] for l, m in zip(one, other)]


def join(plane):
    lines = [[a + b for a, b in zip(plane[q], plane[q + 1])] for q in range(0, len(plane), 2)]
    return [[line[p] + line[p + 1] for p in range(0, len(line), 2)] for line in lines]


def join_within(tile):
    rows = tile.shape[0]
    even = row_of(tile.shape) % 2 == 0
    tile = tile + jnp.where(even, pltpu.roll(tile, rows - 1, 0), pltpu.roll(tile, 1, 0))
    even = lane_of(tile.shape) % 2 == 0
    return tile + jnp.where(even, pltpu.roll(tile, LANES - 1, 1), pltpu.roll(tile, 1, 1))


def scaled(plane, factor):
    return [[tile * factor for tile in line] for line in plane]


def each(lo, hi, body, chunk):
    count = hi - lo
    whole = count // chunk
    if whole == 1:
        for x in range(lo, lo + chunk):
            body(x)
    elif whole > 1:

        def step(i, carry):
            for d in range(chunk):
                body(lo + i * chunk + d)
            return carry

        lax.fori_loop(0, whole, step, 0)
    for x in range(lo + whole * chunk, hi):
        body(x)


FINE = Level(4, 4, 1, True)
LEVEL_1 = Level(2, 2, 1, False)
NEAR_1 = Level(2, 2, 1, True)
LEVEL_2 = Level(1, 1, 1, False)
LEVEL_3 = Level(1, 1, 2, False)
PAD = RIM // 2
PAD_2 = RIM // 4


def zero_planes(ref, indices):
    for x in indices:
        ref[x] = jnp.zeros(ref.shape[1:], ref.dtype)


def coarse_grids(count_x, count_z):
    rows = count_z * BRICK_Z // 4
    shapes = []
    for planes, count in ((4 * count_x + 2 * PAD, 2), (2 * count_x + 2 * PAD_2, 1)):
        shapes += [pltpu.VMEM((planes, count, count, rows, LANES), jnp.float32)] * 5
    return shapes


def coarse_solve(count_x, count_z, where_ref, pieces, grids):
    ua1, ub1, ga1, gb1, b1 = grids[0:5]
    kept_2 = grids[5]
    size_1, size_2, size_3 = 4 * count_x, 2 * count_x, count_x
    rows = b1.shape[3]

    def ends(pad, size):
        return list(range(pad)) + list(range(pad + size, pad + size + pad))

    for ref in (ua1, ub1, ga1, gb1, b1):
        zero_planes(ref, ends(PAD, size_1))
    zero_planes(kept_2, ends(PAD_2, size_2))
    if size_2 <= 8:
        step_2 = size_2
        ua2, ub2, ga2, gb2, b2 = (Held(rows, ends(PAD_2, size_2)) for _ in range(5))
    else:
        step_2 = 8
        ua2, ub2, ga2, gb2, b2 = grids[5:10]
        for ref in (ub2, ga2, gb2):
            zero_planes(ref, ends(PAD_2, size_2))
    ua3, ub3, ga3, gb3, b3 = (Held(rows, ends(1, size_3)) for _ in range(5))
    third = 1.0 / 30.0

    at_x, at_z = where_ref[0], where_ref[1]

    def place(x, load):
        for i in range(4):
            plane = []
            for q in range(2):
                even, odd = [], []
                for z in range(0, count_z, 2):
                    one, two = load(z, i, q), load(z + 1, i, q)
                    first = row_of(one.shape) < 4
                    even.append(jnp.where(first, one, pltpu.roll(two, 4, 0)))
                    odd.append(jnp.where(first, pltpu.roll(one, 4, 0), two))
                plane.append([jnp.concatenate(even, axis=0), jnp.concatenate(odd, axis=0)])
            LEVEL_1.put(b1, gb1, x + i, plane)

    if len(pieces) == 1:

        def gather(n):
            place(PAD + 4 * n, lambda z, i, q: pieces[0][n * count_z + z, i, q])

        each(0, count_x, gather, 1)
    else:

        def gather(n):
            for core in range(2):
                x = PAD + 4 * ((2 * n + core) ^ at_x)
                place(x, lambda z, i, q: pieces[core][n * count_z + (z ^ at_z ^ (count_z - 1)), i, q])

        each(0, count_x // 2, gather, 1)

    def sweep(level, u_in, g_in, u_out, g_out, b):
        return lambda x: level.put(u_out, g_out, x, level.sweep(u_in, g_in, b, x, third))

    each(PAD, PAD + size_1, sweep(LEVEL_1, b1, gb1, ua1, ga1, b1), 16)

    def restrict_1(x):
        fine = PAD + 2 * x
        pair = add_planes(
            LEVEL_1.residual(ua1, ga1, b1, fine), LEVEL_1.residual(ua1, ga1, b1, fine + 1)
        )
        plane = scaled(join(pair), 0.5 * 0.2)
        store_plane(b2, PAD_2 + x, plane)
        LEVEL_2.put(ub2, gb2, PAD_2 + x, plane)

    each(0, size_2, restrict_1, step_2)
    all_2 = (PAD_2, PAD_2 + size_2)
    each(*all_2, sweep(LEVEL_2, ub2, gb2, ua2, ga2, b2), step_2)

    def restrict_2(x):
        fine = PAD_2 + 2 * x
        pair = add_planes(
            LEVEL_2.residual(ua2, ga2, b2, fine), LEVEL_2.residual(ua2, ga2, b2, fine + 1)
        )
        plane = [[join_within(pair[0][0]) * (0.5 * 0.2)]]
        store_plane(b3, 1 + x, plane)
        LEVEL_3.put(ub3, gb3, 1 + x, plane)

    each(0, size_3, restrict_2, size_3)
    now, later = (ub3, gb3), (ua3, ga3)
    for _ in range(COARSE_SWEEPS - 1):
        each(1, 1 + size_3, sweep(LEVEL_3, *now, *later, b3), size_3)
        now, later = later, now

    def prolong_3(x):
        for d in range(2):
            fine = PAD_2 + 2 * x + d
            LEVEL_2.put(ua2, ga2, fine, [[ua2[fine, 0, 0] + now[0][1 + x, 0, 0]]])

    each(0, size_3, prolong_3, size_3)
    each(*all_2, sweep(LEVEL_2, ua2, ga2, ub2, gb2, b2), step_2)

    def last_sweep(x):
        store_plane(kept_2, x, LEVEL_2.sweep(ub2, gb2, b2, x, third))

    each(*all_2, last_sweep, step_2)
    return ua1, kept_2, b1


def coarse_finish(count_x, where_ref, grids):
    ua1, ub1, ga1, gb1, b1 = grids[0:5]
    ua2 = grids[5]
    size_1, size_2 = 4 * count_x, 2 * count_x
    third = 1.0 / 30.0

    def prolong_2(x):
        error = ua2[PAD_2 + x, 0, 0]
        for d in range(2):
            fine = PAD + 2 * x + d
            LEVEL_1.put(
                ua1, ga1, fine, [[t + error for t in line] for line in LEVEL_1.load(ua1, fine)]
            )

    def window(rim):
        count = min(BRICK_X // 2 + 2 * rim, size_1)
        return PAD + jnp.clip(4 * where_ref[0] - rim, 0, size_1 - count), count

    start, count = window(4)

    def sweep(i):
        x = start + i
        LEVEL_1.put(ub1, gb1, x, LEVEL_1.sweep(ua1, ga1, b1, x, third))

    last_start, last_count = window(3)

    def last_sweep(i):
        x = last_start + i
        store_plane(ua1, x, LEVEL_1.sweep(ub1, gb1, b1, x, third))

    each(0, size_2, prolong_2, 8)
    each(0, count, sweep, 12)
    each(0, last_count, last_sweep, 10)
    return ua1


def turned_tile(tile, at_z, rows):
    count = tile.shape[0]
    turned = pltpu.roll(tile, lax.rem(count - 4 * at_z, count), 0)
    return jnp.where(row_of((8, LANES)) < 6, turned[0:8], turned[count - 8 : count]) * rows


def near_finish(coarse, where_ref, masks, near):
    ua1, ua2, b1 = coarse
    ua, ga, ub, gb, b = near
    at_x, at_z = where_ref[0], where_ref[1]
    rows = masks[0]

    def take(i):
        error = ua2[2 * at_x + i // 2, 0, 0]
        plane = [[t + error for t in line] for line in LEVEL_1.load(ua1, 4 * at_x + i)]
        plane = [[turned_tile(t, at_z, rows) for t in line] for line in plane]
        NEAR_1.put(ua, ga, i, plane)
        plane = LEVEL_1.load(b1, 4 * at_x + i)
        store_plane(b, i, [[turned_tile(t, at_z, rows) for t in line] for line in plane])

    each(1, 11, take, 5)

    def sweep(i, weight):
        NEAR_1.put(ub, gb, i, NEAR_1.sweep(ua, ga, b, i, weight))

    def last_sweep(i, weight):
        store_plane(ua, i, NEAR_1.sweep(ub, gb, b, i, weight))

    in_segments(2, 10, sweep, masks, 1.0 / 30.0, 4, PAD, BRICK_X // 2)
    in_segments(3, 9, last_sweep, masks, 1.0 / 30.0, 4, PAD, BRICK_X // 2)
    return ua


def rim_masks(count_x, count_z, where_ref):
    at_x, at_z = where_ref[0], where_ref[1]
    k = row_of((8, LANES))
    low = (at_z > 0).astype(jnp.float32)
    high = (at_z < count_z - 1).astype(jnp.float32)
    rows = jnp.where(k < 4, 1.0, jnp.where(k < 6, high, low))
    below = (at_x > 0).astype(jnp.float32)
    above = (at_x < count_x - 1).astype(jnp.float32)
    return rows, below, above


def in_segments(lo, hi, body, masks, scale, chunk, rim=RIM, brick=BRICK_X):
    rows, below, above = masks
    inner = rows * scale
    for start, end, weight in (
        (lo, min(hi, rim), inner * below),
        (max(lo, rim), min(hi, rim + brick), inner),
        (max(lo, rim + brick), hi, inner * above),
    ):
        if end > start:
            each(start, end, functools.partial(body, weight=weight), chunk)


def fine_sweep(u_in, g_in, u_out, g_out, b_ref, margin, masks):
    def body(x, weight):
        FINE.put(u_out, g_out, x, FINE.sweep(u_in, g_in, b_ref, x, weight))

    in_segments(margin, WIDE_X - margin, body, masks, 1.0 / 30.0, 4)


def add_correction(error_of, u_in, u_out, g_out, margin):
    def body(i):
        error = error_of(i)
        for d in range(2):
            x = 2 * i + d
            plane = [
                [u_in[x, q, p] + error[q // 2][p // 2] for p in range(4)] for q in range(4)
            ]
            FINE.put(u_out, g_out, x, plane)

    each(margin // 2, (WIDE_X - margin) // 2, body, 2)


def send_residual(u_ref, g_ref, b_ref, out_ref):
    def body(i):
        x = RIM + 2 * i
        pair = add_planes(
            FINE.residual(u_ref, g_ref, b_ref, x), FINE.residual(u_ref, g_ref, b_ref, x + 1)
        )
        for q, (even, odd) in enumerate(join(pair)):
            out_ref[i, q] = 0.1 * jnp.where(row_of(even.shape) < 4, even, pltpu.roll(odd, 4, 0))

    each(0, BRICK_X // 2, body, BRICK_X // 2)


def places(size, joins):
    row, column = (lax.broadcasted_iota(jnp.int32, (size, size), d) for d in range(2))
    return joins(row, column).astype(jnp.float32).astype(jnp.bfloat16)


def permuted(values, matrix):
    rest, terms = values, []
    for _ in range(3):
        term = rest.astype(jnp.bfloat16)
        rest = rest - term.astype(jnp.float32)
        terms.append(jnp.dot(term, matrix, preferred_element_type=jnp.float32))
    return terms[0] + (terms[1] + terms[2])


def split_lanes(values):
    size_x, size_z, size_y = values.shape
    matrix = places(size_y, lambda y, l: y == (l % LANES) * 4 + l // LANES)
    split = permuted(values.reshape(size_x * size_z, size_y), matrix)
    return [
        split[:, p * LANES : (p + 1) * LANES].reshape(size_x, size_z, LANES) for p in range(4)
    ]


def lanes_kernel(where_ref, charges_ref, rows_ref, one_ref, two_ref):
    odd = where_ref[1] % 2
    for p, tile in enumerate(split_lanes(charges_ref[...])):
        rows_ref[:, p] = tile
        first, last = tile[:, 0:8], tile[:, 8:16]
        one_ref[:, p] = jnp.where(odd == 0, last, first)
        two_ref[:, p] = jnp.where(odd == 0, first, last)


def near_lanes_kernel(where_ref, charges_ref, rows_ref):
    for p, tile in enumerate(split_lanes(charges_ref[...])):
        rows_ref[:, p] = tile


def down_kernel(count_x, count_z, where_ref, mid_ref, mid_rim_ref, one_ref, one_rim_ref, two_ref,
                two_rim_ref, u_ref, b_ref, out_ref, c_ref, g_ref, h_ref, rows_ref):
    masks = rim_masks(count_x, count_z, where_ref)
    odd = where_ref[0] % 2

    def split_rows(ref, rim_ref, part):
        def split(x):
            for p in range(4):
                rows_ref[x, p, 0:BRICK_Z] = ref[x, p]
                rows_ref[x, p, BRICK_Z:WIDE_Z] = rim_ref[x, p]
                for q in range(4):
                    c_ref[part * BRICK_X + x, q, p] = rows_ref[x, p, pl.ds(q, 8, stride=4), :]

        each(0, BRICK_X, split, 2)

    split_rows(mid_ref, mid_rim_ref, 1)
    split_rows(one_ref, one_rim_ref, 2 - 2 * odd)
    split_rows(two_ref, two_rim_ref, 2 * odd)

    def source(x, weight):
        here = FINE.load(c_ref, x)
        sums = along_z(here, 1, True)
        plane = []
        for q in range(4):
            y_sums = along_y(here[q], 1)
            line = []
            for p in range(4):
                face = (c_ref[x - 1, q, p] + c_ref[x + 1, q, p]) + (sums[q][p] + y_sums[p])
                line.append((here[q][p] * 6.0 + face) * weight)
            plane.append(line)
        FINE.put(b_ref, g_ref, x, plane)

    in_segments(1, WIDE_X - 1, source, masks, 0.2 / 12.0, 4)

    def body(x, weight):
        FINE.put(u_ref, h_ref, x, FINE.sweep(b_ref, g_ref, b_ref, x, weight))

    in_segments(2, WIDE_X - 2, body, masks, 1.0 / 30.0, 4)
    send_residual(u_ref, h_ref, b_ref, out_ref)


def middle_kernel(count_x, count_z, count_pieces, where_ref, *refs):
    pieces, refs = refs[:count_pieces], refs[count_pieces:]
    u_ref, b_ref, v_ref, out_ref, ga_ref, gb_ref, ua_ref, *grids = refs
    masks = rim_masks(count_x, count_z, where_ref)
    coarse_solve(count_x, count_z, where_ref, pieces, grids)
    coarse_ref = coarse_finish(count_x, where_ref, grids)
    at_x, at_z = where_ref[0], where_ref[1]

    def error_of(i):
        plane = LEVEL_1.load(coarse_ref, 4 * at_x + i)
        return [[turned_tile(t, at_z, masks[0]) for t in line] for line in plane]

    add_correction(error_of, u_ref, v_ref, ga_ref, 2)
    fine_sweep(v_ref, ga_ref, ua_ref, gb_ref, b_ref, 3, masks)
    fine_sweep(ua_ref, gb_ref, v_ref, ga_ref, b_ref, 4, masks)
    fine_sweep(v_ref, ga_ref, ua_ref, gb_ref, b_ref, 5, masks)
    fine_sweep(ua_ref, gb_ref, v_ref, ga_ref, b_ref, 6, masks)
    send_residual(v_ref, ga_ref, b_ref, out_ref)


def up_kernel(count_x, count_z, count_pieces, where_ref, *refs):
    pieces, refs = refs[:count_pieces], refs[count_pieces:]
    u_ref, b_ref, out_ref, ga_ref, gb_ref, ua_ref, ub_ref, rows_ref, *refs = refs
    near, grids = refs[:5], refs[5:]
    masks = rim_masks(count_x, count_z, where_ref)
    coarse = coarse_solve(count_x, count_z, where_ref, pieces, grids)
    error_ref = near_finish(coarse, where_ref, masks, near)
    add_correction(lambda i: NEAR_1.load(error_ref, i), u_ref, ua_ref, ga_ref, 6)
    fine_sweep(ua_ref, ga_ref, ub_ref, gb_ref, b_ref, 7, masks)

    def body(x):
        plane = FINE.sweep(ub_ref, gb_ref, b_ref, x, 1.0 / 30.0)
        for q in range(4):
            for p in range(4):
                rows_ref[x - RIM, p, pl.ds(q, 4, stride=4), :] = plane[q][p][0:4]

    each(RIM, RIM + BRICK_X, body, 2)
    tiles = [rows_ref[:, p].reshape(BRICK_X * BRICK_Z, LANES) for p in range(4)]
    matrix = places(out_ref.shape[2], lambda l, y: y == (l % LANES) * 4 + l // LANES)
    out_ref[...] = permuted(jnp.concatenate(tiles, axis=1), matrix).reshape(out_ref.shape)


def call(kernel, outputs, scratch):
    shapes = [jax.ShapeDtypeStruct(shape, jnp.float32) for shape in outputs]
    held = sum(4 * math.prod(shape.shape) for shape in scratch)

    def run(where, *arrays):
        moved = sum(4 * math.prod(array.shape) for array in arrays + tuple(shapes))
        whole = pl.BlockSpec(memory_space=pltpu.VMEM)
        return pl.pallas_call(
            kernel,
            out_shape=shapes,
            in_specs=[pl.BlockSpec(memory_space=pltpu.SMEM)] + [whole] * len(arrays),
            out_specs=[whole] * len(shapes),
            scratch_shapes=scratch,
            compiler_params=pltpu.CompilerParams(vmem_limit_bytes=held + moved + SPARE_BYTES),
        )(where, *arrays)

    return run


def pairs_apart(count, distance):
    return [(i, i ^ distance) for i in range(count)]


def pairs_shifted(count):
    pairs = [(i, i + 1) for i in range(1, count - 1, 2)]
    return pairs + [(target, source) for source, target in pairs]


def swap(axis, values, distance):
    return lax.ppermute(values, axis, pairs_apart(lax.axis_size(axis), distance))


def every_piece(piece):
    count_x, count_z = lax.axis_size("gx"), lax.axis_size("gz")
    line = [swap("gz", piece[None], count_z - 1 - n) for n in range(count_z - 1)] + [piece[None]]
    halves = [jnp.concatenate(half) for half in (line[: count_z // 2], line[count_z // 2 :])]
    held = jnp.concatenate(halves + [swap("gx", half, 2) for half in halves])
    distance = 4
    while distance < count_x:
        held = jnp.concatenate([held, swap("gx", held, distance)])
        distance *= 2
    return held, swap("gx", held, 1)


def per_device(charges):
    count_x, count_z = lax.axis_size("gx"), lax.axis_size("gz")
    at_x, at_z = lax.axis_index("gx"), lax.axis_index("gz")
    where = jnp.stack([at_x, at_z]).astype(jnp.int32)
    brick, rim = (BRICK_X, 4, BRICK_Z, LANES), (BRICK_X, 4, RIM, LANES)
    middle, one, two = call(lanes_kernel, [brick, rim, rim], [])(where, charges)
    x_far, z_two = pairs_shifted(count_x), pairs_shifted(count_z)
    far = lax.ppermute(middle, "gx", x_far)
    (near,) = call(near_lanes_kernel, [brick], [])(where, swap("gx", charges, 1))
    one, two = swap("gz", one, 1), lax.ppermute(two, "gz", z_two)
    even = at_z % 2 == 0
    middle_rim = jnp.concatenate([jnp.where(even, one, two), jnp.where(even, two, one)], axis=2)
    far_rim = lax.ppermute(middle_rim, "gx", x_far)
    near_rim = swap("gx", middle_rim, 1)

    wide = (WIDE_X, 4, 4, 8, LANES)
    piece_shape = (BRICK_X // 2, 2, 8, LANES)
    fine = pltpu.VMEM(wide, jnp.float32)
    grids = coarse_grids(count_x, count_z)
    rows_in = pltpu.VMEM((BRICK_X, 4, WIDE_Z, LANES), jnp.float32)
    close = pltpu.VMEM((WIDE_X // 2, 2, 2, 8, LANES), jnp.float32)
    rows_out = pltpu.VMEM((BRICK_X, 4, BRICK_Z, LANES), jnp.float32)

    u, b, piece = call(
        functools.partial(down_kernel, count_x, count_z),
        [wide, wide, piece_shape],
        [fine] * 3 + [rows_in],
    )(where, middle, middle_rim, near, near_rim, far, far_rim)
    pieces = every_piece(piece)
    u, piece = call(
        functools.partial(middle_kernel, count_x, count_z, len(pieces)),
        [wide, piece_shape],
        [fine] * 3 + grids,
    )(where, *pieces, u, b)
    pieces = every_piece(piece)
    (potential,) = call(
        functools.partial(up_kernel, count_x, count_z, len(pieces)),
        [charges.shape],
        [fine] * 4 + [rows_out] + [close] * 5 + grids,
    )(where, *pieces, u, b)
    return potential


def solution(mesh):
    return jax.shard_map(
        per_device,
        mesh=mesh,
        in_specs=(P(("groups", "gx"), "gz", None),),
        out_specs=P(("groups", "gx"), "gz", None),
        check_vma=False,
    )
```

```python
import functools
import math

import jax
import jax.numpy as jnp
from jax import lax
from jax.experimental import pallas as pl
from jax.experimental.pallas import tpu as pltpu
from jax.sharding import PartitionSpec as P

COARSE_SWEEPS = 8
LANES = 128
RIM = 8
BRICK_X = 8
BRICK_Z = 16
WIDE_X = BRICK_X + 2 * RIM
WIDE_Z = BRICK_Z + 2 * RIM
SPARE_BYTES = 4 * 1024 * 1024


def lane_of(shape):
    return lax.broadcasted_iota(jnp.int32, shape, len(shape) - 1)


def row_of(shape):
    return lax.broadcasted_iota(jnp.int32, shape, len(shape) - 2)


def next_row(tile, step, cyclic):
    rows = tile.shape[0]
    moved = pltpu.roll(tile, rows - step, 0)
    return moved if cyclic else jnp.where(row_of(tile.shape) < rows - step, moved, 0.0)


def last_row(tile, step, cyclic):
    moved = pltpu.roll(tile, step, 0)
    return moved if cyclic else jnp.where(row_of(tile.shape) >= step, moved, 0.0)


def next_lane(tile, step):
    moved = pltpu.roll(tile, LANES - step, 1)
    return jnp.where(lane_of(tile.shape) < LANES - step, moved, 0.0)


def last_lane(tile, step):
    moved = pltpu.roll(tile, step, 1)
    return jnp.where(lane_of(tile.shape) >= step, moved, 0.0)


def load_plane(ref, x, count_q, count_p):
    return [[ref[x, q, p] for p in range(count_p)] for q in range(count_q)]


def store_plane(ref, x, plane):
    for q, line in enumerate(plane):
        for p, tile in enumerate(line):
            ref[x, q, p] = tile


def along_z(plane, step, cyclic):
    count_q, count_p = len(plane), len(plane[0])
    result = []
    for q in range(count_q):
        line = []
        for p in range(count_p):
            after = plane[q + 1][p] if q + 1 < count_q else next_row(plane[0][p], step, cyclic)
            before = plane[q - 1][p] if q > 0 else last_row(plane[-1][p], step, cyclic)
            line.append(after + before)
        result.append(line)
    return result


def along_y(line, step):
    count_p = len(line)
    result = []
    for p in range(count_p):
        after = line[p + 1] if p + 1 < count_p else next_lane(line[0], step)
        before = line[p - 1] if p > 0 else last_lane(line[-1], step)
        result.append(after + before)
    return result


class Level:
    def __init__(self, count_q, count_p, step, cyclic):
        self.count_q, self.count_p, self.step, self.cyclic = count_q, count_p, step, cyclic

    def load(self, ref, x):
        return load_plane(ref, x, self.count_q, self.count_p)

    def put(self, u_ref, g_ref, x, plane):
        store_plane(u_ref, x, plane)
        sums = along_z(plane, self.step, self.cyclic)
        store_plane(
            g_ref,
            x,
            [
                [s + (v + v) for s, v in zip(sum_line, line)]
                for sum_line, line in zip(sums, plane)
            ],
        )

    def spread(self, u_ref, g_ref, x, with_u):
        result = []
        for q in range(self.count_q):
            sides, both = [], []
            for p in range(self.count_p):
                here = g_ref[x, q, p]
                sides.append((u_ref[x - 1, q, p] + u_ref[x + 1, q, p]) + here)
                if with_u:
                    here = here + u_ref[x, q, p]
                both.append((g_ref[x - 1, q, p] + g_ref[x + 1, q, p]) + (here + here))
            result.append([a + b for a, b in zip(both, along_y(sides, self.step))])
        return result

    def sweep(self, u_ref, g_ref, b_ref, x, weight):
        wide = self.spread(u_ref, g_ref, x, True)
        return [
            [b_ref[x, q, p] + wide[q][p] * weight for p in range(self.count_p)]
            for q in range(self.count_q)
        ]

    def residual(self, u_ref, g_ref, b_ref, x):
        wide = self.spread(u_ref, g_ref, x, False)
        return [
            [
                b_ref[x, q, p] * 5.0 + (wide[q][p] - u_ref[x, q, p] * 28.0) * (1.0 / 6.0)
                for p in range(self.count_p)
            ]
            for q in range(self.count_q)
        ]


class Held:
    def __init__(self, rows, zero_at=()):
        self.tiles = {(x, 0, 0): jnp.zeros((rows, LANES), jnp.float32) for x in zero_at}

    def __getitem__(self, place):
        return self.tiles[place]

    def __setitem__(self, place, tile):
        self.tiles[place] = tile


def add_planes(one, other):
    return [[a + b for a, b in zip(l, m)] for l, m in zip(one, other)]


def join(plane):
    lines = [[a + b for a, b in zip(plane[q], plane[q + 1])] for q in range(0, len(plane), 2)]
    return [[line[p] + line[p + 1] for p in range(0, len(line), 2)] for line in lines]


def join_within(tile):
    rows = tile.shape[0]
    even = row_of(tile.shape) % 2 == 0
    tile = tile + jnp.where(even, pltpu.roll(tile, rows - 1, 0), pltpu.roll(tile, 1, 0))
    even = lane_of(tile.shape) % 2 == 0
    return tile + jnp.where(even, pltpu.roll(tile, LANES - 1, 1), pltpu.roll(tile, 1, 1))


def scaled(plane, factor):
    return [[tile * factor for tile in line] for line in plane]


def each(lo, hi, body, chunk):
    count = hi - lo
    whole = count // chunk
    if whole == 1:
        for x in range(lo, lo + chunk):
            body(x)
    elif whole > 1:

        def step(i, carry):
            for d in range(chunk):
                body(lo + i * chunk + d)
            return carry

        lax.fori_loop(0, whole, step, 0)
    for x in range(lo + whole * chunk, hi):
        body(x)


FINE = Level(4, 4, 1, True)
LEVEL_1 = Level(2, 2, 1, False)
NEAR_1 = Level(2, 2, 1, True)
LEVEL_2 = Level(1, 1, 1, False)
LEVEL_3 = Level(1, 1, 2, False)
PAD = RIM // 2
PAD_2 = RIM // 4


def zero_planes(ref, indices):
    for x in indices:
        ref[x] = jnp.zeros(ref.shape[1:], ref.dtype)


def coarse_grids(count_x, count_z):
    rows = count_z * BRICK_Z // 4
    shapes = []
    for planes, count in ((4 * count_x + 2 * PAD, 2), (2 * count_x + 2 * PAD_2, 1)):
        shapes += [pltpu.VMEM((planes, count, count, rows, LANES), jnp.float32)] * 5
    return shapes


def coarse_solve(count_x, count_z, where_ref, pieces, grids):
    ua1, ub1, ga1, gb1, b1 = grids[0:5]
    kept_2 = grids[5]
    size_1, size_2, size_3 = 4 * count_x, 2 * count_x, count_x
    rows = b1.shape[3]

    def ends(pad, size):
        return list(range(pad)) + list(range(pad + size, pad + size + pad))

    for ref in (ua1, ub1, ga1, gb1, b1):
        zero_planes(ref, ends(PAD, size_1))
    zero_planes(kept_2, ends(PAD_2, size_2))
    if size_2 <= 8:
        step_2 = size_2
        ua2, ub2, ga2, gb2, b2 = (Held(rows, ends(PAD_2, size_2)) for _ in range(5))
    else:
        step_2 = 8
        ua2, ub2, ga2, gb2, b2 = grids[5:10]
        for ref in (ub2, ga2, gb2):
            zero_planes(ref, ends(PAD_2, size_2))
    ua3, ub3, ga3, gb3, b3 = (Held(rows, ends(1, size_3)) for _ in range(5))
    third = 1.0 / 30.0

    at_x, at_z = where_ref[0], where_ref[1]

    def place(x, load):
        for i in range(4):
            plane = []
            for q in range(2):
                even, odd = [], []
                for z in range(0, count_z, 2):
                    one, two = load(z, i, q), load(z + 1, i, q)
                    first = row_of(one.shape) < 4
                    even.append(jnp.where(first, one, pltpu.roll(two, 4, 0)))
                    odd.append(jnp.where(first, pltpu.roll(one, 4, 0), two))
                plane.append([jnp.concatenate(even, axis=0), jnp.concatenate(odd, axis=0)])
            LEVEL_1.put(b1, gb1, x + i, plane)

    if len(pieces) == 1:

        def gather(n):
            place(PAD + 4 * n, lambda z, i, q: pieces[0][n * count_z + z, i, q])

        each(0, count_x, gather, 1)
    else:

        def gather(n):
            for core in range(2):
                x = PAD + 4 * ((2 * n + core) ^ at_x)
                place(x, lambda z, i, q: pieces[core][n * count_z + (z ^ at_z ^ (count_z - 1)), i, q])

        each(0, count_x // 2, gather, 1)

    def sweep(level, u_in, g_in, u_out, g_out, b):
        return lambda x: level.put(u_out, g_out, x, level.sweep(u_in, g_in, b, x, third))

    each(PAD, PAD + size_1, sweep(LEVEL_1, b1, gb1, ua1, ga1, b1), 16)

    def restrict_1(x):
        fine = PAD + 2 * x
        pair = add_planes(
            LEVEL_1.residual(ua1, ga1, b1, fine), LEVEL_1.residual(ua1, ga1, b1, fine + 1)
        )
        plane = scaled(join(pair), 0.5 * 0.2)
        store_plane(b2, PAD_2 + x, plane)
        LEVEL_2.put(ub2, gb2, PAD_2 + x, plane)

    each(0, size_2, restrict_1, step_2)
    all_2 = (PAD_2, PAD_2 + size_2)
    each(*all_2, sweep(LEVEL_2, ub2, gb2, ua2, ga2, b2), step_2)

    def restrict_2(x):
        fine = PAD_2 + 2 * x
        pair = add_planes(
            LEVEL_2.residual(ua2, ga2, b2, fine), LEVEL_2.residual(ua2, ga2, b2, fine + 1)
        )
        plane = [[join_within(pair[0][0]) * (0.5 * 0.2)]]
        store_plane(b3, 1 + x, plane)
        LEVEL_3.put(ub3, gb3, 1 + x, plane)

    each(0, size_3, restrict_2, size_3)
    now, later = (ub3, gb3), (ua3, ga3)
    for _ in range(COARSE_SWEEPS - 1):
        each(1, 1 + size_3, sweep(LEVEL_3, *now, *later, b3), size_3)
        now, later = later, now

    def prolong_3(x):
        for d in range(2):
            fine = PAD_2 + 2 * x + d
            LEVEL_2.put(ua2, ga2, fine, [[ua2[fine, 0, 0] + now[0][1 + x, 0, 0]]])

    each(0, size_3, prolong_3, size_3)
    each(*all_2, sweep(LEVEL_2, ua2, ga2, ub2, gb2, b2), step_2)

    def last_sweep(x):
        store_plane(kept_2, x, LEVEL_2.sweep(ub2, gb2, b2, x, third))

    each(*all_2, last_sweep, step_2)
    return ua1, kept_2, b1


def coarse_finish(count_x, where_ref, grids):
    ua1, ub1, ga1, gb1, b1 = grids[0:5]
    ua2 = grids[5]
    size_1, size_2 = 4 * count_x, 2 * count_x
    third = 1.0 / 30.0

    def prolong_2(x):
        error = ua2[PAD_2 + x, 0, 0]
        for d in range(2):
            fine = PAD + 2 * x + d
            LEVEL_1.put(
                ua1, ga1, fine, [[t + error for t in line] for line in LEVEL_1.load(ua1, fine)]
            )

    def window(rim):
        count = min(BRICK_X // 2 + 2 * rim, size_1)
        return PAD + jnp.clip(4 * where_ref[0] - rim, 0, size_1 - count), count

    start, count = window(4)

    def sweep(i):
        x = start + i
        LEVEL_1.put(ub1, gb1, x, LEVEL_1.sweep(ua1, ga1, b1, x, third))

    last_start, last_count = window(3)

    def last_sweep(i):
        x = last_start + i
        store_plane(ua1, x, LEVEL_1.sweep(ub1, gb1, b1, x, third))

    each(0, size_2, prolong_2, 8)
    each(0, count, sweep, 12)
    each(0, last_count, last_sweep, 10)
    return ua1


def turned_tile(tile, at_z, rows):
    count = tile.shape[0]
    turned = pltpu.roll(tile, lax.rem(count - 4 * at_z, count), 0)
    return jnp.where(row_of((8, LANES)) < 6, turned[0:8], turned[count - 8 : count]) * rows


def near_finish(coarse, where_ref, masks, near):
    ua1, ua2, b1 = coarse
    ua, ga, ub, gb, b = near
    at_x, at_z = where_ref[0], where_ref[1]
    rows = masks[0]

    def take(i):
        error = ua2[2 * at_x + i // 2, 0, 0]
        plane = [[t + error for t in line] for line in LEVEL_1.load(ua1, 4 * at_x + i)]
        plane = [[turned_tile(t, at_z, rows) for t in line] for line in plane]
        NEAR_1.put(ua, ga, i, plane)
        plane = LEVEL_1.load(b1, 4 * at_x + i)
        store_plane(b, i, [[turned_tile(t, at_z, rows) for t in line] for line in plane])

    each(1, 11, take, 5)

    def sweep(i, weight):
        NEAR_1.put(ub, gb, i, NEAR_1.sweep(ua, ga, b, i, weight))

    def last_sweep(i, weight):
        store_plane(ua, i, NEAR_1.sweep(ub, gb, b, i, weight))

    in_segments(2, 10, sweep, masks, 1.0 / 30.0, 4, PAD, BRICK_X // 2)
    in_segments(3, 9, last_sweep, masks, 1.0 / 30.0, 4, PAD, BRICK_X // 2)
    return ua


def rim_masks(count_x, count_z, where_ref):
    at_x, at_z = where_ref[0], where_ref[1]
    k = row_of((8, LANES))
    low = (at_z > 0).astype(jnp.float32)
    high = (at_z < count_z - 1).astype(jnp.float32)
    rows = jnp.where(k < 4, 1.0, jnp.where(k < 6, high, low))
    below = (at_x > 0).astype(jnp.float32)
    above = (at_x < count_x - 1).astype(jnp.float32)
    return rows, below, above


def in_segments(lo, hi, body, masks, scale, chunk, rim=RIM, brick=BRICK_X):
    rows, below, above = masks
    inner = rows * scale
    for start, end, weight in (
        (lo, min(hi, rim), inner * below),
        (max(lo, rim), min(hi, rim + brick), inner),
        (max(lo, rim + brick), hi, inner * above),
    ):
        if end > start:
            each(start, end, functools.partial(body, weight=weight), chunk)


def fine_sweep(u_in, g_in, u_out, g_out, b_ref, margin, masks):
    def body(x, weight):
        FINE.put(u_out, g_out, x, FINE.sweep(u_in, g_in, b_ref, x, weight))

    in_segments(margin, WIDE_X - margin, body, masks, 1.0 / 30.0, 4)


def add_correction(error_of, u_in, u_out, g_out, margin):
    def body(i):
        error = error_of(i)
        for d in range(2):
            x = 2 * i + d
            plane = [
                [u_in[x, q, p] + error[q // 2][p // 2] for p in range(4)] for q in range(4)
            ]
            FINE.put(u_out, g_out, x, plane)

    each(margin // 2, (WIDE_X - margin) // 2, body, 2)


def send_residual(u_ref, g_ref, b_ref, out_ref):
    def body(i):
        x = RIM + 2 * i
        pair = add_planes(
            FINE.residual(u_ref, g_ref, b_ref, x), FINE.residual(u_ref, g_ref, b_ref, x + 1)
        )
        for q, (even, odd) in enumerate(join(pair)):
            out_ref[i, q] = 0.1 * jnp.where(row_of(even.shape) < 4, even, pltpu.roll(odd, 4, 0))

    each(0, BRICK_X // 2, body, BRICK_X // 2)


def places(size, joins):
    row, column = (lax.broadcasted_iota(jnp.int32, (size, size), d) for d in range(2))
    return joins(row, column).astype(jnp.float32).astype(jnp.bfloat16)


def permuted(values, matrix):
    rest, terms = values, []
    for _ in range(3):
        term = rest.astype(jnp.bfloat16)
        rest = rest - term.astype(jnp.float32)
        terms.append(jnp.dot(term, matrix, preferred_element_type=jnp.float32))
    return terms[0] + (terms[1] + terms[2])


def split_lanes(values):
    size_x, size_z, size_y = values.shape
    matrix = places(size_y, lambda y, l: y == (l % LANES) * 4 + l // LANES)
    split = permuted(values.reshape(size_x * size_z, size_y), matrix)
    return [
        split[:, p * LANES : (p + 1) * LANES].reshape(size_x, size_z, LANES) for p in range(4)
    ]


def lanes_kernel(where_ref, charges_ref, rows_ref, one_ref, two_ref):
    odd = where_ref[1] % 2
    for p, tile in enumerate(split_lanes(charges_ref[...])):
        rows_ref[:, p] = tile
        first, last = tile[:, 0:8], tile[:, 8:16]
        one_ref[:, p] = jnp.where(odd == 0, last, first)
        two_ref[:, p] = jnp.where(odd == 0, first, last)


def near_lanes_kernel(where_ref, charges_ref, rows_ref):
    for p, tile in enumerate(split_lanes(charges_ref[...])):
        rows_ref[:, p] = tile


def down_kernel(count_x, count_z, where_ref, mid_ref, mid_rim_ref, one_ref, one_rim_ref, two_ref,
                two_rim_ref, u_ref, b_ref, out_ref, c_ref, g_ref, h_ref, rows_ref):
    masks = rim_masks(count_x, count_z, where_ref)
    odd = where_ref[0] % 2

    def split_rows(ref, rim_ref, part):
        def split(x):
            for p in range(4):
                rows_ref[x, p, 0:BRICK_Z] = ref[x, p]
                rows_ref[x, p, BRICK_Z:WIDE_Z] = rim_ref[x, p]
                for q in range(4):
                    c_ref[part * BRICK_X + x, q, p] = rows_ref[x, p, pl.ds(q, 8, stride=4), :]

        each(0, BRICK_X, split, 2)

    split_rows(mid_ref, mid_rim_ref, 1)
    split_rows(one_ref, one_rim_ref, 2 - 2 * odd)
    split_rows(two_ref, two_rim_ref, 2 * odd)

    def source(x, weight):
        here = FINE.load(c_ref, x)
        sums = along_z(here, 1, True)
        plane = []
        for q in range(4):
            y_sums = along_y(here[q], 1)
            line = []
            for p in range(4):
                face = (c_ref[x - 1, q, p] + c_ref[x + 1, q, p]) + (sums[q][p] + y_sums[p])
                line.append((here[q][p] * 6.0 + face) * weight)
            plane.append(line)
        FINE.put(b_ref, g_ref, x, plane)

    in_segments(1, WIDE_X - 1, source, masks, 0.2 / 12.0, 4)

    def body(x, weight):
        FINE.put(u_ref, h_ref, x, FINE.sweep(b_ref, g_ref, b_ref, x, weight))

    in_segments(2, WIDE_X - 2, body, masks, 1.0 / 30.0, 4)
    send_residual(u_ref, h_ref, b_ref, out_ref)


def middle_kernel(count_x, count_z, count_pieces, where_ref, *refs):
    pieces, refs = refs[:count_pieces], refs[count_pieces:]
    u_ref, b_ref, v_ref, out_ref, ga_ref, gb_ref, ua_ref, *grids = refs
    masks = rim_masks(count_x, count_z, where_ref)
    coarse_solve(count_x, count_z, where_ref, pieces, grids)
    coarse_ref = coarse_finish(count_x, where_ref, grids)
    at_x, at_z = where_ref[0], where_ref[1]

    def error_of(i):
        plane = LEVEL_1.load(coarse_ref, 4 * at_x + i)
        return [[turned_tile(t, at_z, masks[0]) for t in line] for line in plane]

    add_correction(error_of, u_ref, v_ref, ga_ref, 2)
    fine_sweep(v_ref, ga_ref, ua_ref, gb_ref, b_ref, 3, masks)
    fine_sweep(ua_ref, gb_ref, v_ref, ga_ref, b_ref, 4, masks)
    fine_sweep(v_ref, ga_ref, ua_ref, gb_ref, b_ref, 5, masks)
    fine_sweep(ua_ref, gb_ref, v_ref, ga_ref, b_ref, 6, masks)
    send_residual(v_ref, ga_ref, b_ref, out_ref)


def up_kernel(count_x, count_z, count_pieces, where_ref, *refs):
    pieces, refs = refs[:count_pieces], refs[count_pieces:]
    u_ref, b_ref, out_ref, ga_ref, gb_ref, ua_ref, ub_ref, rows_ref, *refs = refs
    near, grids = refs[:5], refs[5:]
    masks = rim_masks(count_x, count_z, where_ref)
    coarse = coarse_solve(count_x, count_z, where_ref, pieces, grids)
    error_ref = near_finish(coarse, where_ref, masks, near)
    add_correction(lambda i: NEAR_1.load(error_ref, i), u_ref, ua_ref, ga_ref, 6)
    fine_sweep(ua_ref, ga_ref, ub_ref, gb_ref, b_ref, 7, masks)

    def body(x):
        plane = FINE.sweep(ub_ref, gb_ref, b_ref, x, 1.0 / 30.0)
        for q in range(4):
            for p in range(4):
                rows_ref[x - RIM, p, pl.ds(q, 4, stride=4), :] = plane[q][p][0:4]

    each(RIM, RIM + BRICK_X, body, 2)
    tiles = [rows_ref[:, p].reshape(BRICK_X * BRICK_Z, LANES) for p in range(4)]
    matrix = places(out_ref.shape[2], lambda l, y: y == (l % LANES) * 4 + l // LANES)
    out_ref[...] = permuted(jnp.concatenate(tiles, axis=1), matrix).reshape(out_ref.shape)


def call(kernel, outputs, scratch):
    shapes = [jax.ShapeDtypeStruct(shape, jnp.float32) for shape in outputs]
    held = sum(4 * math.prod(shape.shape) for shape in scratch)

    def run(where, *arrays):
        moved = sum(4 * math.prod(array.shape) for array in arrays + tuple(shapes))
        whole = pl.BlockSpec(memory_space=pltpu.VMEM)
        return pl.pallas_call(
            kernel,
            out_shape=shapes,
            in_specs=[pl.BlockSpec(memory_space=pltpu.SMEM)] + [whole] * len(arrays),
            out_specs=[whole] * len(shapes),
            scratch_shapes=scratch,
            compiler_params=pltpu.CompilerParams(vmem_limit_bytes=held + moved + SPARE_BYTES),
        )(where, *arrays)

    return run


def pairs_apart(count, distance):
    return [(i, i ^ distance) for i in range(count)]


def pairs_shifted(count):
    pairs = [(i, i + 1) for i in range(1, count - 1, 2)]
    return pairs + [(target, source) for source, target in pairs]


def swap(axis, values, distance):
    return lax.ppermute(values, axis, pairs_apart(lax.axis_size(axis), distance))


def every_piece(piece):
    count_x, count_z = lax.axis_size("gx"), lax.axis_size("gz")
    line = [swap("gz", piece[None], count_z - 1 - n) for n in range(count_z - 1)] + [piece[None]]
    halves = [jnp.concatenate(half) for half in (line[: count_z // 2], line[count_z // 2 :])]
    held = jnp.concatenate(halves + [swap("gx", half, 2) for half in halves])
    distance = 4
    while distance < count_x:
        held = jnp.concatenate([held, swap("gx", held, distance)])
        distance *= 2
    return held, swap("gx", held, 1)


def per_device(charges):
    count_x, count_z = lax.axis_size("gx"), lax.axis_size("gz")
    at_x, at_z = lax.axis_index("gx"), lax.axis_index("gz")
    where = jnp.stack([at_x, at_z]).astype(jnp.int32)
    brick, rim = (BRICK_X, 4, BRICK_Z, LANES), (BRICK_X, 4, RIM, LANES)
    middle, one, two = call(lanes_kernel, [brick, rim, rim], [])(where, charges)
    x_far, z_two = pairs_shifted(count_x), pairs_shifted(count_z)
    far = lax.ppermute(middle, "gx", x_far)
    (near,) = call(near_lanes_kernel, [brick], [])(where, swap("gx", charges, 1))
    one, two = swap("gz", one, 1), lax.ppermute(two, "gz", z_two)
    even = at_z % 2 == 0

    def both_rims(from_one, from_two):
        after, before = jnp.where(even, from_one, from_two), jnp.where(even, from_two, from_one)
        return jnp.concatenate([after, before], axis=2)

    middle_rim = both_rims(one, two)
    far_rim = both_rims(lax.ppermute(one, "gx", x_far), lax.ppermute(two, "gx", x_far))
    near_rim = swap("gx", middle_rim, 1)

    wide = (WIDE_X, 4, 4, 8, LANES)
    piece_shape = (BRICK_X // 2, 2, 8, LANES)
    fine = pltpu.VMEM(wide, jnp.float32)
    grids = coarse_grids(count_x, count_z)
    rows_in = pltpu.VMEM((BRICK_X, 4, WIDE_Z, LANES), jnp.float32)
    close = pltpu.VMEM((WIDE_X // 2, 2, 2, 8, LANES), jnp.float32)
    rows_out = pltpu.VMEM((BRICK_X, 4, BRICK_Z, LANES), jnp.float32)

    u, b, piece = call(
        functools.partial(down_kernel, count_x, count_z),
        [wide, wide, piece_shape],
        [fine] * 3 + [rows_in],
    )(where, middle, middle_rim, near, near_rim, far, far_rim)
    pieces = every_piece(piece)
    u, piece = call(
        functools.partial(middle_kernel, count_x, count_z, len(pieces)),
        [wide, piece_shape],
        [fine] * 3 + grids,
    )(where, *pieces, u, b)
    pieces = every_piece(piece)
    (potential,) = call(
        functools.partial(up_kernel, count_x, count_z, len(pieces)),
        [charges.shape],
        [fine] * 4 + [rows_out] + [close] * 5 + grids,
    )(where, *pieces, u, b)
    return potential


def solution(mesh):
    return jax.shard_map(
        per_device,
        mesh=mesh,
        in_specs=(P(("groups", "gx"), "gz", None),),
        out_specs=P(("groups", "gx"), "gz", None),
        check_vma=False,
    )
```

```python
import functools
import math

import jax
import jax.numpy as jnp
from jax import lax
from jax.experimental import pallas as pl
from jax.experimental.pallas import tpu as pltpu
from jax.sharding import PartitionSpec as P

COARSE_SWEEPS = 8
LANES = 128
RIM = 8
BRICK_X = 8
BRICK_Z = 16
WIDE_X = BRICK_X + 2 * RIM
WIDE_Z = BRICK_Z + 2 * RIM
SPARE_BYTES = 4 * 1024 * 1024


def lane_of(shape):
    return lax.broadcasted_iota(jnp.int32, shape, len(shape) - 1)


def row_of(shape):
    return lax.broadcasted_iota(jnp.int32, shape, len(shape) - 2)


def next_row(tile, step, cyclic):
    rows = tile.shape[0]
    moved = pltpu.roll(tile, rows - step, 0)
    return moved if cyclic else jnp.where(row_of(tile.shape) < rows - step, moved, 0.0)


def last_row(tile, step, cyclic):
    moved = pltpu.roll(tile, step, 0)
    return moved if cyclic else jnp.where(row_of(tile.shape) >= step, moved, 0.0)


def next_lane(tile, step):
    moved = pltpu.roll(tile, LANES - step, 1)
    return jnp.where(lane_of(tile.shape) < LANES - step, moved, 0.0)


def last_lane(tile, step):
    moved = pltpu.roll(tile, step, 1)
    return jnp.where(lane_of(tile.shape) >= step, moved, 0.0)


def load_plane(ref, x, count_q, count_p):
    return [[ref[x, q, p] for p in range(count_p)] for q in range(count_q)]


def store_plane(ref, x, plane):
    for q, line in enumerate(plane):
        for p, tile in enumerate(line):
            ref[x, q, p] = tile


def along_z(plane, step, cyclic):
    count_q, count_p = len(plane), len(plane[0])
    result = []
    for q in range(count_q):
        line = []
        for p in range(count_p):
            after = plane[q + 1][p] if q + 1 < count_q else next_row(plane[0][p], step, cyclic)
            before = plane[q - 1][p] if q > 0 else last_row(plane[-1][p], step, cyclic)
            line.append(after + before)
        result.append(line)
    return result


def along_y(line, step):
    count_p = len(line)
    result = []
    for p in range(count_p):
        after = line[p + 1] if p + 1 < count_p else next_lane(line[0], step)
        before = line[p - 1] if p > 0 else last_lane(line[-1], step)
        result.append(after + before)
    return result


class Level:
    def __init__(self, count_q, count_p, step, cyclic):
        self.count_q, self.count_p, self.step, self.cyclic = count_q, count_p, step, cyclic

    def load(self, ref, x):
        return load_plane(ref, x, self.count_q, self.count_p)

    def put(self, u_ref, g_ref, x, plane):
        store_plane(u_ref, x, plane)
        sums = along_z(plane, self.step, self.cyclic)
        store_plane(
            g_ref,
            x,
            [
                [s + (v + v) for s, v in zip(sum_line, line)]
                for sum_line, line in zip(sums, plane)
            ],
        )

    def spread(self, u_ref, g_ref, x, with_u):
        result = []
        for q in range(self.count_q):
            sides, both = [], []
            for p in range(self.count_p):
                here = g_ref[x, q, p]
                sides.append((u_ref[x - 1, q, p] + u_ref[x + 1, q, p]) + here)
                if with_u:
                    here = here + u_ref[x, q, p]
                both.append((g_ref[x - 1, q, p] + g_ref[x + 1, q, p]) + (here + here))
            result.append([a + b for a, b in zip(both, along_y(sides, self.step))])
        return result

    def sweep(self, u_ref, g_ref, b_ref, x, weight):
        wide = self.spread(u_ref, g_ref, x, True)
        return [
            [b_ref[x, q, p] + wide[q][p] * weight for p in range(self.count_p)]
            for q in range(self.count_q)
        ]

    def residual(self, u_ref, g_ref, b_ref, x):
        wide = self.spread(u_ref, g_ref, x, False)
        return [
            [
                b_ref[x, q, p] * 5.0 + (wide[q][p] - u_ref[x, q, p] * 28.0) * (1.0 / 6.0)
                for p in range(self.count_p)
            ]
            for q in range(self.count_q)
        ]


class Held:
    def __init__(self, rows, zero_at=()):
        self.tiles = {(x, 0, 0): jnp.zeros((rows, LANES), jnp.float32) for x in zero_at}

    def __getitem__(self, place):
        return self.tiles[place]

    def __setitem__(self, place, tile):
        self.tiles[place] = tile


def add_planes(one, other):
    return [[a + b for a, b in zip(l, m)] for l, m in zip(one, other)]


def join(plane):
    lines = [[a + b for a, b in zip(plane[q], plane[q + 1])] for q in range(0, len(plane), 2)]
    return [[line[p] + line[p + 1] for p in range(0, len(line), 2)] for line in lines]


def join_within(tile):
    rows = tile.shape[0]
    even = row_of(tile.shape) % 2 == 0
    tile = tile + jnp.where(even, pltpu.roll(tile, rows - 1, 0), pltpu.roll(tile, 1, 0))
    even = lane_of(tile.shape) % 2 == 0
    return tile + jnp.where(even, pltpu.roll(tile, LANES - 1, 1), pltpu.roll(tile, 1, 1))


def scaled(plane, factor):
    return [[tile * factor for tile in line] for line in plane]


def each(lo, hi, body, chunk):
    count = hi - lo
    whole = count // chunk
    if whole == 1:
        for x in range(lo, lo + chunk):
            body(x)
    elif whole > 1:

        def step(i, carry):
            for d in range(chunk):
                body(lo + i * chunk + d)
            return carry

        lax.fori_loop(0, whole, step, 0)
    for x in range(lo + whole * chunk, hi):
        body(x)


FINE = Level(4, 4, 1, True)
LEVEL_1 = Level(2, 2, 1, False)
NEAR_1 = Level(2, 2, 1, True)
LEVEL_2 = Level(1, 1, 1, False)
LEVEL_3 = Level(1, 1, 2, False)
PAD = RIM // 2
PAD_2 = RIM // 4


def zero_planes(ref, indices):
    for x in indices:
        ref[x] = jnp.zeros(ref.shape[1:], ref.dtype)


def coarse_grids(count_x, count_z):
    rows = count_z * BRICK_Z // 4
    shapes = []
    for planes, count in ((4 * count_x + 2 * PAD, 2), (2 * count_x + 2 * PAD_2, 1)):
        shapes += [pltpu.VMEM((planes, count, count, rows, LANES), jnp.float32)] * 5
    return shapes


def coarse_solve(count_x, count_z, where_ref, pieces, grids):
    ua1, ub1, ga1, gb1, b1 = grids[0:5]
    kept_2 = grids[5]
    size_1, size_2, size_3 = 4 * count_x, 2 * count_x, count_x
    rows = b1.shape[3]

    def ends(pad, size):
        return list(range(pad)) + list(range(pad + size, pad + size + pad))

    for ref in (ua1, ub1, ga1, gb1, b1):
        zero_planes(ref, ends(PAD, size_1))
    zero_planes(kept_2, ends(PAD_2, size_2))
    if size_2 <= 8:
        step_2 = size_2
        ua2, ub2, ga2, gb2, b2 = (Held(rows, ends(PAD_2, size_2)) for _ in range(5))
    else:
        step_2 = 8
        ua2, ub2, ga2, gb2, b2 = grids[5:10]
        for ref in (ub2, ga2, gb2):
            zero_planes(ref, ends(PAD_2, size_2))
    ua3, ub3, ga3, gb3, b3 = (Held(rows, ends(1, size_3)) for _ in range(5))
    third = 1.0 / 30.0

    at_x, at_z = where_ref[0], where_ref[1]

    def place(x, load):
        for i in range(4):
            plane = []
            for q in range(2):
                even, odd = [], []
                for z in range(0, count_z, 2):
                    one, two = load(z, i, q), load(z + 1, i, q)
                    first = row_of(one.shape) < 4
                    even.append(jnp.where(first, one, pltpu.roll(two, 4, 0)))
                    odd.append(jnp.where(first, pltpu.roll(one, 4, 0), two))
                plane.append([jnp.concatenate(even, axis=0), jnp.concatenate(odd, axis=0)])
            LEVEL_1.put(b1, gb1, x + i, plane)

    if len(pieces) == 1:

        def gather(n):
            place(PAD + 4 * n, lambda z, i, q: pieces[0][n * count_z + z, i, q])

        each(0, count_x, gather, 1)
    else:

        def gather(n):
            for core in range(2):
                x = PAD + 4 * ((2 * n + core) ^ at_x)
                place(x, lambda z, i, q: pieces[core][n * count_z + (z ^ at_z ^ (count_z - 1)), i, q])

        each(0, count_x // 2, gather, 1)

    def sweep(level, u_in, g_in, u_out, g_out, b):
        return lambda x: level.put(u_out, g_out, x, level.sweep(u_in, g_in, b, x, third))

    each(PAD, PAD + size_1, sweep(LEVEL_1, b1, gb1, ua1, ga1, b1), 16)

    def restrict_1(x):
        fine = PAD + 2 * x
        pair = add_planes(
            LEVEL_1.residual(ua1, ga1, b1, fine), LEVEL_1.residual(ua1, ga1, b1, fine + 1)
        )
        plane = scaled(join(pair), 0.5 * 0.2)
        store_plane(b2, PAD_2 + x, plane)
        LEVEL_2.put(ub2, gb2, PAD_2 + x, plane)

    each(0, size_2, restrict_1, step_2)
    all_2 = (PAD_2, PAD_2 + size_2)
    each(*all_2, sweep(LEVEL_2, ub2, gb2, ua2, ga2, b2), step_2)

    def restrict_2(x):
        fine = PAD_2 + 2 * x
        pair = add_planes(
            LEVEL_2.residual(ua2, ga2, b2, fine), LEVEL_2.residual(ua2, ga2, b2, fine + 1)
        )
        plane = [[join_within(pair[0][0]) * (0.5 * 0.2)]]
        store_plane(b3, 1 + x, plane)
        LEVEL_3.put(ub3, gb3, 1 + x, plane)

    each(0, size_3, restrict_2, size_3)
    now, later = (ub3, gb3), (ua3, ga3)
    for _ in range(COARSE_SWEEPS - 1):
        each(1, 1 + size_3, sweep(LEVEL_3, *now, *later, b3), size_3)
        now, later = later, now

    def prolong_3(x):
        for d in range(2):
            fine = PAD_2 + 2 * x + d
            LEVEL_2.put(ua2, ga2, fine, [[ua2[fine, 0, 0] + now[0][1 + x, 0, 0]]])

    each(0, size_3, prolong_3, size_3)
    each(*all_2, sweep(LEVEL_2, ua2, ga2, ub2, gb2, b2), step_2)

    def last_sweep(x):
        store_plane(kept_2, x, LEVEL_2.sweep(ub2, gb2, b2, x, third))

    each(*all_2, last_sweep, step_2)
    return ua1, kept_2, b1


def coarse_finish(count_x, where_ref, grids):
    ua1, ub1, ga1, gb1, b1 = grids[0:5]
    ua2 = grids[5]
    size_1, size_2 = 4 * count_x, 2 * count_x
    third = 1.0 / 30.0

    def prolong_2(x):
        error = ua2[PAD_2 + x, 0, 0]
        for d in range(2):
            fine = PAD + 2 * x + d
            LEVEL_1.put(
                ua1, ga1, fine, [[t + error for t in line] for line in LEVEL_1.load(ua1, fine)]
            )

    def window(rim):
        count = min(BRICK_X // 2 + 2 * rim, size_1)
        return PAD + jnp.clip(4 * where_ref[0] - rim, 0, size_1 - count), count

    start, count = window(4)

    def sweep(i):
        x = start + i
        LEVEL_1.put(ub1, gb1, x, LEVEL_1.sweep(ua1, ga1, b1, x, third))

    last_start, last_count = window(3)

    def last_sweep(i):
        x = last_start + i
        store_plane(ua1, x, LEVEL_1.sweep(ub1, gb1, b1, x, third))

    each(0, size_2, prolong_2, 8)
    each(0, count, sweep, 12)
    each(0, last_count, last_sweep, 10)
    return ua1


def turned_tile(tile, at_z, rows):
    count = tile.shape[0]
    turned = pltpu.roll(tile, lax.rem(count - 4 * at_z, count), 0)
    return jnp.where(row_of((8, LANES)) < 6, turned[0:8], turned[count - 8 : count]) * rows


def near_finish(coarse, where_ref, masks, near):
    ua1, ua2, b1 = coarse
    ua, ga, ub, gb, b = near
    at_x, at_z = where_ref[0], where_ref[1]
    rows = masks[0]

    def take(i):
        error = ua2[2 * at_x + i // 2, 0, 0]
        plane = [[t + error for t in line] for line in LEVEL_1.load(ua1, 4 * at_x + i)]
        plane = [[turned_tile(t, at_z, rows) for t in line] for line in plane]
        NEAR_1.put(ua, ga, i, plane)
        plane = LEVEL_1.load(b1, 4 * at_x + i)
        store_plane(b, i, [[turned_tile(t, at_z, rows) for t in line] for line in plane])

    each(1, 11, take, 5)

    def sweep(i, weight):
        NEAR_1.put(ub, gb, i, NEAR_1.sweep(ua, ga, b, i, weight))

    def last_sweep(i, weight):
        store_plane(ua, i, NEAR_1.sweep(ub, gb, b, i, weight))

    in_segments(2, 10, sweep, masks, 1.0 / 30.0, 4, PAD, BRICK_X // 2)
    in_segments(3, 9, last_sweep, masks, 1.0 / 30.0, 4, PAD, BRICK_X // 2)
    return ua


def rim_masks(count_x, count_z, where_ref):
    at_x, at_z = where_ref[0], where_ref[1]
    k = row_of((8, LANES))
    low = (at_z > 0).astype(jnp.float32)
    high = (at_z < count_z - 1).astype(jnp.float32)
    rows = jnp.where(k < 4, 1.0, jnp.where(k < 6, high, low))
    below = (at_x > 0).astype(jnp.float32)
    above = (at_x < count_x - 1).astype(jnp.float32)
    return rows, below, above


def in_segments(lo, hi, body, masks, scale, chunk, rim=RIM, brick=BRICK_X):
    rows, below, above = masks
    inner = rows * scale
    for start, end, weight in (
        (lo, min(hi, rim), inner * below),
        (max(lo, rim), min(hi, rim + brick), inner),
        (max(lo, rim + brick), hi, inner * above),
    ):
        if end > start:
            each(start, end, functools.partial(body, weight=weight), chunk)


def fine_sweep(u_in, g_in, u_out, g_out, b_ref, margin, masks):
    def body(x, weight):
        FINE.put(u_out, g_out, x, FINE.sweep(u_in, g_in, b_ref, x, weight))

    in_segments(margin, WIDE_X - margin, body, masks, 1.0 / 30.0, 4)


def add_correction(error_of, u_in, u_out, g_out, margin):
    def body(i):
        error = error_of(i)
        for d in range(2):
            x = 2 * i + d
            plane = [
                [u_in[x, q, p] + error[q // 2][p // 2] for p in range(4)] for q in range(4)
            ]
            FINE.put(u_out, g_out, x, plane)

    each(margin // 2, (WIDE_X - margin) // 2, body, 2)


def send_residual(u_ref, g_ref, b_ref, out_ref):
    def body(i):
        x = RIM + 2 * i
        pair = add_planes(
            FINE.residual(u_ref, g_ref, b_ref, x), FINE.residual(u_ref, g_ref, b_ref, x + 1)
        )
        for q, (even, odd) in enumerate(join(pair)):
            out_ref[i, q] = 0.1 * jnp.where(row_of(even.shape) < 4, even, pltpu.roll(odd, 4, 0))

    each(0, BRICK_X // 2, body, BRICK_X // 2)


def places(size, joins):
    row, column = (lax.broadcasted_iota(jnp.int32, (size, size), d) for d in range(2))
    return joins(row, column).astype(jnp.float32).astype(jnp.bfloat16)


def permuted(values, matrix):
    rest, terms = values, []
    for _ in range(3):
        term = rest.astype(jnp.bfloat16)
        rest = rest - term.astype(jnp.float32)
        terms.append(jnp.dot(term, matrix, preferred_element_type=jnp.float32))
    return terms[0] + (terms[1] + terms[2])


def split_lanes(values):
    size_x, size_z, size_y = values.shape
    matrix = places(size_y, lambda y, l: y == (l % LANES) * 4 + l // LANES)
    split = permuted(values.reshape(size_x * size_z, size_y), matrix)
    return [
        split[:, p * LANES : (p + 1) * LANES].reshape(size_x, size_z, LANES) for p in range(4)
    ]


def lanes_kernel(where_ref, charges_ref, rows_ref, one_ref, two_ref):
    odd = where_ref[1] % 2
    for p, tile in enumerate(split_lanes(charges_ref[...])):
        rows_ref[:, p] = tile
        first, last = tile[:, 0:8], tile[:, 8:16]
        one_ref[:, p] = jnp.where(odd == 0, last, first)
        two_ref[:, p] = jnp.where(odd == 0, first, last)


def row_splitter(rows_ref, c_ref):
    def split_rows(ref, rim_ref, part):
        def split(x):
            for p in range(4):
                rows_ref[x, p, 0:BRICK_Z] = ref[x, p]
                rows_ref[x, p, BRICK_Z:WIDE_Z] = rim_ref[x, p]
                for q in range(4):
                    c_ref[part * BRICK_X + x, q, p] = rows_ref[x, p, pl.ds(q, 8, stride=4), :]

        each(0, BRICK_X, split, 2)

    return split_rows


def source_on(c_ref, b_ref, g_ref, start, count, mask):
    weight = mask * (0.2 / 12.0)

    def body(i):
        x = start + i
        here = FINE.load(c_ref, x)
        sums = along_z(here, 1, True)
        plane = []
        for q in range(4):
            y_sums = along_y(here[q], 1)
            line = []
            for p in range(4):
                face = (c_ref[x - 1, q, p] + c_ref[x + 1, q, p]) + (sums[q][p] + y_sums[p])
                line.append((here[q][p] * 6.0 + face) * weight)
            plane.append(line)
        FINE.put(b_ref, g_ref, x, plane)

    each(0, count, body, 4)


def first_sweep_on(b_ref, g_ref, u_ref, h_ref, start, count, mask):
    weight = mask * (1.0 / 30.0)

    def body(i):
        x = start + i
        FINE.put(u_ref, h_ref, x, FINE.sweep(b_ref, g_ref, b_ref, x, weight))

    each(0, count, body, 4)


def early_kernel(count_x, count_z, where_ref, mid_ref, mid_rim_ref, near_ref, far_ref, c_ref,
                 b_ref, g_ref, u_ref, h_ref, lanes_ref, rows_ref):
    inner = rim_masks(count_x, count_z, where_ref)[0]
    odd = where_ref[0] % 2
    for p, tile in enumerate(split_lanes(near_ref[...])):
        lanes_ref[:, p] = tile
    split_rows = row_splitter(rows_ref, c_ref)
    split_rows(mid_ref, mid_rim_ref, 1)
    split_rows(lanes_ref, mid_rim_ref, 2 - 2 * odd)
    split_rows(far_ref, mid_rim_ref, 2 * odd)
    source_on(c_ref, b_ref, g_ref, 9, 6, inner)
    first_sweep_on(b_ref, g_ref, u_ref, h_ref, 10, 4, inner)


def down_kernel(count_x, count_z, where_ref, near_rim_ref, far_rim_ref, c_in, b_in, g_in, u_in, h_in,
                c_ref, b_ref, g_ref, u_ref, h_ref, out_ref):
    del c_in, b_in, g_in, u_in, h_in
    inner, below, above = rim_masks(count_x, count_z, where_ref)
    odd = where_ref[0] % 2
    far = inner * jnp.where(odd == 0, below, above)
    first = row_of((8, LANES)) < 4

    def join_rows(rim_ref, start):
        def join_plane(i):
            for p in range(4):
                for q in range(4):
                    rim = rim_ref[i, p, pl.ds(q, 4, stride=4), :]
                    rim = jnp.concatenate([rim, rim], axis=0)
                    c_ref[start + i, q, p] = jnp.where(first, c_ref[start + i, q, p], rim)

        each(0, BRICK_X, join_plane, 2)

    join_rows(near_rim_ref, 2 * BRICK_X * (1 - odd))
    join_rows(far_rim_ref, 2 * BRICK_X * odd)
    source_on(c_ref, b_ref, g_ref, 1 + 15 * odd, 7, far)
    source_on(c_ref, b_ref, g_ref, 16 - 15 * odd, 7, inner)
    source_on(c_ref, b_ref, g_ref, 8, 1, inner)
    source_on(c_ref, b_ref, g_ref, 15, 1, inner)
    first_sweep_on(b_ref, g_ref, u_ref, h_ref, 2 + 14 * odd, 6, far)
    first_sweep_on(b_ref, g_ref, u_ref, h_ref, 16 - 14 * odd, 6, inner)
    first_sweep_on(b_ref, g_ref, u_ref, h_ref, 8, 2, inner)
    first_sweep_on(b_ref, g_ref, u_ref, h_ref, 14, 2, inner)
    send_residual(u_ref, h_ref, b_ref, out_ref)


def middle_kernel(count_x, count_z, count_pieces, where_ref, *refs):
    pieces, refs = refs[:count_pieces], refs[count_pieces:]
    u_ref, b_ref, v_ref, out_ref, ga_ref, gb_ref, ua_ref, *grids = refs
    masks = rim_masks(count_x, count_z, where_ref)
    coarse_solve(count_x, count_z, where_ref, pieces, grids)
    coarse_ref = coarse_finish(count_x, where_ref, grids)
    at_x, at_z = where_ref[0], where_ref[1]

    def error_of(i):
        plane = LEVEL_1.load(coarse_ref, 4 * at_x + i)
        return [[turned_tile(t, at_z, masks[0]) for t in line] for line in plane]

    add_correction(error_of, u_ref, v_ref, ga_ref, 2)
    fine_sweep(v_ref, ga_ref, ua_ref, gb_ref, b_ref, 3, masks)
    fine_sweep(ua_ref, gb_ref, v_ref, ga_ref, b_ref, 4, masks)
    fine_sweep(v_ref, ga_ref, ua_ref, gb_ref, b_ref, 5, masks)
    fine_sweep(ua_ref, gb_ref, v_ref, ga_ref, b_ref, 6, masks)
    send_residual(v_ref, ga_ref, b_ref, out_ref)


def up_kernel(count_x, count_z, count_pieces, where_ref, *refs):
    pieces, refs = refs[:count_pieces], refs[count_pieces:]
    u_ref, b_ref, out_ref, ga_ref, gb_ref, ua_ref, ub_ref, rows_ref, *refs = refs
    near, grids = refs[:5], refs[5:]
    masks = rim_masks(count_x, count_z, where_ref)
    coarse = coarse_solve(count_x, count_z, where_ref, pieces, grids)
    error_ref = near_finish(coarse, where_ref, masks, near)
    add_correction(lambda i: NEAR_1.load(error_ref, i), u_ref, ua_ref, ga_ref, 6)
    fine_sweep(ua_ref, ga_ref, ub_ref, gb_ref, b_ref, 7, masks)

    def body(x):
        plane = FINE.sweep(ub_ref, gb_ref, b_ref, x, 1.0 / 30.0)
        for q in range(4):
            for p in range(4):
                rows_ref[x - RIM, p, pl.ds(q, 4, stride=4), :] = plane[q][p][0:4]

    each(RIM, RIM + BRICK_X, body, 2)
    tiles = [rows_ref[:, p].reshape(BRICK_X * BRICK_Z, LANES) for p in range(4)]
    matrix = places(out_ref.shape[2], lambda l, y: y == (l % LANES) * 4 + l // LANES)
    out_ref[...] = permuted(jnp.concatenate(tiles, axis=1), matrix).reshape(out_ref.shape)


def call(kernel, outputs, scratch, in_place=None):
    shapes = [jax.ShapeDtypeStruct(shape, jnp.float32) for shape in outputs]
    held = sum(4 * math.prod(shape.shape) for shape in scratch)

    def run(where, *arrays):
        moved = sum(4 * math.prod(array.shape) for array in arrays + tuple(shapes))
        whole = pl.BlockSpec(memory_space=pltpu.VMEM)
        return pl.pallas_call(
            kernel,
            out_shape=shapes,
            in_specs=[pl.BlockSpec(memory_space=pltpu.SMEM)] + [whole] * len(arrays),
            out_specs=[whole] * len(shapes),
            scratch_shapes=scratch,
            input_output_aliases=in_place or {},
            compiler_params=pltpu.CompilerParams(vmem_limit_bytes=held + moved + SPARE_BYTES),
        )(where, *arrays)

    return run


def pairs_apart(count, distance):
    return [(i, i ^ distance) for i in range(count)]


def pairs_shifted(count):
    pairs = [(i, i + 1) for i in range(1, count - 1, 2)]
    return pairs + [(target, source) for source, target in pairs]


def swap(axis, values, distance):
    return lax.ppermute(values, axis, pairs_apart(lax.axis_size(axis), distance))


def every_piece(piece):
    count_x, count_z = lax.axis_size("gx"), lax.axis_size("gz")
    line = [swap("gz", piece[None], count_z - 1 - n) for n in range(count_z - 1)] + [piece[None]]
    halves = [jnp.concatenate(half) for half in (line[: count_z // 2], line[count_z // 2 :])]
    held = jnp.concatenate(halves + [swap("gx", half, 2) for half in halves])
    distance = 4
    while distance < count_x:
        held = jnp.concatenate([held, swap("gx", held, distance)])
        distance *= 2
    return held, swap("gx", held, 1)


def per_device(charges):
    count_x, count_z = lax.axis_size("gx"), lax.axis_size("gz")
    at_x, at_z = lax.axis_index("gx"), lax.axis_index("gz")
    where = jnp.stack([at_x, at_z]).astype(jnp.int32)
    brick, rim = (BRICK_X, 4, BRICK_Z, LANES), (BRICK_X, 4, RIM, LANES)
    middle, one, two = call(lanes_kernel, [brick, rim, rim], [])(where, charges)
    x_far, z_two = pairs_shifted(count_x), pairs_shifted(count_z)
    far = lax.ppermute(middle, "gx", x_far)
    near = swap("gx", charges, 1)
    one, two = swap("gz", one, 1), lax.ppermute(two, "gz", z_two)
    even = at_z % 2 == 0
    middle_rim = jnp.concatenate([jnp.where(even, one, two), jnp.where(even, two, one)], axis=2)
    far_rim = lax.ppermute(middle_rim, "gx", x_far)
    near_rim = swap("gx", middle_rim, 1)

    wide = (WIDE_X, 4, 4, 8, LANES)
    piece_shape = (BRICK_X // 2, 2, 8, LANES)
    fine = pltpu.VMEM(wide, jnp.float32)
    grids = coarse_grids(count_x, count_z)
    rows_in = pltpu.VMEM((BRICK_X, 4, WIDE_Z, LANES), jnp.float32)
    close = pltpu.VMEM((WIDE_X // 2, 2, 2, 8, LANES), jnp.float32)
    rows_out = pltpu.VMEM((BRICK_X, 4, BRICK_Z, LANES), jnp.float32)

    early = call(
        functools.partial(early_kernel, count_x, count_z),
        [wide] * 5,
        [pltpu.VMEM(brick, jnp.float32), rows_in],
    )(where, middle, middle_rim, near, far)
    _, b, _, u, _, piece = call(
        functools.partial(down_kernel, count_x, count_z),
        [wide] * 5 + [piece_shape],
        [],
        in_place={3 + i: i for i in range(5)},
    )(where, near_rim, far_rim, *early)
    pieces = every_piece(piece)
    u, piece = call(
        functools.partial(middle_kernel, count_x, count_z, len(pieces)),
        [wide, piece_shape],
        [fine] * 3 + grids,
    )(where, *pieces, u, b)
    pieces = every_piece(piece)
    (potential,) = call(
        functools.partial(up_kernel, count_x, count_z, len(pieces)),
        [charges.shape],
        [fine] * 4 + [rows_out] + [close] * 5 + grids,
    )(where, *pieces, u, b)
    return potential


def solution(mesh):
    return jax.shard_map(
        per_device,
        mesh=mesh,
        in_specs=(P(("groups", "gx"), "gz", None),),
        out_specs=P(("groups", "gx"), "gz", None),
        check_vma=False,
    )
```

```python
import functools
import math

import jax
import jax.numpy as jnp
from jax import lax
from jax.experimental import pallas as pl
from jax.experimental.pallas import tpu as pltpu
from jax.sharding import PartitionSpec as P

COARSE_SWEEPS = 8
LANES = 128
RIM = 8
BRICK_X = 8
BRICK_Z = 16
WIDE_X = BRICK_X + 2 * RIM
WIDE_Z = BRICK_Z + 2 * RIM
SPARE_BYTES = 4 * 1024 * 1024


def lane_of(shape):
    return lax.broadcasted_iota(jnp.int32, shape, len(shape) - 1)


def row_of(shape):
    return lax.broadcasted_iota(jnp.int32, shape, len(shape) - 2)


def next_row(tile, step, cyclic):
    rows = tile.shape[0]
    moved = pltpu.roll(tile, rows - step, 0)
    return moved if cyclic else jnp.where(row_of(tile.shape) < rows - step, moved, 0.0)


def last_row(tile, step, cyclic):
    moved = pltpu.roll(tile, step, 0)
    return moved if cyclic else jnp.where(row_of(tile.shape) >= step, moved, 0.0)


def next_lane(tile, step):
    moved = pltpu.roll(tile, LANES - step, 1)
    return jnp.where(lane_of(tile.shape) < LANES - step, moved, 0.0)


def last_lane(tile, step):
    moved = pltpu.roll(tile, step, 1)
    return jnp.where(lane_of(tile.shape) >= step, moved, 0.0)


def load_plane(ref, x, count_q, count_p):
    return [[ref[x, q, p] for p in range(count_p)] for q in range(count_q)]


def store_plane(ref, x, plane):
    for q, line in enumerate(plane):
        for p, tile in enumerate(line):
            ref[x, q, p] = tile


def along_z(plane, step, cyclic):
    count_q, count_p = len(plane), len(plane[0])
    result = []
    for q in range(count_q):
        line = []
        for p in range(count_p):
            after = plane[q + 1][p] if q + 1 < count_q else next_row(plane[0][p], step, cyclic)
            before = plane[q - 1][p] if q > 0 else last_row(plane[-1][p], step, cyclic)
            line.append(after + before)
        result.append(line)
    return result


def along_y(line, step):
    count_p = len(line)
    result = []
    for p in range(count_p):
        after = line[p + 1] if p + 1 < count_p else next_lane(line[0], step)
        before = line[p - 1] if p > 0 else last_lane(line[-1], step)
        result.append(after + before)
    return result


class Level:
    def __init__(self, count_q, count_p, step, cyclic):
        self.count_q, self.count_p, self.step, self.cyclic = count_q, count_p, step, cyclic

    def load(self, ref, x):
        return load_plane(ref, x, self.count_q, self.count_p)

    def put(self, u_ref, g_ref, x, plane):
        store_plane(u_ref, x, plane)
        sums = along_z(plane, self.step, self.cyclic)
        store_plane(
            g_ref,
            x,
            [
                [s + (v + v) for s, v in zip(sum_line, line)]
                for sum_line, line in zip(sums, plane)
            ],
        )

    def spread(self, u_ref, g_ref, x, with_u):
        result = []
        for q in range(self.count_q):
            sides, both = [], []
            for p in range(self.count_p):
                here = g_ref[x, q, p]
                sides.append((u_ref[x - 1, q, p] + u_ref[x + 1, q, p]) + here)
                if with_u:
                    here = here + u_ref[x, q, p]
                both.append((g_ref[x - 1, q, p] + g_ref[x + 1, q, p]) + (here + here))
            result.append([a + b for a, b in zip(both, along_y(sides, self.step))])
        return result

    def sweep(self, u_ref, g_ref, b_ref, x, weight):
        wide = self.spread(u_ref, g_ref, x, True)
        return [
            [b_ref[x, q, p] + wide[q][p] * weight for p in range(self.count_p)]
            for q in range(self.count_q)
        ]

    def residual(self, u_ref, g_ref, b_ref, x):
        wide = self.spread(u_ref, g_ref, x, False)
        return [
            [
                b_ref[x, q, p] * 5.0 + (wide[q][p] - u_ref[x, q, p] * 28.0) * (1.0 / 6.0)
                for p in range(self.count_p)
            ]
            for q in range(self.count_q)
        ]


class Held:
    def __init__(self, rows, zero_at=()):
        self.tiles = {(x, 0, 0): jnp.zeros((rows, LANES), jnp.float32) for x in zero_at}

    def __getitem__(self, place):
        return self.tiles[place]

    def __setitem__(self, place, tile):
        self.tiles[place] = tile


def add_planes(one, other):
    return [[a + b for a, b in zip(l, m)] for l, m in zip(one, other)]


def join(plane):
    lines = [[a + b for a, b in zip(plane[q], plane[q + 1])] for q in range(0, len(plane), 2)]
    return [[line[p] + line[p + 1] for p in range(0, len(line), 2)] for line in lines]


def join_within(tile):
    rows = tile.shape[0]
    even = row_of(tile.shape) % 2 == 0
    tile = tile + jnp.where(even, pltpu.roll(tile, rows - 1, 0), pltpu.roll(tile, 1, 0))
    even = lane_of(tile.shape) % 2 == 0
    return tile + jnp.where(even, pltpu.roll(tile, LANES - 1, 1), pltpu.roll(tile, 1, 1))


def scaled(plane, factor):
    return [[tile * factor for tile in line] for line in plane]


def each(lo, hi, body, chunk):
    count = hi - lo
    whole = count // chunk
    if whole == 1:
        for x in range(lo, lo + chunk):
            body(x)
    elif whole > 1:

        def step(i, carry):
            for d in range(chunk):
                body(lo + i * chunk + d)
            return carry

        lax.fori_loop(0, whole, step, 0)
    for x in range(lo + whole * chunk, hi):
        body(x)


FINE = Level(4, 4, 1, True)
LEVEL_1 = Level(2, 2, 1, False)
NEAR_1 = Level(2, 2, 1, True)
LEVEL_2 = Level(1, 1, 1, False)
LEVEL_3 = Level(1, 1, 2, False)
PAD = RIM // 2
PAD_2 = RIM // 4


def zero_planes(ref, indices):
    for x in indices:
        ref[x] = jnp.zeros(ref.shape[1:], ref.dtype)


def coarse_grids(count_x, count_z):
    rows = count_z * BRICK_Z // 4
    shapes = []
    for planes, count in ((4 * count_x + 2 * PAD, 2), (2 * count_x + 2 * PAD_2, 1)):
        shapes += [pltpu.VMEM((planes, count, count, rows, LANES), jnp.float32)] * 5
    return shapes


def coarse_solve(count_x, count_z, where_ref, pieces, grids):
    ua1, ub1, ga1, gb1, b1 = grids[0:5]
    kept_2 = grids[5]
    size_1, size_2, size_3 = 4 * count_x, 2 * count_x, count_x
    rows = b1.shape[3]

    def ends(pad, size):
        return list(range(pad)) + list(range(pad + size, pad + size + pad))

    for ref in (ua1, ub1, ga1, gb1, b1):
        zero_planes(ref, ends(PAD, size_1))
    zero_planes(kept_2, ends(PAD_2, size_2))
    if size_2 <= 8:
        step_2 = size_2
        ua2, ub2, ga2, gb2, b2 = (Held(rows, ends(PAD_2, size_2)) for _ in range(5))
    else:
        step_2 = 8
        ua2, ub2, ga2, gb2, b2 = grids[5:10]
        for ref in (ub2, ga2, gb2):
            zero_planes(ref, ends(PAD_2, size_2))
    ua3, ub3, ga3, gb3, b3 = (Held(rows, ends(1, size_3)) for _ in range(5))
    third = 1.0 / 30.0

    at_x, at_z = where_ref[0], where_ref[1]

    def place(x, load):
        for i in range(4):
            plane = []
            for q in range(2):
                even, odd = [], []
                for z in range(0, count_z, 2):
                    one, two = load(z, i, q), load(z + 1, i, q)
                    first = row_of(one.shape) < 4
                    even.append(jnp.where(first, one, pltpu.roll(two, 4, 0)))
                    odd.append(jnp.where(first, pltpu.roll(one, 4, 0), two))
                plane.append([jnp.concatenate(even, axis=0), jnp.concatenate(odd, axis=0)])
            LEVEL_1.put(b1, gb1, x + i, plane)

    if len(pieces) == 1:

        def gather(n):
            place(PAD + 4 * n, lambda z, i, q: pieces[0][n * count_z + z, i, q])

        each(0, count_x, gather, 1)
    else:

        def gather(n):
            for core in range(2):
                x = PAD + 4 * ((2 * n + core) ^ at_x)
                place(x, lambda z, i, q: pieces[core][n * count_z + (z ^ at_z ^ (count_z - 1)), i, q])

        each(0, count_x // 2, gather, 2)

    def sweep(level, u_in, g_in, u_out, g_out, b):
        return lambda x: level.put(u_out, g_out, x, level.sweep(u_in, g_in, b, x, third))

    each(PAD, PAD + size_1, sweep(LEVEL_1, b1, gb1, ua1, ga1, b1), 16)

    def restrict_1(x):
        fine = PAD + 2 * x
        pair = add_planes(
            LEVEL_1.residual(ua1, ga1, b1, fine), LEVEL_1.residual(ua1, ga1, b1, fine + 1)
        )
        plane = scaled(join(pair), 0.5 * 0.2)
        store_plane(b2, PAD_2 + x, plane)
        LEVEL_2.put(ub2, gb2, PAD_2 + x, plane)

    each(0, size_2, restrict_1, step_2)
    all_2 = (PAD_2, PAD_2 + size_2)
    each(*all_2, sweep(LEVEL_2, ub2, gb2, ua2, ga2, b2), step_2)

    def restrict_2(x):
        fine = PAD_2 + 2 * x
        pair = add_planes(
            LEVEL_2.residual(ua2, ga2, b2, fine), LEVEL_2.residual(ua2, ga2, b2, fine + 1)
        )
        plane = [[join_within(pair[0][0]) * (0.5 * 0.2)]]
        store_plane(b3, 1 + x, plane)
        LEVEL_3.put(ub3, gb3, 1 + x, plane)

    each(0, size_3, restrict_2, size_3)
    now, later = (ub3, gb3), (ua3, ga3)
    for _ in range(COARSE_SWEEPS - 1):
        each(1, 1 + size_3, sweep(LEVEL_3, *now, *later, b3), size_3)
        now, later = later, now

    def prolong_3(x):
        for d in range(2):
            fine = PAD_2 + 2 * x + d
            LEVEL_2.put(ua2, ga2, fine, [[ua2[fine, 0, 0] + now[0][1 + x, 0, 0]]])

    each(0, size_3, prolong_3, size_3)
    each(*all_2, sweep(LEVEL_2, ua2, ga2, ub2, gb2, b2), step_2)

    def last_sweep(x):
        store_plane(kept_2, x, LEVEL_2.sweep(ub2, gb2, b2, x, third))

    each(*all_2, last_sweep, step_2)
    return ua1, kept_2, b1


def coarse_finish(count_x, where_ref, grids):
    ua1, ub1, ga1, gb1, b1 = grids[0:5]
    ua2 = grids[5]
    size_1, size_2 = 4 * count_x, 2 * count_x
    third = 1.0 / 30.0

    def prolong_2(x):
        error = ua2[PAD_2 + x, 0, 0]
        for d in range(2):
            fine = PAD + 2 * x + d
            LEVEL_1.put(
                ua1, ga1, fine, [[t + error for t in line] for line in LEVEL_1.load(ua1, fine)]
            )

    def window(rim):
        count = min(BRICK_X // 2 + 2 * rim, size_1)
        return PAD + jnp.clip(4 * where_ref[0] - rim, 0, size_1 - count), count

    start, count = window(4)

    def sweep(i):
        x = start + i
        LEVEL_1.put(ub1, gb1, x, LEVEL_1.sweep(ua1, ga1, b1, x, third))

    last_start, last_count = window(3)

    def last_sweep(i):
        x = last_start + i
        store_plane(ua1, x, LEVEL_1.sweep(ub1, gb1, b1, x, third))

    each(0, size_2, prolong_2, 8)
    each(0, count, sweep, 12)
    each(0, last_count, last_sweep, 10)
    return ua1


def turned_tile(tile, at_z, rows):
    count = tile.shape[0]
    turned = pltpu.roll(tile, lax.rem(count - 4 * at_z, count), 0)
    return jnp.where(row_of((8, LANES)) < 6, turned[0:8], turned[count - 8 : count]) * rows


def near_finish(coarse, where_ref, masks, near):
    ua1, ua2, b1 = coarse
    ua, ga, ub, gb, b = near
    at_x, at_z = where_ref[0], where_ref[1]
    rows = masks[0]

    def take(i):
        error = ua2[2 * at_x + i // 2, 0, 0]
        plane = [[t + error for t in line] for line in LEVEL_1.load(ua1, 4 * at_x + i)]
        plane = [[turned_tile(t, at_z, rows) for t in line] for line in plane]
        NEAR_1.put(ua, ga, i, plane)
        plane = LEVEL_1.load(b1, 4 * at_x + i)
        store_plane(b, i, [[turned_tile(t, at_z, rows) for t in line] for line in plane])

    each(1, 11, take, 5)

    def sweep(i, weight):
        NEAR_1.put(ub, gb, i, NEAR_1.sweep(ua, ga, b, i, weight))

    def last_sweep(i, weight):
        store_plane(ua, i, NEAR_1.sweep(ub, gb, b, i, weight))

    in_segments(2, 10, sweep, masks, 1.0 / 30.0, 4, PAD, BRICK_X // 2)
    in_segments(3, 9, last_sweep, masks, 1.0 / 30.0, 4, PAD, BRICK_X // 2)
    return ua


def rim_masks(count_x, count_z, where_ref):
    at_x, at_z = where_ref[0], where_ref[1]
    k = row_of((8, LANES))
    low = (at_z > 0).astype(jnp.float32)
    high = (at_z < count_z - 1).astype(jnp.float32)
    rows = jnp.where(k < 4, 1.0, jnp.where(k < 6, high, low))
    below = (at_x > 0).astype(jnp.float32)
    above = (at_x < count_x - 1).astype(jnp.float32)
    return rows, below, above


def in_segments(lo, hi, body, masks, scale, chunk, rim=RIM, brick=BRICK_X):
    rows, below, above = masks
    inner = rows * scale
    for start, end, weight in (
        (lo, min(hi, rim), inner * below),
        (max(lo, rim), min(hi, rim + brick), inner),
        (max(lo, rim + brick), hi, inner * above),
    ):
        if end > start:
            each(start, end, functools.partial(body, weight=weight), chunk)


def fine_sweep(u_in, g_in, u_out, g_out, b_ref, margin, masks):
    def body(x, weight):
        FINE.put(u_out, g_out, x, FINE.sweep(u_in, g_in, b_ref, x, weight))

    in_segments(margin, WIDE_X - margin, body, masks, 1.0 / 30.0, 4)


def add_correction(error_of, u_in, u_out, g_out, margin):
    def body(i):
        error = error_of(i)
        for d in range(2):
            x = 2 * i + d
            plane = [
                [u_in[x, q, p] + error[q // 2][p // 2] for p in range(4)] for q in range(4)
            ]
            FINE.put(u_out, g_out, x, plane)

    each(margin // 2, (WIDE_X - margin) // 2, body, 2)


def send_residual(u_ref, g_ref, b_ref, out_ref):
    def body(i):
        x = RIM + 2 * i
        pair = add_planes(
            FINE.residual(u_ref, g_ref, b_ref, x), FINE.residual(u_ref, g_ref, b_ref, x + 1)
        )
        for q, (even, odd) in enumerate(join(pair)):
            out_ref[i, q] = 0.1 * jnp.where(row_of(even.shape) < 4, even, pltpu.roll(odd, 4, 0))

    each(0, BRICK_X // 2, body, BRICK_X // 2)


def places(size, joins):
    row, column = (lax.broadcasted_iota(jnp.int32, (size, size), d) for d in range(2))
    return joins(row, column).astype(jnp.float32).astype(jnp.bfloat16)


def permuted(values, matrix):
    rest, terms = values, []
    for _ in range(3):
        term = rest.astype(jnp.bfloat16)
        rest = rest - term.astype(jnp.float32)
        terms.append(jnp.dot(term, matrix, preferred_element_type=jnp.float32))
    return terms[0] + (terms[1] + terms[2])


def lane_places(size):
    return places(size, lambda y, l: y == (l % LANES) * 4 + l // LANES)


def split_lanes(values, matrix):
    size_x, size_z, size_y = values.shape
    split = permuted(values.reshape(size_x * size_z, size_y), matrix)
    return [
        split[:, p * LANES : (p + 1) * LANES].reshape(size_x, size_z, LANES) for p in range(4)
    ]


def lanes_kernel(where_ref, charges_ref, rows_ref, one_ref, two_ref, held_ref, semaphore):
    copy = pltpu.make_async_copy(charges_ref, held_ref, semaphore)
    copy.start()
    odd = where_ref[1] % 2
    matrix = lane_places(charges_ref.shape[2])
    copy.wait()
    for p, tile in enumerate(split_lanes(held_ref[...], matrix)):
        rows_ref[:, p] = tile
        first, last = tile[:, 0:8], tile[:, 8:16]
        one_ref[:, p] = jnp.where(odd == 0, last, first)
        two_ref[:, p] = jnp.where(odd == 0, first, last)


def row_splitter(rows_ref, c_ref):
    def split_rows(ref, rim_ref, part):
        def split(x):
            for p in range(4):
                rows_ref[x, p, 0:BRICK_Z] = ref[x, p]
                rows_ref[x, p, BRICK_Z:WIDE_Z] = rim_ref[x, p]
                for q in range(4):
                    c_ref[part * BRICK_X + x, q, p] = rows_ref[x, p, pl.ds(q, 8, stride=4), :]

        each(0, BRICK_X, split, 2)

    return split_rows


def source_on(c_ref, b_ref, g_ref, start, count, mask):
    weight = mask * (0.2 / 12.0)

    def body(i):
        x = start + i
        here = FINE.load(c_ref, x)
        sums = along_z(here, 1, True)
        plane = []
        for q in range(4):
            y_sums = along_y(here[q], 1)
            line = []
            for p in range(4):
                face = (c_ref[x - 1, q, p] + c_ref[x + 1, q, p]) + (sums[q][p] + y_sums[p])
                line.append((here[q][p] * 6.0 + face) * weight)
            plane.append(line)
        FINE.put(b_ref, g_ref, x, plane)

    each(0, count, body, 4)


def first_sweep_on(b_ref, g_ref, u_ref, h_ref, start, count, mask):
    weight = mask * (1.0 / 30.0)

    def body(i):
        x = start + i
        FINE.put(u_ref, h_ref, x, FINE.sweep(b_ref, g_ref, b_ref, x, weight))

    each(0, count, body, 4)


def early_kernel(count_x, count_z, where_ref, mid_ref, mid_rim_ref, near_ref, far_ref, c_ref,
                 b_ref, g_ref, u_ref, h_ref, matrix_ref, lanes_ref, rows_ref):
    inner = rim_masks(count_x, count_z, where_ref)[0]
    odd = where_ref[0] % 2
    size = near_ref.shape[2]
    for p, tile in enumerate(split_lanes(near_ref[...], lane_places(size))):
        lanes_ref[:, p] = tile
    matrix_ref[...] = places(size, lambda l, y: y == (l % LANES) * 4 + l // LANES)
    split_rows = row_splitter(rows_ref, c_ref)
    split_rows(mid_ref, mid_rim_ref, 1)
    split_rows(lanes_ref, mid_rim_ref, 2 - 2 * odd)
    split_rows(far_ref, mid_rim_ref, 2 * odd)
    source_on(c_ref, b_ref, g_ref, 9, 6, inner)
    first_sweep_on(b_ref, g_ref, u_ref, h_ref, 10, 4, inner)


def down_kernel(count_x, count_z, where_ref, near_rim_ref, far_rim_ref, c_in, b_in, g_in, u_in, h_in,
                c_ref, b_ref, g_ref, u_ref, h_ref, out_ref):
    del c_in, b_in, g_in, u_in, h_in
    inner, below, above = rim_masks(count_x, count_z, where_ref)
    odd = where_ref[0] % 2
    far = inner * jnp.where(odd == 0, below, above)
    first = row_of((8, LANES)) < 4

    def join_rows(rim_ref, start):
        def join_plane(i):
            for p in range(4):
                for q in range(4):
                    rim = rim_ref[i, p, pl.ds(q, 4, stride=4), :]
                    rim = jnp.concatenate([rim, rim], axis=0)
                    c_ref[start + i, q, p] = jnp.where(first, c_ref[start + i, q, p], rim)

        each(0, BRICK_X, join_plane, 2)

    join_rows(near_rim_ref, 2 * BRICK_X * (1 - odd))
    join_rows(far_rim_ref, 2 * BRICK_X * odd)
    source_on(c_ref, b_ref, g_ref, 1 + 15 * odd, 7, far)
    source_on(c_ref, b_ref, g_ref, 16 - 15 * odd, 7, inner)
    source_on(c_ref, b_ref, g_ref, 8, 1, inner)
    source_on(c_ref, b_ref, g_ref, 15, 1, inner)
    first_sweep_on(b_ref, g_ref, u_ref, h_ref, 2 + 14 * odd, 6, far)
    first_sweep_on(b_ref, g_ref, u_ref, h_ref, 16 - 14 * odd, 6, inner)
    first_sweep_on(b_ref, g_ref, u_ref, h_ref, 8, 2, inner)
    first_sweep_on(b_ref, g_ref, u_ref, h_ref, 14, 2, inner)
    send_residual(u_ref, h_ref, b_ref, out_ref)


def middle_kernel(count_x, count_z, count_pieces, where_ref, *refs):
    pieces, refs = refs[:count_pieces], refs[count_pieces:]
    u_ref, b_ref, v_ref, out_ref, ga_ref, gb_ref, ua_ref, *grids = refs
    masks = rim_masks(count_x, count_z, where_ref)
    coarse_solve(count_x, count_z, where_ref, pieces, grids)
    coarse_ref = coarse_finish(count_x, where_ref, grids)
    at_x, at_z = where_ref[0], where_ref[1]

    def error_of(i):
        plane = LEVEL_1.load(coarse_ref, 4 * at_x + i)
        return [[turned_tile(t, at_z, masks[0]) for t in line] for line in plane]

    add_correction(error_of, u_ref, v_ref, ga_ref, 2)
    fine_sweep(v_ref, ga_ref, ua_ref, gb_ref, b_ref, 3, masks)
    fine_sweep(ua_ref, gb_ref, v_ref, ga_ref, b_ref, 4, masks)
    fine_sweep(v_ref, ga_ref, ua_ref, gb_ref, b_ref, 5, masks)
    fine_sweep(ua_ref, gb_ref, v_ref, ga_ref, b_ref, 6, masks)
    send_residual(v_ref, ga_ref, b_ref, out_ref)


def up_kernel(count_x, count_z, count_pieces, where_ref, *refs):
    pieces, refs = refs[:count_pieces], refs[count_pieces:]
    u_ref, b_ref, matrix_ref, out_ref, ga_ref, gb_ref, ua_ref, ub_ref, rows_ref, *refs = refs
    near, grids = refs[:5], refs[5:]
    masks = rim_masks(count_x, count_z, where_ref)
    coarse = coarse_solve(count_x, count_z, where_ref, pieces, grids)
    error_ref = near_finish(coarse, where_ref, masks, near)
    add_correction(lambda i: NEAR_1.load(error_ref, i), u_ref, ua_ref, ga_ref, 6)
    fine_sweep(ua_ref, ga_ref, ub_ref, gb_ref, b_ref, 7, masks)

    def body(x):
        plane = FINE.sweep(ub_ref, gb_ref, b_ref, x, 1.0 / 30.0)
        for q in range(4):
            for p in range(4):
                rows_ref[x - RIM, p, pl.ds(q, 4, stride=4), :] = plane[q][p][0:4]

    each(RIM, RIM + BRICK_X, body, 2)
    tiles = [rows_ref[:, p].reshape(BRICK_X * BRICK_Z, LANES) for p in range(4)]
    whole = permuted(jnp.concatenate(tiles, axis=1), matrix_ref[...])
    out_ref[...] = whole.reshape(out_ref.shape)


def call(kernel, outputs, scratch, in_place=None, far_in=False):
    shapes = [
        shape if hasattr(shape, "dtype") else jax.ShapeDtypeStruct(shape, jnp.float32)
        for shape in outputs
    ]
    held = sum(4 * math.prod(shape.shape) for shape in scratch if hasattr(shape, "shape"))

    def run(where, *arrays):
        moved = sum(4 * math.prod(array.shape) for array in arrays + tuple(shapes))
        whole = pl.BlockSpec(memory_space=pltpu.VMEM)
        return pl.pallas_call(
            kernel,
            out_shape=shapes,
            in_specs=[pl.BlockSpec(memory_space=pltpu.SMEM)]
            + [pl.BlockSpec(memory_space=pltpu.HBM) if far_in else whole] * len(arrays),
            out_specs=[whole] * len(shapes),
            scratch_shapes=scratch,
            input_output_aliases=in_place or {},
            compiler_params=pltpu.CompilerParams(vmem_limit_bytes=held + moved + SPARE_BYTES),
        )(where, *arrays)

    return run


def pairs_apart(count, distance):
    return [(i, i ^ distance) for i in range(count)]


def pairs_shifted(count):
    pairs = [(i, i + 1) for i in range(1, count - 1, 2)]
    return pairs + [(target, source) for source, target in pairs]


def swap(axis, values, distance):
    return lax.ppermute(values, axis, pairs_apart(lax.axis_size(axis), distance))


def every_piece(piece):
    count_x, count_z = lax.axis_size("gx"), lax.axis_size("gz")
    line = [swap("gz", piece[None], count_z - 1 - n) for n in range(count_z - 1)] + [piece[None]]
    halves = [jnp.concatenate(half) for half in (line[: count_z // 2], line[count_z // 2 :])]
    held = jnp.concatenate(halves + [swap("gx", half, 2) for half in halves])
    distance = 4
    while distance < count_x:
        held = jnp.concatenate([held, swap("gx", held, distance)])
        distance *= 2
    return held, swap("gx", held, 1)


def per_device(charges):
    count_x, count_z = lax.axis_size("gx"), lax.axis_size("gz")
    at_x, at_z = lax.axis_index("gx"), lax.axis_index("gz")
    where = jnp.stack([at_x, at_z]).astype(jnp.int32)
    brick, rim = (BRICK_X, 4, BRICK_Z, LANES), (BRICK_X, 4, RIM, LANES)
    middle, one, two = call(
        lanes_kernel,
        [brick, rim, rim],
        [pltpu.VMEM(charges.shape, jnp.float32), pltpu.SemaphoreType.DMA],
        far_in=True,
    )(where, charges)
    x_far, z_two = pairs_shifted(count_x), pairs_shifted(count_z)
    far = lax.ppermute(middle, "gx", x_far)
    near = swap("gx", charges, 1)
    one, two = swap("gz", one, 1), lax.ppermute(two, "gz", z_two)
    even = at_z % 2 == 0
    middle_rim = jnp.concatenate([jnp.where(even, one, two), jnp.where(even, two, one)], axis=2)
    far_rim = lax.ppermute(middle_rim, "gx", x_far)
    near_rim = swap("gx", middle_rim, 1)

    wide = (WIDE_X, 4, 4, 8, LANES)
    piece_shape = (BRICK_X // 2, 2, 8, LANES)
    fine = pltpu.VMEM(wide, jnp.float32)
    grids = coarse_grids(count_x, count_z)
    rows_in = pltpu.VMEM((BRICK_X, 4, WIDE_Z, LANES), jnp.float32)
    close = pltpu.VMEM((WIDE_X // 2, 2, 2, 8, LANES), jnp.float32)
    rows_out = pltpu.VMEM((BRICK_X, 4, BRICK_Z, LANES), jnp.float32)

    size = charges.shape[2]
    *early, matrix = call(
        functools.partial(early_kernel, count_x, count_z),
        [wide] * 5 + [jax.ShapeDtypeStruct((size, size), jnp.bfloat16)],
        [pltpu.VMEM(brick, jnp.float32), rows_in],
    )(where, middle, middle_rim, near, far)
    _, b, _, u, _, piece = call(
        functools.partial(down_kernel, count_x, count_z),
        [wide] * 5 + [piece_shape],
        [],
        in_place={3 + i: i for i in range(5)},
    )(where, near_rim, far_rim, *early)
    pieces = every_piece(piece)
    u, piece = call(
        functools.partial(middle_kernel, count_x, count_z, len(pieces)),
        [wide, piece_shape],
        [fine] * 3 + grids,
    )(where, *pieces, u, b)
    pieces = every_piece(piece)
    (potential,) = call(
        functools.partial(up_kernel, count_x, count_z, len(pieces)),
        [charges.shape],
        [fine] * 4 + [rows_out] + [close] * 5 + grids,
    )(where, *pieces, u, b, matrix)
    return potential


def solution(mesh):
    return jax.shard_map(
        per_device,
        mesh=mesh,
        in_specs=(P(("groups", "gx"), "gz", None),),
        out_specs=P(("groups", "gx"), "gz", None),
        check_vma=False,
    )
```

```python
import functools
import math

import jax
import jax.numpy as jnp
from jax import lax
from jax.experimental import pallas as pl
from jax.experimental.pallas import tpu as pltpu
from jax.sharding import PartitionSpec as P

COARSE_SWEEPS = 8
LANES = 128
RIM = 8
BRICK_X = 8
BRICK_Z = 16
WIDE_X = BRICK_X + 2 * RIM
WIDE_Z = BRICK_Z + 2 * RIM
SPARE_BYTES = 4 * 1024 * 1024


def lane_of(shape):
    return lax.broadcasted_iota(jnp.int32, shape, len(shape) - 1)


def row_of(shape):
    return lax.broadcasted_iota(jnp.int32, shape, len(shape) - 2)


def next_row(tile, step, cyclic):
    rows = tile.shape[0]
    moved = pltpu.roll(tile, rows - step, 0)
    return moved if cyclic else jnp.where(row_of(tile.shape) < rows - step, moved, 0.0)


def last_row(tile, step, cyclic):
    moved = pltpu.roll(tile, step, 0)
    return moved if cyclic else jnp.where(row_of(tile.shape) >= step, moved, 0.0)


def next_lane(tile, step):
    moved = pltpu.roll(tile, LANES - step, 1)
    return jnp.where(lane_of(tile.shape) < LANES - step, moved, 0.0)


def last_lane(tile, step):
    moved = pltpu.roll(tile, step, 1)
    return jnp.where(lane_of(tile.shape) >= step, moved, 0.0)


def load_plane(ref, x, count_q, count_p):
    return [[ref[x, q, p] for p in range(count_p)] for q in range(count_q)]


def store_plane(ref, x, plane):
    for q, line in enumerate(plane):
        for p, tile in enumerate(line):
            ref[x, q, p] = tile


def along_z(plane, step, cyclic):
    count_q, count_p = len(plane), len(plane[0])
    result = []
    for q in range(count_q):
        line = []
        for p in range(count_p):
            after = plane[q + 1][p] if q + 1 < count_q else next_row(plane[0][p], step, cyclic)
            before = plane[q - 1][p] if q > 0 else last_row(plane[-1][p], step, cyclic)
            line.append(after + before)
        result.append(line)
    return result


def along_y(line, step):
    count_p = len(line)
    result = []
    for p in range(count_p):
        after = line[p + 1] if p + 1 < count_p else next_lane(line[0], step)
        before = line[p - 1] if p > 0 else last_lane(line[-1], step)
        result.append(after + before)
    return result


class Level:
    def __init__(self, count_q, count_p, step, cyclic):
        self.count_q, self.count_p, self.step, self.cyclic = count_q, count_p, step, cyclic

    def load(self, ref, x):
        return load_plane(ref, x, self.count_q, self.count_p)

    def put(self, u_ref, g_ref, x, plane):
        store_plane(u_ref, x, plane)
        sums = along_z(plane, self.step, self.cyclic)
        store_plane(
            g_ref,
            x,
            [
                [s + (v + v) for s, v in zip(sum_line, line)]
                for sum_line, line in zip(sums, plane)
            ],
        )

    def spread(self, u_ref, g_ref, x, with_u):
        result = []
        for q in range(self.count_q):
            sides, both = [], []
            for p in range(self.count_p):
                here = g_ref[x, q, p]
                sides.append((u_ref[x - 1, q, p] + u_ref[x + 1, q, p]) + here)
                if with_u:
                    here = here + u_ref[x, q, p]
                both.append((g_ref[x - 1, q, p] + g_ref[x + 1, q, p]) + (here + here))
            result.append([a + b for a, b in zip(both, along_y(sides, self.step))])
        return result

    def sweep(self, u_ref, g_ref, b_ref, x, weight):
        wide = self.spread(u_ref, g_ref, x, True)
        return [
            [b_ref[x, q, p] + wide[q][p] * weight for p in range(self.count_p)]
            for q in range(self.count_q)
        ]

    def residual(self, u_ref, g_ref, b_ref, x):
        wide = self.spread(u_ref, g_ref, x, False)
        return [
            [
                b_ref[x, q, p] * 5.0 + (wide[q][p] - u_ref[x, q, p] * 28.0) * (1.0 / 6.0)
                for p in range(self.count_p)
            ]
            for q in range(self.count_q)
        ]


class Held:
    def __init__(self, rows, zero_at=()):
        self.tiles = {(x, 0, 0): jnp.zeros((rows, LANES), jnp.float32) for x in zero_at}

    def __getitem__(self, place):
        return self.tiles[place]

    def __setitem__(self, place, tile):
        self.tiles[place] = tile


def add_planes(one, other):
    return [[a + b for a, b in zip(l, m)] for l, m in zip(one, other)]


def join(plane):
    lines = [[a + b for a, b in zip(plane[q], plane[q + 1])] for q in range(0, len(plane), 2)]
    return [[line[p] + line[p + 1] for p in range(0, len(line), 2)] for line in lines]


def join_within(tile):
    rows = tile.shape[0]
    even = row_of(tile.shape) % 2 == 0
    tile = tile + jnp.where(even, pltpu.roll(tile, rows - 1, 0), pltpu.roll(tile, 1, 0))
    even = lane_of(tile.shape) % 2 == 0
    return tile + jnp.where(even, pltpu.roll(tile, LANES - 1, 1), pltpu.roll(tile, 1, 1))


def scaled(plane, factor):
    return [[tile * factor for tile in line] for line in plane]


def each(lo, hi, body, chunk):
    count = hi - lo
    whole = count // chunk
    if whole == 1:
        for x in range(lo, lo + chunk):
            body(x)
    elif whole > 1:

        def step(i, carry):
            for d in range(chunk):
                body(lo + i * chunk + d)
            return carry

        lax.fori_loop(0, whole, step, 0)
    for x in range(lo + whole * chunk, hi):
        body(x)


FINE = Level(4, 4, 1, True)
LEVEL_1 = Level(2, 2, 1, False)
NEAR_1 = Level(2, 2, 1, True)
LEVEL_2 = Level(1, 1, 1, False)
LEVEL_3 = Level(1, 1, 2, False)
PAD = RIM // 2
PAD_2 = RIM // 4


def zero_planes(ref, indices):
    for x in indices:
        ref[x] = jnp.zeros(ref.shape[1:], ref.dtype)


def coarse_grids(count_x, count_z):
    rows = count_z * BRICK_Z // 4
    shapes = []
    for planes, count in ((4 * count_x + 2 * PAD, 2), (2 * count_x + 2 * PAD_2, 1)):
        shapes += [pltpu.VMEM((planes, count, count, rows, LANES), jnp.float32)] * 5
    return shapes


def coarse_solve(count_x, count_z, where_ref, pieces, grids):
    ua1, ub1, ga1, gb1, b1 = grids[0:5]
    kept_2 = grids[5]
    size_1, size_2, size_3 = 4 * count_x, 2 * count_x, count_x
    rows = b1.shape[3]

    def ends(pad, size):
        return list(range(pad)) + list(range(pad + size, pad + size + pad))

    for ref in (ua1, ub1, ga1, gb1, b1):
        zero_planes(ref, ends(PAD, size_1))
    zero_planes(kept_2, ends(PAD_2, size_2))
    if size_2 <= 8:
        step_2 = size_2
        ua2, ub2, ga2, gb2, b2 = (Held(rows, ends(PAD_2, size_2)) for _ in range(5))
    else:
        step_2 = 8
        ua2, ub2, ga2, gb2, b2 = grids[5:10]
        for ref in (ub2, ga2, gb2):
            zero_planes(ref, ends(PAD_2, size_2))
    ua3, ub3, ga3, gb3, b3 = (Held(rows, ends(1, size_3)) for _ in range(5))
    third = 1.0 / 30.0

    at_x, at_z = where_ref[0], where_ref[1]

    def place(x, load):
        for i in range(4):
            plane = []
            for q in range(2):
                even, odd = [], []
                for z in range(0, count_z, 2):
                    one, two = load(z, i, q), load(z + 1, i, q)
                    first = row_of(one.shape) < 4
                    even.append(jnp.where(first, one, pltpu.roll(two, 4, 0)))
                    odd.append(jnp.where(first, pltpu.roll(one, 4, 0), two))
                plane.append([jnp.concatenate(even, axis=0), jnp.concatenate(odd, axis=0)])
            LEVEL_1.put(b1, gb1, x + i, plane)

    if len(pieces) == 1:

        def gather(n):
            place(PAD + 4 * n, lambda z, i, q: pieces[0][n * count_z + z, i, q])

        each(0, count_x, gather, 1)
    else:

        def gather(n):
            for core in range(2):
                x = PAD + 4 * ((2 * n + core) ^ at_x)
                place(x, lambda z, i, q: pieces[core][n * count_z + (z ^ at_z ^ (count_z - 1)), i, q])

        each(0, count_x // 2, gather, 1)

    def sweep(level, u_in, g_in, u_out, g_out, b):
        return lambda x: level.put(u_out, g_out, x, level.sweep(u_in, g_in, b, x, third))

    each(PAD, PAD + size_1, sweep(LEVEL_1, b1, gb1, ua1, ga1, b1), 16)

    def restrict_1(x):
        fine = PAD + 2 * x
        pair = add_planes(
            LEVEL_1.residual(ua1, ga1, b1, fine), LEVEL_1.residual(ua1, ga1, b1, fine + 1)
        )
        plane = scaled(join(pair), 0.5 * 0.2)
        store_plane(b2, PAD_2 + x, plane)
        LEVEL_2.put(ub2, gb2, PAD_2 + x, plane)

    each(0, size_2, restrict_1, step_2)
    all_2 = (PAD_2, PAD_2 + size_2)
    each(*all_2, sweep(LEVEL_2, ub2, gb2, ua2, ga2, b2), step_2)

    def restrict_2(x):
        fine = PAD_2 + 2 * x
        pair = add_planes(
            LEVEL_2.residual(ua2, ga2, b2, fine), LEVEL_2.residual(ua2, ga2, b2, fine + 1)
        )
        plane = [[join_within(pair[0][0]) * (0.5 * 0.2)]]
        store_plane(b3, 1 + x, plane)
        LEVEL_3.put(ub3, gb3, 1 + x, plane)

    each(0, size_3, restrict_2, size_3)
    now, later = (ub3, gb3), (ua3, ga3)
    for _ in range(COARSE_SWEEPS - 1):
        each(1, 1 + size_3, sweep(LEVEL_3, *now, *later, b3), size_3)
        now, later = later, now

    def prolong_3(x):
        for d in range(2):
            fine = PAD_2 + 2 * x + d
            LEVEL_2.put(ua2, ga2, fine, [[ua2[fine, 0, 0] + now[0][1 + x, 0, 0]]])

    each(0, size_3, prolong_3, size_3)
    each(*all_2, sweep(LEVEL_2, ua2, ga2, ub2, gb2, b2), step_2)

    def last_sweep(x):
        store_plane(kept_2, x, LEVEL_2.sweep(ub2, gb2, b2, x, third))

    each(*all_2, last_sweep, step_2)
    return ua1, kept_2, b1


def coarse_finish(count_x, where_ref, grids):
    ua1, ub1, ga1, gb1, b1 = grids[0:5]
    ua2 = grids[5]
    size_1, size_2 = 4 * count_x, 2 * count_x
    third = 1.0 / 30.0

    def prolong_2(x):
        error = ua2[PAD_2 + x, 0, 0]
        for d in range(2):
            fine = PAD + 2 * x + d
            LEVEL_1.put(
                ua1, ga1, fine, [[t + error for t in line] for line in LEVEL_1.load(ua1, fine)]
            )

    def window(rim):
        count = min(BRICK_X // 2 + 2 * rim, size_1)
        return PAD + jnp.clip(4 * where_ref[0] - rim, 0, size_1 - count), count

    start, count = window(4)

    def sweep(i):
        x = start + i
        LEVEL_1.put(ub1, gb1, x, LEVEL_1.sweep(ua1, ga1, b1, x, third))

    last_start, last_count = window(3)

    def last_sweep(i):
        x = last_start + i
        store_plane(ua1, x, LEVEL_1.sweep(ub1, gb1, b1, x, third))

    each(0, size_2, prolong_2, 8)
    each(0, count, sweep, 12)
    each(0, last_count, last_sweep, 10)
    return ua1


def turned_tile(tile, at_z, rows):
    count = tile.shape[0]
    turned = pltpu.roll(tile, lax.rem(count - 4 * at_z, count), 0)
    return jnp.where(row_of((8, LANES)) < 6, turned[0:8], turned[count - 8 : count]) * rows


def near_finish(coarse, where_ref, masks, near):
    ua1, ua2, b1 = coarse
    ua, ga, ub, gb, b = near
    at_x, at_z = where_ref[0], where_ref[1]
    rows = masks[0]

    def take(i):
        error = ua2[2 * at_x + i // 2, 0, 0]
        plane = [[t + error for t in line] for line in LEVEL_1.load(ua1, 4 * at_x + i)]
        plane = [[turned_tile(t, at_z, rows) for t in line] for line in plane]
        NEAR_1.put(ua, ga, i, plane)
        plane = LEVEL_1.load(b1, 4 * at_x + i)
        store_plane(b, i, [[turned_tile(t, at_z, rows) for t in line] for line in plane])

    each(1, 11, take, 5)

    def sweep(i, weight):
        NEAR_1.put(ub, gb, i, NEAR_1.sweep(ua, ga, b, i, weight))

    def last_sweep(i, weight):
        store_plane(ua, i, NEAR_1.sweep(ub, gb, b, i, weight))

    in_segments(2, 10, sweep, masks, 1.0 / 30.0, 4, PAD, BRICK_X // 2)
    in_segments(3, 9, last_sweep, masks, 1.0 / 30.0, 4, PAD, BRICK_X // 2)
    return ua


def rim_masks(count_x, count_z, where_ref):
    at_x, at_z = where_ref[0], where_ref[1]
    k = row_of((8, LANES))
    low = (at_z > 0).astype(jnp.float32)
    high = (at_z < count_z - 1).astype(jnp.float32)
    rows = jnp.where(k < 4, 1.0, jnp.where(k < 6, high, low))
    below = (at_x > 0).astype(jnp.float32)
    above = (at_x < count_x - 1).astype(jnp.float32)
    return rows, below, above


def in_segments(lo, hi, body, masks, scale, chunk, rim=RIM, brick=BRICK_X):
    rows, below, above = masks
    inner = rows * scale
    for start, end, weight in (
        (lo, min(hi, rim), inner * below),
        (max(lo, rim), min(hi, rim + brick), inner),
        (max(lo, rim + brick), hi, inner * above),
    ):
        if end > start:
            each(start, end, functools.partial(body, weight=weight), chunk)


def fine_sweep(u_in, g_in, u_out, g_out, b_ref, margin, masks):
    def body(x, weight):
        FINE.put(u_out, g_out, x, FINE.sweep(u_in, g_in, b_ref, x, weight))

    in_segments(margin, WIDE_X - margin, body, masks, 1.0 / 30.0, 8)


def add_correction(error_of, u_in, u_out, g_out, margin):
    def body(i):
        error = error_of(i)
        for d in range(2):
            x = 2 * i + d
            plane = [
                [u_in[x, q, p] + error[q // 2][p // 2] for p in range(4)] for q in range(4)
            ]
            FINE.put(u_out, g_out, x, plane)

    each(margin // 2, (WIDE_X - margin) // 2, body, 6)


def send_residual(u_ref, g_ref, b_ref, out_ref):
    def body(i):
        x = RIM + 2 * i
        pair = add_planes(
            FINE.residual(u_ref, g_ref, b_ref, x), FINE.residual(u_ref, g_ref, b_ref, x + 1)
        )
        for q, (even, odd) in enumerate(join(pair)):
            out_ref[i, q] = 0.1 * jnp.where(row_of(even.shape) < 4, even, pltpu.roll(odd, 4, 0))

    each(0, BRICK_X // 2, body, BRICK_X // 2)


def places(size, joins):
    row, column = (lax.broadcasted_iota(jnp.int32, (size, size), d) for d in range(2))
    return joins(row, column).astype(jnp.float32).astype(jnp.bfloat16)


def permuted(values, matrix):
    rest, terms = values, []
    for _ in range(3):
        term = rest.astype(jnp.bfloat16)
        rest = rest - term.astype(jnp.float32)
        terms.append(jnp.dot(term, matrix, preferred_element_type=jnp.float32))
    return terms[0] + (terms[1] + terms[2])


def split_lanes(values):
    size_x, size_z, size_y = values.shape
    matrix = places(size_y, lambda y, l: y == (l % LANES) * 4 + l // LANES)
    split = permuted(values.reshape(size_x * size_z, size_y), matrix)
    return [
        split[:, p * LANES : (p + 1) * LANES].reshape(size_x, size_z, LANES) for p in range(4)
    ]


def lanes_kernel(where_ref, charges_ref, rows_ref, one_ref, two_ref):
    odd = where_ref[1] % 2
    for p, tile in enumerate(split_lanes(charges_ref[...])):
        rows_ref[:, p] = tile
        first, last = tile[:, 0:8], tile[:, 8:16]
        one_ref[:, p] = jnp.where(odd == 0, last, first)
        two_ref[:, p] = jnp.where(odd == 0, first, last)


def row_splitter(rows_ref, c_ref):
    def split_rows(ref, rim_ref, part):
        def split(x):
            for p in range(4):
                rows_ref[x, p, 0:BRICK_Z] = ref[x, p]
                rows_ref[x, p, BRICK_Z:WIDE_Z] = rim_ref[x, p]
                for q in range(4):
                    c_ref[part * BRICK_X + x, q, p] = rows_ref[x, p, pl.ds(q, 8, stride=4), :]

        each(0, BRICK_X, split, 2)

    return split_rows


def source_on(c_ref, b_ref, g_ref, start, count, mask):
    weight = mask * (0.2 / 12.0)

    def body(i):
        x = start + i
        here = FINE.load(c_ref, x)
        sums = along_z(here, 1, True)
        plane = []
        for q in range(4):
            y_sums = along_y(here[q], 1)
            line = []
            for p in range(4):
                face = (c_ref[x - 1, q, p] + c_ref[x + 1, q, p]) + (sums[q][p] + y_sums[p])
                line.append((here[q][p] * 6.0 + face) * weight)
            plane.append(line)
        FINE.put(b_ref, g_ref, x, plane)

    each(0, count, body, 8)


def first_sweep_on(b_ref, g_ref, u_ref, h_ref, start, count, mask):
    weight = mask * (1.0 / 30.0)

    def body(i):
        x = start + i
        FINE.put(u_ref, h_ref, x, FINE.sweep(b_ref, g_ref, b_ref, x, weight))

    each(0, count, body, 8)


def early_kernel(count_x, count_z, where_ref, mid_ref, mid_rim_ref, near_ref, far_ref, c_ref,
                 b_ref, g_ref, u_ref, h_ref, lanes_ref, rows_ref):
    inner = rim_masks(count_x, count_z, where_ref)[0]
    odd = where_ref[0] % 2
    for p, tile in enumerate(split_lanes(near_ref[...])):
        lanes_ref[:, p] = tile
    split_rows = row_splitter(rows_ref, c_ref)
    split_rows(mid_ref, mid_rim_ref, 1)
    split_rows(lanes_ref, mid_rim_ref, 2 - 2 * odd)
    split_rows(far_ref, mid_rim_ref, 2 * odd)
    source_on(c_ref, b_ref, g_ref, 9, 6, inner)
    first_sweep_on(b_ref, g_ref, u_ref, h_ref, 10, 4, inner)


def down_kernel(count_x, count_z, where_ref, near_rim_ref, far_rim_ref, c_in, b_in, g_in, u_in, h_in,
                c_ref, b_ref, g_ref, u_ref, h_ref, out_ref):
    del c_in, b_in, g_in, u_in, h_in
    inner, below, above = rim_masks(count_x, count_z, where_ref)
    odd = where_ref[0] % 2
    far = inner * jnp.where(odd == 0, below, above)
    first = row_of((8, LANES)) < 4

    def join_rows(rim_ref, start):
        def join_plane(i):
            for p in range(4):
                for q in range(4):
                    rim = rim_ref[i, p, pl.ds(q, 4, stride=4), :]
                    rim = jnp.concatenate([rim, rim], axis=0)
                    c_ref[start + i, q, p] = jnp.where(first, c_ref[start + i, q, p], rim)

        each(0, BRICK_X, join_plane, 2)

    join_rows(near_rim_ref, 2 * BRICK_X * (1 - odd))
    join_rows(far_rim_ref, 2 * BRICK_X * odd)
    source_on(c_ref, b_ref, g_ref, 1 + 15 * odd, 7, far)
    source_on(c_ref, b_ref, g_ref, 16 - 15 * odd, 7, inner)
    source_on(c_ref, b_ref, g_ref, 8, 1, inner)
    source_on(c_ref, b_ref, g_ref, 15, 1, inner)
    first_sweep_on(b_ref, g_ref, u_ref, h_ref, 2 + 14 * odd, 6, far)
    first_sweep_on(b_ref, g_ref, u_ref, h_ref, 16 - 14 * odd, 6, inner)
    first_sweep_on(b_ref, g_ref, u_ref, h_ref, 8, 2, inner)
    first_sweep_on(b_ref, g_ref, u_ref, h_ref, 14, 2, inner)
    send_residual(u_ref, h_ref, b_ref, out_ref)


def middle_kernel(count_x, count_z, count_pieces, where_ref, *refs):
    pieces, refs = refs[:count_pieces], refs[count_pieces:]
    u_ref, b_ref, v_ref, out_ref, ga_ref, gb_ref, ua_ref, *grids = refs
    masks = rim_masks(count_x, count_z, where_ref)
    coarse_solve(count_x, count_z, where_ref, pieces, grids)
    coarse_ref = coarse_finish(count_x, where_ref, grids)
    at_x, at_z = where_ref[0], where_ref[1]

    def error_of(i):
        plane = LEVEL_1.load(coarse_ref, 4 * at_x + i)
        return [[turned_tile(t, at_z, masks[0]) for t in line] for line in plane]

    add_correction(error_of, u_ref, v_ref, ga_ref, 2)
    fine_sweep(v_ref, ga_ref, ua_ref, gb_ref, b_ref, 3, masks)
    fine_sweep(ua_ref, gb_ref, v_ref, ga_ref, b_ref, 4, masks)
    fine_sweep(v_ref, ga_ref, ua_ref, gb_ref, b_ref, 5, masks)
    fine_sweep(ua_ref, gb_ref, v_ref, ga_ref, b_ref, 6, masks)
    send_residual(v_ref, ga_ref, b_ref, out_ref)


def up_kernel(count_x, count_z, count_pieces, where_ref, *refs):
    pieces, refs = refs[:count_pieces], refs[count_pieces:]
    u_ref, b_ref, out_ref, ga_ref, gb_ref, ua_ref, ub_ref, rows_ref, *refs = refs
    near, grids = refs[:5], refs[5:]
    masks = rim_masks(count_x, count_z, where_ref)
    coarse = coarse_solve(count_x, count_z, where_ref, pieces, grids)
    error_ref = near_finish(coarse, where_ref, masks, near)
    add_correction(lambda i: NEAR_1.load(error_ref, i), u_ref, ua_ref, ga_ref, 6)
    fine_sweep(ua_ref, ga_ref, ub_ref, gb_ref, b_ref, 7, masks)

    def body(x):
        plane = FINE.sweep(ub_ref, gb_ref, b_ref, x, 1.0 / 30.0)
        for q in range(4):
            for p in range(4):
                rows_ref[x - RIM, p, pl.ds(q, 4, stride=4), :] = plane[q][p][0:4]

    each(RIM, RIM + BRICK_X, body, 4)
    tiles = [rows_ref[:, p].reshape(BRICK_X * BRICK_Z, LANES) for p in range(4)]
    matrix = places(out_ref.shape[2], lambda l, y: y == (l % LANES) * 4 + l // LANES)
    out_ref[...] = permuted(jnp.concatenate(tiles, axis=1), matrix).reshape(out_ref.shape)


def call(kernel, outputs, scratch, in_place=None):
    shapes = [jax.ShapeDtypeStruct(shape, jnp.float32) for shape in outputs]
    held = sum(4 * math.prod(shape.shape) for shape in scratch)

    def run(where, *arrays):
        moved = sum(4 * math.prod(array.shape) for array in arrays + tuple(shapes))
        whole = pl.BlockSpec(memory_space=pltpu.VMEM)
        return pl.pallas_call(
            kernel,
            out_shape=shapes,
            in_specs=[pl.BlockSpec(memory_space=pltpu.SMEM)] + [whole] * len(arrays),
            out_specs=[whole] * len(shapes),
            scratch_shapes=scratch,
            input_output_aliases=in_place or {},
            compiler_params=pltpu.CompilerParams(vmem_limit_bytes=held + moved + SPARE_BYTES),
        )(where, *arrays)

    return run


def pairs_apart(count, distance):
    return [(i, i ^ distance) for i in range(count)]


def pairs_shifted(count):
    pairs = [(i, i + 1) for i in range(1, count - 1, 2)]
    return pairs + [(target, source) for source, target in pairs]


def swap(axis, values, distance):
    return lax.ppermute(values, axis, pairs_apart(lax.axis_size(axis), distance))


def every_piece(piece):
    count_x, count_z = lax.axis_size("gx"), lax.axis_size("gz")
    line = [swap("gz", piece[None], count_z - 1 - n) for n in range(count_z - 1)] + [piece[None]]
    halves = [jnp.concatenate(half) for half in (line[: count_z // 2], line[count_z // 2 :])]
    held = jnp.concatenate(halves + [swap("gx", half, 2) for half in halves])
    distance = 4
    while distance < count_x:
        held = jnp.concatenate([held, swap("gx", held, distance)])
        distance *= 2
    return held, swap("gx", held, 1)


def per_device(charges):
    count_x, count_z = lax.axis_size("gx"), lax.axis_size("gz")
    at_x, at_z = lax.axis_index("gx"), lax.axis_index("gz")
    where = jnp.stack([at_x, at_z]).astype(jnp.int32)
    brick, rim = (BRICK_X, 4, BRICK_Z, LANES), (BRICK_X, 4, RIM, LANES)
    middle, one, two = call(lanes_kernel, [brick, rim, rim], [])(where, charges)
    x_far, z_two = pairs_shifted(count_x), pairs_shifted(count_z)
    far = lax.ppermute(middle, "gx", x_far)
    near = swap("gx", charges, 1)
    one, two = swap("gz", one, 1), lax.ppermute(two, "gz", z_two)
    even = at_z % 2 == 0
    middle_rim = jnp.concatenate([jnp.where(even, one, two), jnp.where(even, two, one)], axis=2)
    far_rim = lax.ppermute(middle_rim, "gx", x_far)
    near_rim = swap("gx", middle_rim, 1)

    wide = (WIDE_X, 4, 4, 8, LANES)
    piece_shape = (BRICK_X // 2, 2, 8, LANES)
    fine = pltpu.VMEM(wide, jnp.float32)
    grids = coarse_grids(count_x, count_z)
    rows_in = pltpu.VMEM((BRICK_X, 4, WIDE_Z, LANES), jnp.float32)
    close = pltpu.VMEM((WIDE_X // 2, 2, 2, 8, LANES), jnp.float32)
    rows_out = pltpu.VMEM((BRICK_X, 4, BRICK_Z, LANES), jnp.float32)

    early = call(
        functools.partial(early_kernel, count_x, count_z),
        [wide] * 5,
        [pltpu.VMEM(brick, jnp.float32), rows_in],
    )(where, middle, middle_rim, near, far)
    _, b, _, u, _, piece = call(
        functools.partial(down_kernel, count_x, count_z),
        [wide] * 5 + [piece_shape],
        [],
        in_place={3 + i: i for i in range(5)},
    )(where, near_rim, far_rim, *early)
    pieces = every_piece(piece)
    u, piece = call(
        functools.partial(middle_kernel, count_x, count_z, len(pieces)),
        [wide, piece_shape],
        [fine] * 3 + grids,
    )(where, *pieces, u, b)
    pieces = every_piece(piece)
    (potential,) = call(
        functools.partial(up_kernel, count_x, count_z, len(pieces)),
        [charges.shape],
        [fine] * 4 + [rows_out] + [close] * 5 + grids,
    )(where, *pieces, u, b)
    return potential


def solution(mesh):
    return jax.shard_map(
        per_device,
        mesh=mesh,
        in_specs=(P(("groups", "gx"), "gz", None),),
        out_specs=P(("groups", "gx"), "gz", None),
        check_vma=False,
    )
```

```python
import functools
import math

import jax
import jax.numpy as jnp
from jax import lax
from jax.experimental import pallas as pl
from jax.experimental.pallas import tpu as pltpu
from jax.sharding import PartitionSpec as P

COARSE_SWEEPS = 8
LANES = 128
RIM = 8
BRICK_X = 8
BRICK_Z = 16
WIDE_X = BRICK_X + 2 * RIM
WIDE_Z = BRICK_Z + 2 * RIM
SPARE_BYTES = 4 * 1024 * 1024


def lane_of(shape):
    return lax.broadcasted_iota(jnp.int32, shape, len(shape) - 1)


def row_of(shape):
    return lax.broadcasted_iota(jnp.int32, shape, len(shape) - 2)


def next_row(tile, step, cyclic):
    rows = tile.shape[0]
    moved = pltpu.roll(tile, rows - step, 0)
    return moved if cyclic else jnp.where(row_of(tile.shape) < rows - step, moved, 0.0)


def last_row(tile, step, cyclic):
    moved = pltpu.roll(tile, step, 0)
    return moved if cyclic else jnp.where(row_of(tile.shape) >= step, moved, 0.0)


def next_lane(tile, step):
    moved = pltpu.roll(tile, LANES - step, 1)
    return jnp.where(lane_of(tile.shape) < LANES - step, moved, 0.0)


def last_lane(tile, step):
    moved = pltpu.roll(tile, step, 1)
    return jnp.where(lane_of(tile.shape) >= step, moved, 0.0)


def load_plane(ref, x, count_q, count_p):
    return [[ref[x, q, p] for p in range(count_p)] for q in range(count_q)]


def store_plane(ref, x, plane):
    for q, line in enumerate(plane):
        for p, tile in enumerate(line):
            ref[x, q, p] = tile


def along_z(plane, step, cyclic):
    count_q, count_p = len(plane), len(plane[0])
    result = []
    for q in range(count_q):
        line = []
        for p in range(count_p):
            after = plane[q + 1][p] if q + 1 < count_q else next_row(plane[0][p], step, cyclic)
            before = plane[q - 1][p] if q > 0 else last_row(plane[-1][p], step, cyclic)
            line.append(after + before)
        result.append(line)
    return result


def along_y(line, step):
    count_p = len(line)
    result = []
    for p in range(count_p):
        after = line[p + 1] if p + 1 < count_p else next_lane(line[0], step)
        before = line[p - 1] if p > 0 else last_lane(line[-1], step)
        result.append(after + before)
    return result


class Level:
    def __init__(self, count_q, count_p, step, cyclic):
        self.count_q, self.count_p, self.step, self.cyclic = count_q, count_p, step, cyclic

    def load(self, ref, x):
        return load_plane(ref, x, self.count_q, self.count_p)

    def put(self, u_ref, g_ref, x, plane):
        store_plane(u_ref, x, plane)
        sums = along_z(plane, self.step, self.cyclic)
        store_plane(
            g_ref,
            x,
            [
                [s + (v + v) for s, v in zip(sum_line, line)]
                for sum_line, line in zip(sums, plane)
            ],
        )

    def spread(self, u_ref, g_ref, x, with_u):
        result = []
        for q in range(self.count_q):
            sides, both = [], []
            for p in range(self.count_p):
                here = g_ref[x, q, p]
                sides.append((u_ref[x - 1, q, p] + u_ref[x + 1, q, p]) + here)
                if with_u:
                    here = here + u_ref[x, q, p]
                both.append((g_ref[x - 1, q, p] + g_ref[x + 1, q, p]) + (here + here))
            result.append([a + b for a, b in zip(both, along_y(sides, self.step))])
        return result

    def sweep(self, u_ref, g_ref, b_ref, x, weight):
        wide = self.spread(u_ref, g_ref, x, True)
        return [
            [b_ref[x, q, p] + wide[q][p] * weight for p in range(self.count_p)]
            for q in range(self.count_q)
        ]

    def residual(self, u_ref, g_ref, b_ref, x):
        wide = self.spread(u_ref, g_ref, x, False)
        return [
            [
                b_ref[x, q, p] * 5.0 + (wide[q][p] - u_ref[x, q, p] * 28.0) * (1.0 / 6.0)
                for p in range(self.count_p)
            ]
            for q in range(self.count_q)
        ]


class Held:
    def __init__(self, rows, zero_at=()):
        self.tiles = {(x, 0, 0): jnp.zeros((rows, LANES), jnp.float32) for x in zero_at}

    def __getitem__(self, place):
        return self.tiles[place]

    def __setitem__(self, place, tile):
        self.tiles[place] = tile


def add_planes(one, other):
    return [[a + b for a, b in zip(l, m)] for l, m in zip(one, other)]


def join(plane):
    lines = [[a + b for a, b in zip(plane[q], plane[q + 1])] for q in range(0, len(plane), 2)]
    return [[line[p] + line[p + 1] for p in range(0, len(line), 2)] for line in lines]


def join_within(tile):
    rows = tile.shape[0]
    even = row_of(tile.shape) % 2 == 0
    tile = tile + jnp.where(even, pltpu.roll(tile, rows - 1, 0), pltpu.roll(tile, 1, 0))
    even = lane_of(tile.shape) % 2 == 0
    return tile + jnp.where(even, pltpu.roll(tile, LANES - 1, 1), pltpu.roll(tile, 1, 1))


def scaled(plane, factor):
    return [[tile * factor for tile in line] for line in plane]


def each(lo, hi, body, chunk):
    count = hi - lo
    whole = count // chunk
    if whole == 1:
        for x in range(lo, lo + chunk):
            body(x)
    elif whole > 1:

        def step(i, carry):
            for d in range(chunk):
                body(lo + i * chunk + d)
            return carry

        lax.fori_loop(0, whole, step, 0)
    for x in range(lo + whole * chunk, hi):
        body(x)


FINE = Level(4, 4, 1, True)
LEVEL_1 = Level(2, 2, 1, False)
NEAR_1 = Level(2, 2, 1, True)
LEVEL_2 = Level(1, 1, 1, False)
LEVEL_3 = Level(1, 1, 2, False)
PAD = RIM // 2
PAD_2 = RIM // 4


def zero_planes(ref, indices):
    for x in indices:
        ref[x] = jnp.zeros(ref.shape[1:], ref.dtype)


def coarse_grids(count_x, count_z):
    rows = count_z * BRICK_Z // 4
    shapes = []
    for planes, count in ((4 * count_x + 2 * PAD, 2), (2 * count_x + 2 * PAD_2, 1)):
        shapes += [pltpu.VMEM((planes, count, count, rows, LANES), jnp.float32)] * 5
    return shapes


def coarse_solve(count_x, count_z, where_ref, pieces, grids):
    ua1, ub1, ga1, gb1, b1 = grids[0:5]
    kept_2 = grids[5]
    size_1, size_2, size_3 = 4 * count_x, 2 * count_x, count_x
    rows = b1.shape[3]

    def ends(pad, size):
        return list(range(pad)) + list(range(pad + size, pad + size + pad))

    for ref in (ua1, ub1, ga1, gb1, b1):
        zero_planes(ref, ends(PAD, size_1))
    zero_planes(kept_2, ends(PAD_2, size_2))
    if size_2 <= 8:
        step_2 = size_2
        ua2, ub2, ga2, gb2, b2 = (Held(rows, ends(PAD_2, size_2)) for _ in range(5))
    else:
        step_2 = 8
        ua2, ub2, ga2, gb2, b2 = grids[5:10]
        for ref in (ub2, ga2, gb2):
            zero_planes(ref, ends(PAD_2, size_2))
    ua3, ub3, ga3, gb3, b3 = (Held(rows, ends(1, size_3)) for _ in range(5))
    third = 1.0 / 30.0

    at_x, at_z = where_ref[0], where_ref[1]

    def place(x, load):
        for i in range(4):
            plane = []
            for q in range(2):
                even, odd = [], []
                for z in range(0, count_z, 2):
                    one, two = load(z, i, q), load(z + 1, i, q)
                    first = row_of(one.shape) < 4
                    even.append(jnp.where(first, one, pltpu.roll(two, 4, 0)))
                    odd.append(jnp.where(first, pltpu.roll(one, 4, 0), two))
                plane.append([jnp.concatenate(even, axis=0), jnp.concatenate(odd, axis=0)])
            LEVEL_1.put(b1, gb1, x + i, plane)

    if len(pieces) == 1:

        def gather(n):
            place(PAD + 4 * n, lambda z, i, q: pieces[0][n * count_z + z, i, q])

        each(0, count_x, gather, 1)
    else:

        def gather(n):
            for core in range(2):
                x = PAD + 4 * ((2 * n + core) ^ at_x)
                place(x, lambda z, i, q: pieces[core][n * count_z + (z ^ at_z ^ (count_z - 1)), i, q])

        each(0, count_x // 2, gather, 1)

    def sweep(level, u_in, g_in, u_out, g_out, b):
        return lambda x: level.put(u_out, g_out, x, level.sweep(u_in, g_in, b, x, third))

    each(PAD, PAD + size_1, sweep(LEVEL_1, b1, gb1, ua1, ga1, b1), 16)

    def restrict_1(x):
        fine = PAD + 2 * x
        pair = add_planes(
            LEVEL_1.residual(ua1, ga1, b1, fine), LEVEL_1.residual(ua1, ga1, b1, fine + 1)
        )
        plane = scaled(join(pair), 0.5 * 0.2)
        store_plane(b2, PAD_2 + x, plane)
        LEVEL_2.put(ub2, gb2, PAD_2 + x, plane)

    each(0, size_2, restrict_1, step_2)
    all_2 = (PAD_2, PAD_2 + size_2)
    each(*all_2, sweep(LEVEL_2, ub2, gb2, ua2, ga2, b2), step_2)

    def restrict_2(x):
        fine = PAD_2 + 2 * x
        pair = add_planes(
            LEVEL_2.residual(ua2, ga2, b2, fine), LEVEL_2.residual(ua2, ga2, b2, fine + 1)
        )
        plane = [[join_within(pair[0][0]) * (0.5 * 0.2)]]
        store_plane(b3, 1 + x, plane)
        LEVEL_3.put(ub3, gb3, 1 + x, plane)

    each(0, size_3, restrict_2, size_3)
    now, later = (ub3, gb3), (ua3, ga3)
    for _ in range(COARSE_SWEEPS - 1):
        each(1, 1 + size_3, sweep(LEVEL_3, *now, *later, b3), size_3)
        now, later = later, now

    def prolong_3(x):
        for d in range(2):
            fine = PAD_2 + 2 * x + d
            LEVEL_2.put(ua2, ga2, fine, [[ua2[fine, 0, 0] + now[0][1 + x, 0, 0]]])

    each(0, size_3, prolong_3, size_3)
    each(*all_2, sweep(LEVEL_2, ua2, ga2, ub2, gb2, b2), step_2)

    def last_sweep(x):
        store_plane(kept_2, x, LEVEL_2.sweep(ub2, gb2, b2, x, third))

    each(*all_2, last_sweep, step_2)
    return ua1, kept_2, b1


def coarse_finish(count_x, where_ref, grids):
    ua1, ub1, ga1, gb1, b1 = grids[0:5]
    ua2 = grids[5]
    size_1, size_2 = 4 * count_x, 2 * count_x
    third = 1.0 / 30.0

    def prolong_2(x):
        error = ua2[PAD_2 + x, 0, 0]
        for d in range(2):
            fine = PAD + 2 * x + d
            LEVEL_1.put(
                ua1, ga1, fine, [[t + error for t in line] for line in LEVEL_1.load(ua1, fine)]
            )

    def window(rim):
        count = min(BRICK_X // 2 + 2 * rim, size_1)
        return PAD + jnp.clip(4 * where_ref[0] - rim, 0, size_1 - count), count

    start, count = window(4)

    def sweep(i):
        x = start + i
        LEVEL_1.put(ub1, gb1, x, LEVEL_1.sweep(ua1, ga1, b1, x, third))

    last_start, last_count = window(3)

    def last_sweep(i):
        x = last_start + i
        store_plane(ua1, x, LEVEL_1.sweep(ub1, gb1, b1, x, third))

    each(0, size_2, prolong_2, 8)
    each(0, count, sweep, 12)
    each(0, last_count, last_sweep, 10)
    return ua1


def turned_tile(tile, at_z, rows):
    count = tile.shape[0]
    turned = pltpu.roll(tile, lax.rem(count - 4 * at_z, count), 0)
    return jnp.where(row_of((8, LANES)) < 6, turned[0:8], turned[count - 8 : count]) * rows


def near_finish(coarse, where_ref, masks, near):
    ua1, ua2, b1 = coarse
    ua, ga, ub, gb, b = near
    at_x, at_z = where_ref[0], where_ref[1]
    rows = masks[0]

    def take(i):
        error = ua2[2 * at_x + i // 2, 0, 0]
        plane = [[t + error for t in line] for line in LEVEL_1.load(ua1, 4 * at_x + i)]
        plane = [[turned_tile(t, at_z, rows) for t in line] for line in plane]
        NEAR_1.put(ua, ga, i, plane)
        plane = LEVEL_1.load(b1, 4 * at_x + i)
        store_plane(b, i, [[turned_tile(t, at_z, rows) for t in line] for line in plane])

    each(1, 11, take, 5)

    def sweep(i, weight):
        NEAR_1.put(ub, gb, i, NEAR_1.sweep(ua, ga, b, i, weight))

    def last_sweep(i, weight):
        store_plane(ua, i, NEAR_1.sweep(ub, gb, b, i, weight))

    in_segments(2, 10, sweep, masks, 1.0 / 30.0, 4, PAD, BRICK_X // 2)
    in_segments(3, 9, last_sweep, masks, 1.0 / 30.0, 4, PAD, BRICK_X // 2)
    return ua


def rim_masks(count_x, count_z, where_ref):
    at_x, at_z = where_ref[0], where_ref[1]
    k = row_of((8, LANES))
    low = (at_z > 0).astype(jnp.float32)
    high = (at_z < count_z - 1).astype(jnp.float32)
    rows = jnp.where(k < 4, 1.0, jnp.where(k < 6, high, low))
    below = (at_x > 0).astype(jnp.float32)
    above = (at_x < count_x - 1).astype(jnp.float32)
    return rows, below, above


def in_segments(lo, hi, body, masks, scale, chunk, rim=RIM, brick=BRICK_X):
    rows, below, above = masks
    inner = rows * scale
    for start, end, weight in (
        (lo, min(hi, rim), inner * below),
        (max(lo, rim), min(hi, rim + brick), inner),
        (max(lo, rim + brick), hi, inner * above),
    ):
        if end > start:
            each(start, end, functools.partial(body, weight=weight), chunk)


def fine_sweep(u_in, g_in, u_out, g_out, b_ref, margin, masks):
    def body(x, weight):
        FINE.put(u_out, g_out, x, FINE.sweep(u_in, g_in, b_ref, x, weight))

    in_segments(margin, WIDE_X - margin, body, masks, 1.0 / 30.0, 8)


def add_correction(error_of, u_in, u_out, g_out, margin):
    def body(i):
        error = error_of(i)
        for d in range(2):
            x = 2 * i + d
            plane = [
                [u_in[x, q, p] + error[q // 2][p // 2] for p in range(4)] for q in range(4)
            ]
            FINE.put(u_out, g_out, x, plane)

    each(margin // 2, (WIDE_X - margin) // 2, body, 6)


def send_residual(u_ref, g_ref, b_ref, out_ref):
    def body(i):
        x = RIM + 2 * i
        pair = add_planes(
            FINE.residual(u_ref, g_ref, b_ref, x), FINE.residual(u_ref, g_ref, b_ref, x + 1)
        )
        for q, (even, odd) in enumerate(join(pair)):
            out_ref[i, q] = 0.1 * jnp.where(row_of(even.shape) < 4, even, pltpu.roll(odd, 4, 0))

    each(0, BRICK_X // 2, body, BRICK_X // 2)


def places(size, joins):
    row, column = (lax.broadcasted_iota(jnp.int32, (size, size), d) for d in range(2))
    return joins(row, column).astype(jnp.float32).astype(jnp.bfloat16)


def permuted(values, matrix):
    rest, terms = values, []
    for _ in range(3):
        term = rest.astype(jnp.bfloat16)
        rest = rest - term.astype(jnp.float32)
        terms.append(jnp.dot(term, matrix, preferred_element_type=jnp.float32))
    return terms[0] + (terms[1] + terms[2])


def split_lanes(values):
    size_x, size_z, size_y = values.shape
    matrix = places(size_y, lambda y, l: y == (l % LANES) * 4 + l // LANES)
    split = permuted(values.reshape(size_x * size_z, size_y), matrix)
    return [
        split[:, p * LANES : (p + 1) * LANES].reshape(size_x, size_z, LANES) for p in range(4)
    ]


def lanes_kernel(where_ref, charges_ref, rows_ref, one_ref, two_ref):
    odd = where_ref[1] % 2
    for p, tile in enumerate(split_lanes(charges_ref[...])):
        rows_ref[:, p] = tile
        first, last = tile[:, 0:8], tile[:, 8:16]
        one_ref[:, p] = jnp.where(odd == 0, last, first)
        two_ref[:, p] = jnp.where(odd == 0, first, last)


def row_splitter(rows_ref, c_ref):
    def split_rows(ref, rim_ref, part):
        def split(x):
            for p in range(4):
                rows_ref[x, p, 0:BRICK_Z] = ref[x, p]
                rows_ref[x, p, BRICK_Z:WIDE_Z] = rim_ref[x, p]
                for q in range(4):
                    c_ref[part * BRICK_X + x, q, p] = rows_ref[x, p, pl.ds(q, 8, stride=4), :]

        each(0, BRICK_X, split, 2)

    return split_rows


def source_on(c_ref, b_ref, g_ref, start, count, mask):
    weight = mask * (0.2 / 12.0)

    def body(i):
        x = start + i
        here = FINE.load(c_ref, x)
        sums = along_z(here, 1, True)
        plane = []
        for q in range(4):
            y_sums = along_y(here[q], 1)
            line = []
            for p in range(4):
                face = (c_ref[x - 1, q, p] + c_ref[x + 1, q, p]) + (sums[q][p] + y_sums[p])
                line.append((here[q][p] * 6.0 + face) * weight)
            plane.append(line)
        FINE.put(b_ref, g_ref, x, plane)

    each(0, count, body, 8)


def first_sweep_on(b_ref, g_ref, u_ref, h_ref, start, count, mask):
    weight = mask * (1.0 / 30.0)

    def body(i):
        x = start + i
        FINE.put(u_ref, h_ref, x, FINE.sweep(b_ref, g_ref, b_ref, x, weight))

    each(0, count, body, 8)


def early_kernel(count_x, count_z, where_ref, mid_ref, mid_rim_ref, near_ref, far_ref, c_ref,
                 b_ref, g_ref, u_ref, h_ref, lanes_ref, rows_ref):
    inner = rim_masks(count_x, count_z, where_ref)[0]
    odd = where_ref[0] % 2
    for p, tile in enumerate(split_lanes(near_ref[...])):
        lanes_ref[:, p] = tile
    split_rows = row_splitter(rows_ref, c_ref)
    split_rows(mid_ref, mid_rim_ref, 1)
    split_rows(lanes_ref, mid_rim_ref, 2 - 2 * odd)
    split_rows(far_ref, mid_rim_ref, 2 * odd)
    source_on(c_ref, b_ref, g_ref, 9, 6, inner)
    first_sweep_on(b_ref, g_ref, u_ref, h_ref, 10, 4, inner)


def down_kernel(count_x, count_z, where_ref, near_rim_ref, far_rim_ref, c_in, b_in, g_in, u_in, h_in,
                c_ref, b_ref, g_ref, u_ref, h_ref, out_ref):
    del c_in, b_in, g_in, u_in, h_in
    inner, below, above = rim_masks(count_x, count_z, where_ref)
    odd = where_ref[0] % 2
    far = inner * jnp.where(odd == 0, below, above)
    first = row_of((8, LANES)) < 4

    def join_rows(rim_ref, start):
        def join_plane(i):
            for p in range(4):
                for q in range(4):
                    rim = rim_ref[i, p, pl.ds(q, 4, stride=4), :]
                    rim = jnp.concatenate([rim, rim], axis=0)
                    c_ref[start + i, q, p] = jnp.where(first, c_ref[start + i, q, p], rim)

        each(0, BRICK_X, join_plane, 2)

    join_rows(near_rim_ref, 2 * BRICK_X * (1 - odd))
    join_rows(far_rim_ref, 2 * BRICK_X * odd)
    source_on(c_ref, b_ref, g_ref, 1 + 15 * odd, 7, far)
    source_on(c_ref, b_ref, g_ref, 16 - 15 * odd, 7, inner)
    source_on(c_ref, b_ref, g_ref, 8, 1, inner)
    source_on(c_ref, b_ref, g_ref, 15, 1, inner)
    first_sweep_on(b_ref, g_ref, u_ref, h_ref, 2 + 14 * odd, 6, far)
    first_sweep_on(b_ref, g_ref, u_ref, h_ref, 16 - 14 * odd, 6, inner)
    first_sweep_on(b_ref, g_ref, u_ref, h_ref, 8, 2, inner)
    first_sweep_on(b_ref, g_ref, u_ref, h_ref, 14, 2, inner)
    send_residual(u_ref, h_ref, b_ref, out_ref)


def middle_kernel(count_x, count_z, count_pieces, where_ref, *refs):
    pieces, refs = refs[:count_pieces], refs[count_pieces:]
    u_ref, b_ref, v_ref, out_ref, ga_ref, gb_ref, ua_ref, *grids = refs
    masks = rim_masks(count_x, count_z, where_ref)
    coarse_solve(count_x, count_z, where_ref, pieces, grids)
    coarse_ref = coarse_finish(count_x, where_ref, grids)
    at_x, at_z = where_ref[0], where_ref[1]

    def error_of(i):
        plane = LEVEL_1.load(coarse_ref, 4 * at_x + i)
        return [[turned_tile(t, at_z, masks[0]) for t in line] for line in plane]

    add_correction(error_of, u_ref, v_ref, ga_ref, 2)
    fine_sweep(v_ref, ga_ref, ua_ref, gb_ref, b_ref, 3, masks)
    fine_sweep(ua_ref, gb_ref, v_ref, ga_ref, b_ref, 4, masks)
    fine_sweep(v_ref, ga_ref, ua_ref, gb_ref, b_ref, 5, masks)
    fine_sweep(ua_ref, gb_ref, v_ref, ga_ref, b_ref, 6, masks)
    send_residual(v_ref, ga_ref, b_ref, out_ref)


def up_kernel(count_x, count_z, count_pieces, where_ref, *refs):
    pieces, refs = refs[:count_pieces], refs[count_pieces:]
    u_ref, b_ref, out_ref, ga_ref, gb_ref, ua_ref, ub_ref, rows_ref, *refs = refs
    near, grids = refs[:5], refs[5:]
    masks = rim_masks(count_x, count_z, where_ref)
    coarse = coarse_solve(count_x, count_z, where_ref, pieces, grids)
    error_ref = near_finish(coarse, where_ref, masks, near)
    add_correction(lambda i: NEAR_1.load(error_ref, i), u_ref, ua_ref, ga_ref, 6)
    fine_sweep(ua_ref, ga_ref, ub_ref, gb_ref, b_ref, 7, masks)

    def body(x):
        plane = FINE.sweep(ub_ref, gb_ref, b_ref, x, 1.0 / 30.0)
        for q in range(4):
            for p in range(4):
                rows_ref[x - RIM, p, pl.ds(q, 4, stride=4), :] = plane[q][p][0:4]

    each(RIM, RIM + BRICK_X, body, 4)
    tiles = [rows_ref[:, p].reshape(BRICK_X * BRICK_Z, LANES) for p in range(4)]
    matrix = places(out_ref.shape[2], lambda l, y: y == (l % LANES) * 4 + l // LANES)
    out_ref[...] = permuted(jnp.concatenate(tiles, axis=1), matrix).reshape(out_ref.shape)


def call(kernel, outputs, scratch, in_place=None):
    shapes = [jax.ShapeDtypeStruct(shape, jnp.float32) for shape in outputs]
    held = sum(4 * math.prod(shape.shape) for shape in scratch)

    def run(where, *arrays):
        moved = sum(4 * math.prod(array.shape) for array in arrays + tuple(shapes))
        whole = pl.BlockSpec(memory_space=pltpu.VMEM)
        return pl.pallas_call(
            kernel,
            out_shape=shapes,
            in_specs=[pl.BlockSpec(memory_space=pltpu.SMEM)] + [whole] * len(arrays),
            out_specs=[whole] * len(shapes),
            scratch_shapes=scratch,
            input_output_aliases=in_place or {},
            compiler_params=pltpu.CompilerParams(vmem_limit_bytes=held + moved + SPARE_BYTES),
        )(where, *arrays)

    return run


def pairs_apart(count, distance):
    return [(i, i ^ distance) for i in range(count)]


def pairs_shifted(count):
    pairs = [(i, i + 1) for i in range(1, count - 1, 2)]
    return pairs + [(target, source) for source, target in pairs]


def swap(axis, values, distance):
    return lax.ppermute(values, axis, pairs_apart(lax.axis_size(axis), distance))


def every_piece(piece):
    count_x, count_z = lax.axis_size("gx"), lax.axis_size("gz")
    line = [swap("gz", piece[None], count_z - 1 - n) for n in range(count_z - 1)] + [piece[None]]
    parts = [jnp.concatenate(part) for part in (line[:1], line[1:])]
    held = jnp.concatenate(parts + [swap("gx", part, 2) for part in parts])
    distance = 4
    while distance < count_x:
        held = jnp.concatenate([held, swap("gx", held, distance)])
        distance *= 2
    return held, swap("gx", held, 1)


def per_device(charges):
    count_x, count_z = lax.axis_size("gx"), lax.axis_size("gz")
    at_x, at_z = lax.axis_index("gx"), lax.axis_index("gz")
    where = jnp.stack([at_x, at_z]).astype(jnp.int32)
    brick, rim = (BRICK_X, 4, BRICK_Z, LANES), (BRICK_X, 4, RIM, LANES)
    middle, one, two = call(lanes_kernel, [brick, rim, rim], [])(where, charges)
    x_far, z_two = pairs_shifted(count_x), pairs_shifted(count_z)
    far = lax.ppermute(middle, "gx", x_far)
    near = swap("gx", charges, 1)
    one, two = swap("gz", one, 1), lax.ppermute(two, "gz", z_two)
    even = at_z % 2 == 0
    middle_rim = jnp.concatenate([jnp.where(even, one, two), jnp.where(even, two, one)], axis=2)
    far_rim = lax.ppermute(middle_rim, "gx", x_far)
    near_rim = swap("gx", middle_rim, 1)

    wide = (WIDE_X, 4, 4, 8, LANES)
    piece_shape = (BRICK_X // 2, 2, 8, LANES)
    fine = pltpu.VMEM(wide, jnp.float32)
    grids = coarse_grids(count_x, count_z)
    rows_in = pltpu.VMEM((BRICK_X, 4, WIDE_Z, LANES), jnp.float32)
    close = pltpu.VMEM((WIDE_X // 2, 2, 2, 8, LANES), jnp.float32)
    rows_out = pltpu.VMEM((BRICK_X, 4, BRICK_Z, LANES), jnp.float32)

    early = call(
        functools.partial(early_kernel, count_x, count_z),
        [wide] * 5,
        [pltpu.VMEM(brick, jnp.float32), rows_in],
    )(where, middle, middle_rim, near, far)
    _, b, _, u, _, piece = call(
        functools.partial(down_kernel, count_x, count_z),
        [wide] * 5 + [piece_shape],
        [],
        in_place={3 + i: i for i in range(5)},
    )(where, near_rim, far_rim, *early)
    pieces = every_piece(piece)
    u, piece = call(
        functools.partial(middle_kernel, count_x, count_z, len(pieces)),
        [wide, piece_shape],
        [fine] * 3 + grids,
    )(where, *pieces, u, b)
    pieces = every_piece(piece)
    (potential,) = call(
        functools.partial(up_kernel, count_x, count_z, len(pieces)),
        [charges.shape],
        [fine] * 4 + [rows_out] + [close] * 5 + grids,
    )(where, *pieces, u, b)
    return potential


def solution(mesh):
    return jax.shard_map(
        per_device,
        mesh=mesh,
        in_specs=(P(("groups", "gx"), "gz", None),),
        out_specs=P(("groups", "gx"), "gz", None),
        check_vma=False,
    )
```
